32 devices in a mesh: segment: 2 (over core), dp: 8 (over z, x), mp: 2 (over y).
Axes of the slice: x: 2, y: 2, z: 4, core: 2. Of those that a mesh axis runs over, the one named last changes fastest.
Arguments:
- grad_top: bfloat16 [4096, 2048], P('dp'), may hold values from -6 to 6
- saved_query: bfloat16 [2, 4096, 2048], P('segment', 'dp', 'mp'), may hold values from -12 to 12
- saved_key: bfloat16 [2, 6144, 2048], P('segment', 'dp', 'mp'), may hold values from -4 to 4
- saved_value: bfloat16 [2, 6144, 2048], P('segment', 'dp', 'mp'), may hold values from -6 to 6
- w_query: bfloat16 [2, 2048, 2048], P('segment', 'mp', 'dp'), may hold values from -0.125 to 0.125
- w_key: bfloat16 [2, 2048, 2048], P('segment', 'mp', 'dp'), may hold values from -0.125 to 0.125
- w_value: bfloat16 [2, 2048, 2048], P('segment', 'mp', 'dp'), may hold values from -0.125 to 0.125
- w_out: bfloat16 [2, 2048, 2048], P('segment', 'mp', 'dp'), may hold values from -0.125 to 0.125
- query_length: int32 [16, 2], P('dp'), may hold values from 64 to 128
- key_offset: int32 [16, 2], P('dp'), may hold values from 0 to 2, as said below
- key_length: int32 [16, 2], P('dp'), may hold values from 64 to 256
- tile_owner: int32 [16, 3], replicated, may hold values from 0 to 47, as said below
Outputs:
- section_grads: bfloat16 [2, 4096, 2048], P('segment', 'dp', 'mp')
- encoder_grads: bfloat16 [6144, 2048], P('dp', ('segment', 'mp'))
The draws below stay inside these ranges and needn't reach their ends.
Inputs may be any that keep to these rules, and one draw needn't show every extreme that they name: Example 0 takes tiles 0 to key_offset[s, 1] - 1 and example 1 the rest of the sequence's encoder tiles; each example holds at least one tile and its rows fit in its tiles. `tile_owner`: every global tile appears once. Tile t is owned by dp index t // 6; the owner of a tile of dp index i (sequences i * 2 to i * 2 + 1) is i - 1, i or i + 1, wrapping around. Each dp index hands 1 to 2 tiles to each neighbour, and 2 is reached in every draw.
All inputs are finite; a program needn't handle non-finite values.
Results may differ from the reference program's by a relative error of at most 0.019.
Values may be sent and summed in bfloat16 or wider, within the bound.
A program may use at most 128 MiB of HBM per device.

```python
import jax
import jax.numpy as jnp
from jax import lax

D = 2048
HEADS = 8
DH = 256
TILE = 128
NEX = 2
M = 2
CAP = 2
TK = 384
TQ = 256
SEQS = 16
Q_ROWS = 4096
K_ROWS = 6144
N_MP = 2


def packing_table(key):
    base_key = jax.random.fold_in(key, 11)
    first_key, second_key, third_key = jax.random.split(base_key, 3)
    key_tiles = TK // TILE
    first = jax.random.randint(first_key, (SEQS,), 1, key_tiles)
    first = first.at[0].set(key_tiles - 1)
    offsets = jnp.stack([jnp.zeros_like(first), first], axis=1)
    tiles_each = jnp.stack([first, key_tiles - first], axis=1)
    spread = jax.random.randint(second_key, (SEQS, NEX), 0, 1 << 20)
    key_len = TILE // 2 + spread % (tiles_each * TILE - TILE // 2 + 1)
    key_len = key_len.at[0, 0].set((key_tiles - 1) * TILE)
    query_len = jax.random.randint(third_key, (SEQS, NEX), TILE // 2, TILE + 1)
    query_len = query_len.at[0, 0].set(TILE)
    return (offsets.astype(jnp.int32), key_len.astype(jnp.int32), query_len.astype(jnp.int32))


def draw_query_length(key, part):
    return packing_table(key)[2]


def draw_key_offset(key, part):
    return packing_table(key)[0]


def draw_key_length(key, part):
    return packing_table(key)[1]


def draw_tile_owner(key, part):
    base_key = jax.random.fold_in(key, 23)
    send_key, order_key, slot_key = jax.random.split(base_key, 3)
    devices = SEQS // M
    per_device = M * TK // TILE
    sends = jax.random.randint(send_key, (devices,), 1, CAP + 1).at[0].set(CAP)
    previous = jnp.roll(sends, 1)
    order = jax.vmap(lambda sub_key: jax.random.permutation(sub_key, per_device))(jax.random.split(order_key, devices))
    slots = jax.vmap(lambda sub_key: jax.random.permutation(sub_key, per_device))(jax.random.split(slot_key, devices))
    device_ids = jnp.arange(devices, dtype=jnp.int32)[:, None]
    place_ids = jnp.arange(per_device, dtype=jnp.int32)[None, :]
    right_count = sends[:, None]
    left_count = previous[:, None]
    go_right = place_ids < right_count
    go_left = (place_ids >= right_count) & (place_ids < right_count + left_count)
    owner = jnp.where(go_right, (device_ids + 1) % devices, jnp.where(go_left, (device_ids - 1 + devices) % devices, device_ids))
    received_rows = jnp.where(go_right, place_ids, jnp.where(go_left, per_device - left_count + place_ids - right_count, left_count + place_ids - right_count - left_count))
    global_tile = owner * per_device + slots[owner, received_rows]
    inverse = jnp.argsort(order, axis=1)
    dest = jnp.take_along_axis(global_tile, inverse, axis=1)
    return dest.reshape(SEQS, TK // TILE).astype(jnp.int32)


def draw_saved_query(key, part):
    drawn = jax.random.normal(jax.random.fold_in(key, 41), (2, Q_ROWS, HEADS * DH), jnp.float32)
    return jnp.clip(drawn, -4.0, 4.0).astype(jnp.bfloat16)


def draw_saved_key(key, part):
    drawn = jax.random.normal(jax.random.fold_in(key, 43), (2, K_ROWS, HEADS * DH), jnp.float32)
    return jnp.clip(drawn, -4.0, 4.0).astype(jnp.bfloat16)


def steps_of(stream_key, extent, cuts, low, high):
    loudness = 1.0
    for axis_at, blocks in cuts:
        steps = jax.random.uniform(jax.random.fold_in(jax.random.fold_in(stream_key, 6), axis_at), (blocks,), jnp.float32, low / len(cuts), high / len(cuts))
        loudness = loudness * jnp.repeat(jnp.exp(steps), extent[axis_at] // blocks).reshape((-1,) + (1,) * (len(extent) - 1 - axis_at))
    return loudness


def centred(key, extent, scale, reach, pieces=(), held_as=jnp.bfloat16):
    factor_of = steps_of(key, extent, pieces, -0.22, 0.18) if pieces else 1.0
    values = jax.random.normal(key, extent, jnp.float32) * scale * factor_of
    return jnp.minimum(jnp.maximum(values, -reach), reach).astype(held_as)


def setup_inputs(seed: int = 0) -> dict:
    arg_keys = jax.random.split(jax.random.key(seed), 13)
    grad_top = centred(arg_keys[0], (Q_ROWS, D), 1.0, 6.0, ((0, 8),))
    saved_query = draw_saved_query(jax.random.fold_in(arg_keys[12], 71), 0)
    saved_key = draw_saved_key(jax.random.fold_in(arg_keys[12], 71), 0)
    saved_value = centred(arg_keys[3], (2, K_ROWS, HEADS * DH), 1.0, 6.0, ((0, 2), (1, 8), (2, 2)))
    w_query = centred(arg_keys[4], (2, HEADS * DH, D), D ** -0.5, 0.125, ((0, 2), (1, 2), (2, 8)))
    w_key = centred(arg_keys[5], (2, HEADS * DH, D), D ** -0.5, 0.125, ((0, 2), (1, 2), (2, 8)))
    w_value = centred(arg_keys[6], (2, HEADS * DH, D), D ** -0.5, 0.125, ((0, 2), (1, 2), (2, 8)))
    w_out = centred(arg_keys[7], (2, HEADS * DH, D), (HEADS * DH) ** -0.5, 0.125, ((0, 2), (1, 2), (2, 8)))
    query_length = draw_query_length(jax.random.fold_in(arg_keys[12], 71), 0)
    key_offset = draw_key_offset(jax.random.fold_in(arg_keys[12], 71), 0)
    key_length = draw_key_length(jax.random.fold_in(arg_keys[12], 71), 0)
    tile_owner = draw_tile_owner(jax.random.fold_in(arg_keys[12], 71), 0)
    return {"grad_top": grad_top, "saved_query": saved_query, "saved_key": saved_key, "saved_value": saved_value, "w_query": w_query, "w_key": w_key, "w_value": w_value, "w_out": w_out, "query_length": query_length, "key_offset": key_offset, "key_length": key_length, "tile_owner": tile_owner}


masked_floor = -1.0e30


def example_mask(query_length, key_offset, key_length):
    row_ids = jnp.arange(TQ, dtype=jnp.int32)[:, None]
    starts = jnp.arange(NEX, dtype=jnp.int32)[None, :] * TILE
    inside_q = (row_ids >= starts) & (row_ids < starts + query_length[None, :])
    col_ids = jnp.arange(TK, dtype=jnp.int32)[:, None]
    key_start = key_offset[None, :] * TILE
    inside_k = (col_ids >= key_start) & (col_ids < key_start + key_length[None, :])
    return jnp.any(inside_q[:, None, :] & inside_k[None, :, :], axis=-1)


def sequence_backward(grad_in, query_block, key_block, value_block, query_length, key_offset, key_length, w_query, w_out):
    score_scale = DH ** -0.5
    out_grad = jnp.dot(grad_in, w_out.T, preferred_element_type=jnp.float32).astype(jnp.bfloat16)
    q_heads = query_block.reshape(TQ, HEADS, DH).astype(jnp.float32)
    k_heads = key_block.reshape(TK, HEADS, DH).astype(jnp.float32)
    v_heads = value_block.reshape(TK, HEADS, DH).astype(jnp.float32)
    grad_heads = out_grad.reshape(TQ, HEADS, DH).astype(jnp.float32)
    scores = jnp.einsum("qhd,khd->hqk", q_heads, k_heads) * score_scale
    allowed = example_mask(query_length, key_offset, key_length)[None]
    masked = jnp.where(allowed, scores, masked_floor)
    row_max = jnp.max(masked, axis=-1, keepdims=True)
    exp_terms = jnp.where(allowed, jnp.exp(masked - row_max), 0.0)
    denominator = jnp.maximum(jnp.sum(exp_terms, axis=-1, keepdims=True), 1.0)
    attention_probs = exp_terms / denominator
    prob_bf = attention_probs.astype(jnp.bfloat16).astype(jnp.float32)
    attended = jnp.einsum("hqk,khd->qhd", prob_bf, v_heads)
    out_dot = jnp.sum(grad_heads * attended, axis=-1)
    prob_grad = jnp.einsum("qhd,khd->hqk", grad_heads, v_heads)
    score_grad = (attention_probs * (prob_grad - jnp.transpose(out_dot)[:, :, None])).astype(jnp.bfloat16).astype(jnp.float32)
    query_grad = (jnp.einsum("hqk,khd->qhd", score_grad, k_heads) * score_scale).astype(jnp.bfloat16)
    key_gradient = (jnp.einsum("hqk,qhd->khd", score_grad, q_heads) * score_scale).astype(jnp.bfloat16)
    value_grad = jnp.einsum("hqk,qhd->khd", prob_bf, grad_heads).astype(jnp.bfloat16)
    mixed_grad = jnp.dot(query_grad.reshape(TQ, HEADS * DH), w_query, preferred_element_type=jnp.float32)
    section = (grad_in.astype(jnp.float32) + mixed_grad).astype(jnp.bfloat16)
    return section, key_gradient.reshape(TK, HEADS * DH), value_grad.reshape(TK, HEADS * DH)


def layer_backward(grad_rows, query_all, key_all, value_all, w_query, w_out, query_length, key_offset, key_length):
    def one_sequence(items):
        return sequence_backward(items[0], items[1], items[2], items[3], items[4], items[5], items[6], w_query, w_out)

    sections, key_grads, value_grads = lax.map(one_sequence, (
        grad_rows.reshape(SEQS, TQ, D), query_all.reshape(SEQS, TQ, HEADS * DH),
        key_all.reshape(SEQS, TK, HEADS * DH), value_all.reshape(SEQS, TK, HEADS * DH),
        query_length, key_offset, key_length))
    return sections.reshape(Q_ROWS, D), key_grads.reshape(K_ROWS, HEADS * DH), value_grads.reshape(K_ROWS, HEADS * DH)


def group_parts(key_grads, value_grads, w_key, w_value):
    group_width = HEADS * DH // N_MP
    total = jnp.zeros((K_ROWS, D), jnp.float32)
    for group in range(N_MP):
        low = group * group_width
        high = low + group_width
        part_sum = jnp.dot(key_grads[:, low:high], w_key[low:high], preferred_element_type=jnp.float32)
        part_sum = part_sum + jnp.dot(value_grads[:, low:high], w_value[low:high], preferred_element_type=jnp.float32)
        rounded = lax.optimization_barrier(part_sum.astype(jnp.bfloat16))
        total = total + rounded.astype(jnp.float32)
    return total


def reference(grad_top, saved_query, saved_key, saved_value, w_query, w_key, w_value, w_out, query_length, key_offset, key_length, tile_owner):
    upper, key_upper, value_upper = layer_backward(grad_top, saved_query[1], saved_key[1], saved_value[1], w_query[1], w_out[1], query_length, key_offset, key_length)
    lower, key_lower, value_lower = layer_backward(upper, saved_query[0], saved_key[0], saved_value[0], w_query[0], w_out[0], query_length, key_offset, key_length)
    encoder_total = group_parts(key_upper, value_upper, w_key[1], w_value[1])
    encoder_total = encoder_total + group_parts(key_lower, value_lower, w_key[0], w_value[0])
    source_tiles = encoder_total.astype(jnp.bfloat16).reshape(SEQS * (TK // TILE), TILE, D)
    placed_tiles = jnp.zeros_like(source_tiles).at[tile_owner.reshape(-1).astype(jnp.int32)].set(source_tiles)
    return jnp.stack([lower, upper]), placed_tiles.reshape(K_ROWS, D)
```

```python
import functools

import jax
import jax.numpy as jnp
from jax import lax
from jax.experimental import pallas as pl
from jax.experimental.pallas import tpu as pltpu
from jax.sharding import PartitionSpec as P

DH = 256
TILE = 128
CAP = 2
BLOCK = 256
masked_floor = -1e30
BF16, F32 = jnp.bfloat16, jnp.float32


def dot(a, b, ca, cb):
    return lax.dot_general(a, b, (((ca,), (cb,)), ((), ())), preferred_element_type=F32)


def tick_kernel(count, half, sc, g_ref, q_ref, k_ref, v_ref, *rest):
    wo, wq = rest[:count], rest[count : 2 * count]
    mixed_ref, kg_ref, vg_ref, acc = rest[2 * count :]
    head = pl.program_id(0)
    per = half // BLOCK
    scale = DH ** (-0.5)

    def place(b):
        src = sc[b]
        return src // per, pl.ds(pl.multiple_of((src % per) * BLOCK, BLOCK), BLOCK)

    og = None
    for b in range(count):
        at, cols = place(b)
        term = dot(g_ref[at, :, cols], wo[b][...], 1, 1)
        og = term if og is None else og + term
    og = og.astype(BF16)
    q, k, v = q_ref[0], k_ref[0], v_ref[0]
    scores = dot(q, k, 1, 1) * scale
    rows = lax.broadcasted_iota(jnp.int32, scores.shape, 0)
    cols_id = lax.broadcasted_iota(jnp.int32, scores.shape, 1)
    allowed = None
    for e in range(2):
        q_len, k_off, k_len = sc[count + e], sc[count + 2 + e] * TILE, sc[count + 4 + e]
        hit = (rows >= e * TILE) & (rows < e * TILE + q_len)
        hit = hit & (cols_id >= k_off) & (cols_id < k_off + k_len)
        allowed = hit if allowed is None else allowed | hit
    masked = jnp.where(allowed, scores, masked_floor)
    top = jnp.max(masked, axis=-1, keepdims=True)
    terms = jnp.where(allowed, jnp.exp(masked - top), 0.0)
    prob = terms / jnp.maximum(jnp.sum(terms, axis=-1, keepdims=True), 1.0)
    prob_bf = prob.astype(BF16)
    attended = dot(prob_bf, v, 1, 0)
    out_dot = jnp.sum(og.astype(F32) * attended, axis=-1, keepdims=True)
    sg = (prob * (dot(og, v, 1, 1) - out_dot)).astype(BF16)
    qg = (dot(sg, k, 1, 0) * scale).astype(BF16)
    kg_ref[...] = (dot(sg, q, 0, 0) * scale).astype(BF16)
    vg_ref[...] = dot(prob_bf, og, 0, 0).astype(BF16)

    @pl.when(head == 0)
    def _():
        acc[...] = jnp.zeros_like(acc)

    for b in range(count):
        at, cols = place(b)
        acc[at, :, cols] += dot(qg, wq[b][...], 1, 0)

    @pl.when(head == pl.num_programs(0) - 1)
    def _():
        mixed_ref[...] = acc[...].astype(BF16)


def run_tick(scalars, grad, at, seq, saved_q, saved_k, saved_v, wo, wq, q_rows, k_rows):
    half = grad.shape[2]
    heads = saved_q.shape[2] // DH
    count = len(wo)
    weight = pl.BlockSpec((DH, BLOCK), lambda h, sc: (h, 0))
    macs = heads * q_rows * DH * (4 * half + 6 * k_rows)
    return pl.pallas_call(
        functools.partial(tick_kernel, count, half),
        grid_spec=pltpu.PrefetchScalarGridSpec(
            num_scalar_prefetch=1,
            grid=(heads,),
            in_specs=[
                pl.BlockSpec((2, q_rows, half), lambda h, sc: (0, at, 0)),
                pl.BlockSpec((1, q_rows, DH), lambda h, sc: (0, seq, h)),
                pl.BlockSpec((1, k_rows, DH), lambda h, sc: (0, seq, h)),
                pl.BlockSpec((1, k_rows, DH), lambda h, sc: (0, seq, h)),
            ]
            + [weight] * (2 * count),
            out_specs=[
                pl.BlockSpec((2, q_rows, half), lambda h, sc: (0, 0, 0)),
                pl.BlockSpec((k_rows, DH), lambda h, sc: (0, h)),
                pl.BlockSpec((k_rows, DH), lambda h, sc: (0, h)),
            ],
            scratch_shapes=[pltpu.VMEM((2, q_rows, half), F32)],
        ),
        out_shape=[
            jax.ShapeDtypeStruct((2, q_rows, half), BF16),
            jax.ShapeDtypeStruct((k_rows, heads * DH), BF16),
            jax.ShapeDtypeStruct((k_rows, heads * DH), BF16),
        ],
        compiler_params=pltpu.CompilerParams(vmem_limit_bytes=40 << 20),
        cost_estimate=pl.CostEstimate(
            flops=2 * macs, bytes_accessed=16 << 20, transcendentals=heads * q_rows * k_rows
        ),
    )(scalars, grad, saved_q, saved_k, saved_v, *wo, *wq)


def encoder_kernel(count, quarter, sc, kg_ref, vg_ref, *rest):
    wk, wv, out_ref = rest[:count], rest[count : 2 * count], rest[2 * count]
    per = quarter // BLOCK
    kg, vg = kg_ref[...], vg_ref[...]
    for b in range(count):
        src = sc[b]
        cols = pl.ds(pl.multiple_of((src % per) * BLOCK, BLOCK), BLOCK)
        part = dot(kg, wk[b][...], 1, 0) + dot(vg, wv[b][...], 1, 0)
        out_ref[src // per, :, cols] = part.astype(BF16)


def run_encoder(scalars, kg, vg, wk, wv):
    count = len(wk)
    rows, depth = kg.shape
    quarter = count * BLOCK // 4
    step = 256
    whole = pl.BlockSpec((depth, BLOCK), lambda i, sc: (0, 0))
    return pl.pallas_call(
        functools.partial(encoder_kernel, count, quarter),
        grid_spec=pltpu.PrefetchScalarGridSpec(
            num_scalar_prefetch=1,
            grid=(rows // step,),
            in_specs=[pl.BlockSpec((step, depth), lambda i, sc: (i, 0))] * 2
            + [whole] * (2 * count),
            out_specs=pl.BlockSpec((4, step, quarter), lambda i, sc: (0, i, 0)),
        ),
        out_shape=jax.ShapeDtypeStruct((4, rows, quarter), BF16),
        compiler_params=pltpu.CompilerParams(vmem_limit_bytes=48 << 20),
        cost_estimate=pl.CostEstimate(
            flops=16 * rows * depth * quarter, bytes_accessed=14 << 20, transcendentals=0
        ),
    )(scalars, kg, vg, *wk, *wv)


def pick_kernel(sc, local_ref, left_ref, right_ref):
    for c in range(CAP):
        left_ref[c] = local_ref[sc[c]]
        right_ref[c] = local_ref[sc[CAP + c]]


def place_kernel(sc, left_ref, local_ref, right_ref, out_ref):
    tiles = local_ref.shape[0]
    for s in range(tiles):
        i = sc[s]

        @pl.when(i < CAP)
        def _():
            out_ref[s] = left_ref[jnp.minimum(i, CAP - 1)]

        @pl.when((i >= CAP) & (i < CAP + tiles))
        def _():
            out_ref[s] = local_ref[jnp.clip(i - CAP, 0, tiles - 1)]

        @pl.when(i >= CAP + tiles)
        def _():
            out_ref[s] = right_ref[jnp.clip(i - CAP - tiles, 0, CAP - 1)]


def small_call(body, scalars, arrays, outs):
    vmem = pl.BlockSpec(memory_space=pltpu.VMEM)
    single = not isinstance(outs, list)
    return pl.pallas_call(
        body,
        in_specs=[pl.BlockSpec(memory_space=pltpu.SMEM)] + [vmem] * len(arrays),
        out_specs=vmem if single else [vmem] * len(outs),
        out_shape=outs,
        compiler_params=pltpu.CompilerParams(vmem_limit_bytes=24 << 20),
    )(scalars, *arrays)


def gathered(shard):
    full = lax.all_gather(shard, "dp", axis=1, tiled=True)
    blocks = [full[:, i : i + BLOCK] for i in range(0, full.shape[1], BLOCK)]
    return blocks, list(jnp.arange(len(blocks), dtype=jnp.int32))


def chain_kernel(dims, sc, own, top_hbm, q_hbm, k_hbm, v_hbm, wo_hbm, wq_hbm, wk_hbm, wv_hbm,
                 sections_ref, out_ref,
                 wbuf, g, q_ref, k_ref, v_ref, acc, qg, kg, vg, mixed, other, parts, near, fwd, far,
                 kg_in, vg_in, lent, lent_in, back, loc, inc, snd,
                 ldw, ldg, ldq, zs, zr, xs, xr, ms, mr, gs, gr, ks, kr, ps, pr, ys, yr,
                 us, ur, rs, rr, hs, hr, gate):
    q_rows, k_rows, heads, devices = dims
    depth = heads * DH
    scale = DH ** (-0.5)
    seg, me, mp = lax.axis_index("segment"), lax.axis_index("dp"), lax.axis_index("mp")
    z, x = me // 2, me % 2
    side = z // 2
    mesh_id = pl.DeviceIdType.MESH
    plane = {"e": 3 * side, "m": 1 + side, "n": 2 - side, "f": 3 - 3 * side}
    blk = {c: plane[c] * 2 + x for c in plane}
    blk.update({"p" + c: plane[c] * 2 + 1 - x for c in plane})
    at_end = (z == 0) | (z == 3)
    side_peer, cross, core = (seg, z * 2 + 1 - x, mp), (seg, me, 1 - mp), (1 - seg, me, mp)
    diag = jnp.where(x == 0, (me + devices - 1) % devices, (me + 1) % devices)
    end_peer, mid_peer = (seg, plane["e"] * 2 + x, mp), (seg, plane["m"] * 2 + x, mp)
    far_mid = (seg, plane["n"] * 2 + x, mp)
    upper, lower = pl.ds(0, depth // 2), pl.ds(depth // 2, depth // 2)
    whole = pl.ds(0, depth)
    step = 256

    def load(src, dst, sem):
        return pltpu.make_async_copy(src, dst, sem)

    weights = (wo_hbm, wq_hbm, wk_hbm, wv_hbm)
    w_loads = [load(weights[u].at[0], wbuf.at[u, me], ldw.at[u]) for u in range(4)]
    in_loads = [load(a.at[0], b, ldq.at[i])
                for i, (a, b) in enumerate(((q_hbm, q_ref), (k_hbm, k_ref), (v_hbm, v_ref)))]

    def g_load(b):
        cols = pl.ds(pl.multiple_of(b * BLOCK, BLOCK), BLOCK)
        return load(top_hbm.at[:, cols], g.at[b], ldg.at[b])

    w_loads[0].start()

    barrier = pltpu.get_barrier_semaphore()

    def greet(peers):
        for peer in peers:
            pl.semaphore_signal(barrier, inc=1, device_id=peer, device_id_type=mesh_id)

    all_peers = [side_peer, cross, core, (seg, diag, mp)]
    greet(all_peers)

    @pl.when(at_end)
    def _():
        greet([mid_peer])

        @pl.when(seg == 0)
        def _():
            greet([(1, plane["m"] * 2 + x, mp)])

    @pl.when(jnp.logical_not(at_end))
    def _():
        greet([end_peer, far_mid])

        @pl.when(seg == 1)
        def _():
            greet([(0, plane["e"] * 2 + x, mp)])

    @pl.when(seg == 1)
    def _():
        for b in range(8):
            g_load(b).start()

    for c in w_loads[1:] + in_loads:
        c.start()
    for c in w_loads:
        c.wait()

    pl.semaphore_wait(barrier, jnp.where(at_end, 6 - seg, 6 + seg))

    def loop(rows, body):
        def one(i, carry):
            body(pl.ds(pl.multiple_of(i * step, step), step))
            return carry

        lax.fori_loop(0, rows // step, one, 0)

    class Role:
        def __init__(self, end, layer):
            self.end, self.layer = end, layer
            self.pending = []
            self.started = False


        def send(self, src, dst, a, b, peer, cond=None):
            copy = pltpu.make_async_remote_copy(
                src_ref=src, dst_ref=dst, send_sem=a, recv_sem=b, device_id=peer, device_id_type=mesh_id
            )
            self.pending.append((cond, copy))
            if cond is None:
                copy.start()
            else:
                pl.when(cond)(copy.start)

        def recv(self, dst, a, b):
            pltpu.make_async_remote_copy(
                src_ref=dst, dst_ref=dst, send_sem=a, recv_sem=b, device_id=side_peer,
                device_id_type=mesh_id,
            ).wait_recv()

        def finish(self):
            for cond, copy in self.pending:
                if cond is None:
                    copy.wait_send()
                else:
                    pl.when(cond)(copy.wait_send)

        def w(self, u, name, rows=whole):
            return wbuf.at[u, blk[name], rows]

        def zsend(self, kind, u, name, peer, rows=whole):
            ref = self.w(u, name, rows)
            self.send(ref, ref, zs.at[kind, u], zr.at[kind, u], peer)

        def zrecv(self, kind, u, name, rows=whole):
            self.recv(self.w(u, name, rows), zs.at[kind, u], zr.at[kind, u])

        def lent_unit(self, u):
            return self.layer == 1 and u >= 2

        def x_rows(self, u, name):
            if name != "f":
                return whole
            if self.end:
                return lower if u < 2 else whole
            return whole if self.lent_unit(u) else lower

        def xsend(self, u, name):
            ref = self.w(u, name, self.x_rows(u, name))
            i = "emnf".index(name)
            self.send(ref, ref, xs.at[i, u], xr.at[i, u], side_peer)

        def xrecv(self, u, name):
            i = "emnf".index(name)
            self.recv(self.w(u, "p" + name, self.x_rows(u, name)), xs.at[i, u], xr.at[i, u])

        def A(self, u):
            if self.end:
                self.zsend(0, u, "e", mid_peer)
                if not self.lent_unit(u):
                    self.xsend(u, "e")
            else:
                if not self.lent_unit(u):
                    self.zsend(2, u, "m", end_peer)
                self.zsend(6, u, "m", far_mid)
                self.xsend(u, "m")

        def Be(self, u):
            self.zrecv(0, u, "e")
            self.zsend(7, u, "e", far_mid)
            if self.lent_unit(u):
                self.xsend(u, "e")

        def Bp(self, u):
            if self.end:
                self.xrecv(u, "e")
                self.zsend(1, u, "pe", mid_peer)
            elif not self.lent_unit(u):
                self.zrecv(1, u, "pe")
                self.zsend(8, u, "pe", far_mid, upper)

        def Cm(self, u):
            self.zrecv(2, u, "m")
            self.xsend(u, "m")

        def C(self, u):
            if self.end:
                self.zrecv(3, u, "n")
                self.xsend(u, "n")
            else:
                self.zrecv(6, u, "n")
                if not self.lent_unit(u):
                    self.zsend(3, u, "n", end_peer)
                self.xsend(u, "n")

        def Df(self, u):
            if self.end:
                self.zrecv(4, u, "f")
            else:
                self.zrecv(7, u, "f")
                if not self.lent_unit(u):
                    self.zsend(4, u, "f", end_peer)
            self.xsend(u, "f")

        def Dp(self, u):
            if self.end:
                if u < 2:
                    self.zrecv(5, u, "pf", upper)
            elif not self.lent_unit(u):
                self.zrecv(8, u, "pf", upper)
                if u < 2:
                    self.zsend(5, u, "pf", end_peer, upper)


        def out_block(self, name):
            b = blk[name]
            if self.layer == 1:
                g_load(b).wait()
            else:
                self.recv(g.at[b], gs.at[b], gr.at[b])
            first = not self.started
            self.started = True

            def body(rows):
                term = dot(g[b, rows, :], wbuf[0, b], 1, 1)
                acc[rows, :] = term if first else acc[rows, :] + term

            loop(2 * q_rows, body)

        def attend(self, s):
            qs, kb = s * q_rows, s * k_rows
            rows = lax.broadcasted_iota(jnp.int32, (q_rows, k_rows), 0)
            cols = lax.broadcasted_iota(jnp.int32, (q_rows, k_rows), 1)
            allowed = None
            for e in range(2):
                q_len, k_off, k_len = sc[s, e], sc[s, 2 + e] * TILE, sc[s, 4 + e]
                hit = (rows >= e * TILE) & (rows < e * TILE + q_len)
                hit = hit & (cols >= k_off) & (cols < k_off + k_len)
                allowed = hit if allowed is None else allowed | hit

            def one_head(h, carry):
                hd = pl.ds(pl.multiple_of(h * DH, DH), DH)
                og = acc[qs : qs + q_rows, hd].astype(BF16)
                q = q_ref[qs : qs + q_rows, hd]
                k = k_ref[kb : kb + k_rows, hd]
                v = v_ref[kb : kb + k_rows, hd]
                scores = dot(q, k, 1, 1) * scale
                masked = jnp.where(allowed, scores, masked_floor)
                peak = jnp.max(masked, axis=-1, keepdims=True)
                terms = jnp.where(allowed, jnp.exp(masked - peak), 0.0)
                prob = terms / jnp.maximum(jnp.sum(terms, axis=-1, keepdims=True), 1.0)
                prob_bf = prob.astype(BF16)
                attended = dot(prob_bf, v, 1, 0)
                out_dot = jnp.sum(og.astype(F32) * attended, axis=-1, keepdims=True)
                sg = (prob * (dot(og, v, 1, 1) - out_dot)).astype(BF16)
                qg[qs : qs + q_rows, hd] = (dot(sg, k, 1, 0) * scale).astype(BF16)
                kg[kb : kb + k_rows, hd] = (dot(sg, q, 0, 0) * scale).astype(BF16)
                vg[kb : kb + k_rows, hd] = dot(prob_bf, og, 0, 0).astype(BF16)
                return carry

            lax.fori_loop(0, heads, one_head, 0)

        def query_block(self, name):
            b, half = blk[name], plane[name[-1]] // 2

            def body(rows):
                mixed[b, rows, :] = dot(qg[rows, :], wbuf[1, b], 1, 0).astype(BF16)

            loop(2 * q_rows, body)
            self.send(mixed.at[b], other.at[b], ms.at[b], mr.at[b], cross,
                      None if self.layer == 1 else half != mp)

        def section_block(self, name):
            b, half = blk[name], plane[name[-1]] // 2
            cols = pl.ds(pl.multiple_of((b % 4) * BLOCK, BLOCK), BLOCK)

            def total(rows):
                change = mixed[b, rows, :].astype(F32) + other[b, rows, :].astype(F32)
                return (g[b, rows, :].astype(F32) + change).astype(BF16)

            def keep(value):
                @pl.when(half == mp)
                def _():
                    def body(rows):
                        sections_ref[0, rows, cols] = value(rows)

                    loop(2 * q_rows, body)

            if self.layer == 1:
                self.recv(other.at[b], ms.at[b], mr.at[b])

                def body(rows):
                    g[b, rows, :] = total(rows)

                loop(2 * q_rows, body)
                self.send(g.at[b], g.at[b], gs.at[b], gr.at[b], core)
                keep(lambda rows: g[b, rows, :])
            else:

                @pl.when(half == mp)
                def _():
                    self.recv(other.at[b], ms.at[b], mr.at[b])

                keep(total)

        def project(self, kref, vref, dst, b):
            def body(rows):
                part = dot(kref[rows, :], wbuf[2, b], 1, 0) + dot(vref[rows, :], wbuf[3, b], 1, 0)
                dst[b, rows, :] = part.astype(BF16)

            loop(2 * k_rows, body)

        def encode(self, name):
            b, p = blk[name], plane[name[-1]]
            self.project(kg, vg, parts, b)
            if not (self.end and self.layer == 1):
                self.send(parts.at[b], near.at[b % 4], ps.at[b], pr.at[b], core, p // 2 != self.layer)

        def encode_lent(self, name):
            b, p = blk[name], plane[name[-1]]
            self.project(kg_in, vg_in, lent, b)
            i = (p // 2) * 2 + b % 2
            self.send(lent.at[b], lent_in.at[i], us.at[i], ur.at[i], cross, p % 2 != mp)

        def give_back(self, name):
            b, p = blk[name], plane[name[-1]]
            i = (p // 2) * 2 + b % 2

            @pl.when(p % 2 == mp)
            def _():
                self.recv(lent_in.at[i], us.at[i], ur.at[i])

                def body(rows):
                    both = lent[b, rows, :].astype(F32) + lent_in[i, rows, :].astype(F32)
                    lent[b, rows, :] = both.astype(BF16)

                loop(2 * k_rows, body)

            self.send(lent.at[b], back.at[b % 2], rs.at[i], rr.at[b % 2],
                      (p // 2, plane["e"] * 2 + x, mp), p % 2 == mp)

        def reduce_cores(self, name):
            b, p, j = blk[name], plane[name[-1]], blk[name] % 2
            here = p // 2 == self.layer
            onward = here & (p % 2 != mp)
            single = self.end and self.layer == 0
            if single:
                self.send(parts.at[b], far.at[j], ys.at[j], yr.at[j], cross, onward)
                return

            @pl.when(here)
            def _():
                self.recv(near.at[b % 4], ps.at[b], pr.at[b])

            if self.end:
                self.send(near.at[b % 4], far.at[j], ys.at[j], yr.at[j], cross, onward)
                return

            def both(rows):
                return (parts[b, rows, :].astype(F32) + near[b % 4, rows, :].astype(F32)).astype(BF16)

            @pl.when(onward)
            def _():
                def body(rows):
                    fwd[j, rows, :] = both(rows)

                loop(2 * k_rows, body)

            self.send(fwd.at[j], far.at[j], ys.at[j], yr.at[j], cross, onward)

        def reduce_heads(self, name):
            b, p, j = blk[name], plane[name[-1]], blk[name] % 2
            mine = (p // 2 == self.layer) & (p % 2 == mp)

            @pl.when(mine)
            def _():
                self.recv(far.at[j], ys.at[j], yr.at[j])
                if self.end:
                    self.recv(back.at[j], rs.at[j], rr.at[j])

                def body(t, carry):
                    rows = pl.ds(pl.multiple_of(t * TILE, TILE), TILE)
                    total = far[j, rows, :].astype(F32)
                    if self.end:
                        total += back[j, rows, :].astype(F32)
                    if not (self.end and self.layer == 1):
                        total += parts[b, rows, :].astype(F32)
                    if not (self.end and self.layer == 0):
                        total += near[b % 4, rows, :].astype(F32)
                    loc[j, t] = total.astype(BF16)
                    return carry

                lax.fori_loop(0, 2 * k_rows // TILE, body, 0)
                for c in range(CAP):
                    snd[j, c] = loc[j, pick_left[c]]
                    snd[j, CAP + c] = loc[j, pick_right[c]]

            left, right = (seg, (me + devices - 1) % devices, mp), (seg, (me + 1) % devices, mp)
            to_left, to_right = pl.ds(0, CAP), pl.ds(CAP, CAP)
            self.send(snd.at[j, to_left], inc.at[j, to_right], hs.at[j, 0], hr.at[j, 0], left, mine)
            self.send(snd.at[j, to_right], inc.at[j, to_left], hs.at[j, 1], hr.at[j, 1], right, mine)

        def place(self):
            for j in range(2):
                self.recv(inc.at[j, pl.ds(CAP, CAP)], hs.at[j, 0], hr.at[j, 0])
                self.recv(inc.at[j, pl.ds(0, CAP)], hs.at[j, 1], hr.at[j, 1])
            for j in range(2):
                for t in range(tiles):
                    i = take[t]
                    kept = loc[j, jnp.minimum(i, tiles - 1)]
                    came = inc[j, jnp.clip(i - tiles, 0, 2 * CAP - 1)]
                    out_ref[t * TILE : (t + 1) * TILE, j * BLOCK : (j + 1) * BLOCK] = jnp.where(
                        i < tiles, kept, came
                    )

    tiles = 2 * k_rows // TILE
    per = tiles // 2

    def globals_of(source):
        return [own[source * 2 + t // per, t % per] for t in range(tiles)]

    def picks(goes, to):
        seen, chosen = jnp.int32(0), [jnp.int32(0)] * CAP
        for t in range(tiles):
            hit = (goes[t] >= to * tiles) & (goes[t] < (to + 1) * tiles)
            chosen = [jnp.where(hit & (seen == c), t, chosen[c]) for c in range(CAP)]
            seen = seen + hit.astype(jnp.int32)
        return chosen

    left_of, right_of = (me + devices - 1) % devices, (me + 1) % devices
    mine_goes = globals_of(me)
    pick_left, pick_right = picks(mine_goes, left_of), picks(mine_goes, right_of)
    take = [jnp.int32(0)] * tiles
    for source, base in ((me, 0), (left_of, tiles), (right_of, tiles + CAP)):
        goes = mine_goes if base == 0 else globals_of(source)
        seen = jnp.int32(0)
        for t in range(tiles):
            slot = goes[t] - me * tiles
            hit = (slot >= 0) & (slot < tiles)
            value = t if base == 0 else base + seen
            take = [jnp.where(slot == s, value, take[s]) for s in range(tiles)]
            seen = seen + hit.astype(jnp.int32)

    def mid_upper():
        r = Role(False, 1)
        r.A(0)
        r.out_block("m")
        r.Be(0)
        r.out_block("e")
        r.C(0)
        r.out_block("n")
        r.Bp(0)
        r.out_block("pe")
        r.Df(0)
        r.A(1)
        pl.semaphore_signal(gate, inc=1, device_id=core, device_id_type=mesh_id)
        r.out_block("f")
        r.xrecv(0, "m")
        r.out_block("pm")
        r.xrecv(0, "n")
        r.out_block("pn")
        r.Dp(0)
        r.xrecv(0, "f")
        r.out_block("pf")
        for c in in_loads:
            c.wait()
        r.attend(0)
        r.Be(1)
        r.C(1)
        r.attend(1)
        r.query_block("m")
        r.query_block("e")
        r.Bp(1)
        r.query_block("n")
        r.query_block("pe")
        r.Df(1)
        r.A(2)
        r.A(3)
        r.section_block("m")
        r.query_block("f")
        r.section_block("e")
        r.xrecv(1, "m")
        r.query_block("pm")
        r.section_block("n")
        r.section_block("pe")
        r.xrecv(1, "n")
        r.query_block("pn")
        r.section_block("f")
        r.section_block("pm")
        r.Dp(1)
        r.xrecv(1, "f")
        r.query_block("pf")
        r.section_block("pn")
        r.Be(2)
        r.Be(3)
        r.section_block("pf")
        r.encode("m")
        r.C(2)
        r.C(3)
        r.encode("e")
        r.encode("n")
        r.xrecv(2, "m")
        r.xrecv(3, "m")
        r.encode("pm")
        r.Df(2)
        r.Df(3)
        r.encode("f")
        r.recv(kg_in, ks.at[0], kr.at[0])
        r.recv(vg_in, ks.at[1], kr.at[1])
        r.encode_lent("m")
        r.encode_lent("e")
        r.encode_lent("n")
        r.give_back("m")
        r.encode_lent("pm")
        r.give_back("e")
        r.encode_lent("f")
        r.give_back("n")
        last = "pm"
        before = "f"
        for name in ("e", "n", "f"):
            r.xrecv(2, name)
            r.xrecv(3, name)
            r.encode("p" + name)
            r.encode_lent("p" + name)
            r.give_back(last)
            last, before = before, "p" + name
        r.give_back(last)
        r.give_back(before)
        reduce_all(r)

    def reduce_all(r):
        names = order_mid if not r.end else order_end
        for i, name in enumerate(names):
            r.reduce_cores(name)
            if i:
                r.reduce_heads(names[i - 1])
        r.reduce_heads(names[-1])
        r.place()
        r.finish()

    order_mid = ["m", "e", "pm", "pe", "n", "pn", "f", "pf"]
    order_end = ["e", "pe", "m", "pm", "n", "pn", "f", "pf"]

    def mid_lower():
        r = Role(False, 0)
        pl.semaphore_wait(gate, 1)
        r.A(0)
        r.Be(0)
        r.C(0)
        r.Bp(0)
        r.Df(0)
        r.A(1)
        r.Dp(0)
        for name in "mnf":
            r.xrecv(0, name)
        r.Be(1)
        r.C(1)
        r.Bp(1)
        r.out_block("m")
        r.out_block("e")
        r.Df(1)
        r.A(2)
        r.A(3)
        r.out_block("n")
        r.out_block("pe")
        r.out_block("f")
        r.Dp(1)
        r.out_block("pm")
        r.out_block("pn")
        r.out_block("pf")
        for c in in_loads:
            c.wait()
        r.attend(0)
        r.Be(2)
        r.Be(3)
        r.attend(1)
        r.C(2)
        r.C(3)
        for name in ("m", "e", "n", "pe"):
            r.query_block(name)
        r.Bp(2)
        r.Bp(3)
        for name in "mnf":
            r.xrecv(1, name)
        for name in ("f", "pm", "pn", "pf"):
            r.query_block(name)
        r.Df(2)
        r.Df(3)
        r.encode("m")
        r.encode("e")
        r.reduce_cores("m")
        for name in ("m", "e", "n", "pe"):
            r.section_block(name)
        r.xrecv(2, "m")
        r.xrecv(3, "m")
        r.encode("pm")
        r.reduce_cores("e")
        r.reduce_heads("m")
        r.encode("pe")
        r.reduce_cores("pm")
        r.reduce_heads("e")
        r.Dp(2)
        r.Dp(3)
        for name in ("f", "pm", "pn", "pf"):
            r.section_block(name)
        r.encode("n")
        r.reduce_cores("pe")
        r.reduce_heads("pm")
        r.xrecv(2, "n")
        r.xrecv(3, "n")
        r.encode("pn")
        r.reduce_cores("n")
        r.reduce_heads("pe")
        r.encode("f")
        r.reduce_cores("pn")
        r.reduce_heads("n")
        r.xrecv(2, "f")
        r.xrecv(3, "f")
        r.encode("pf")
        r.reduce_cores("f")
        r.reduce_heads("pn")
        r.reduce_cores("pf")
        r.reduce_heads("f")
        r.reduce_heads("pf")
        r.place()
        r.finish()

    def end_upper():
        r = Role(True, 1)
        r.A(0)
        r.out_block("e")
        r.Cm(0)
        r.Bp(0)
        r.out_block("m")
        r.C(0)
        r.out_block("pe")
        r.A(1)
        r.out_block("n")
        r.Df(0)
        pl.semaphore_signal(gate, inc=1, device_id=core, device_id_type=mesh_id)
        r.out_block("f")
        r.xrecv(0, "m")
        r.out_block("pm")
        r.xrecv(0, "n")
        r.out_block("pn")
        r.Dp(0)
        r.xrecv(0, "f")
        r.out_block("pf")
        for c in in_loads:
            c.wait()
        r.attend(0)
        r.Cm(1)
        r.Bp(1)
        r.attend(1)
        r.C(1)
        r.send(kg, kg_in, ks.at[0], kr.at[0], mid_peer)
        r.send(vg, vg_in, ks.at[1], kr.at[1], mid_peer)
        r.A(2)
        r.A(3)
        r.query_block("e")
        r.query_block("pe")
        r.query_block("m")
        r.section_block("e")
        r.query_block("n")
        r.section_block("pe")
        r.Df(1)
        r.query_block("f")
        r.section_block("m")
        r.xrecv(1, "m")
        r.query_block("pm")
        r.section_block("n")
        r.xrecv(1, "n")
        r.query_block("pn")
        r.section_block("f")
        r.section_block("pm")
        r.Dp(1)
        r.xrecv(1, "f")
        r.query_block("pf")
        r.section_block("pn")
        r.section_block("pf")
        reduce_all(r)

    def end_lower():
        r = Role(True, 0)
        pl.semaphore_wait(gate, 1)
        r.A(0)
        r.Cm(0)
        r.Bp(0)
        r.C(0)
        r.A(1)
        r.Df(0)
        r.Cm(1)
        r.Bp(1)
        r.Dp(0)
        for name in "mnf":
            r.xrecv(0, name)
        r.C(1)
        r.A(2)
        r.A(3)
        r.out_block("e")
        r.out_block("pe")
        r.out_block("m")
        r.out_block("n")
        r.Df(1)
        r.out_block("f")
        r.out_block("pm")
        r.out_block("pn")
        r.Dp(1)
        r.out_block("pf")
        for c in in_loads:
            c.wait()
        r.attend(0)
        r.Cm(2)
        r.Cm(3)
        r.Bp(2)
        r.Bp(3)
        r.attend(1)
        r.C(2)
        r.C(3)
        for name in ("e", "pe", "m", "n"):
            r.query_block(name)
        for name in "mnf":
            r.xrecv(1, name)
        for name in ("f", "pm", "pn", "pf"):
            r.query_block(name)
        r.encode("e")
        r.encode("pe")
        r.reduce_cores("e")
        r.encode("m")
        r.reduce_cores("pe")
        r.Df(2)
        r.Df(3)
        for name in ("e", "pe", "m", "n"):
            r.section_block(name)
        r.xrecv(2, "m")
        r.xrecv(3, "m")
        r.encode("pm")
        r.reduce_cores("m")
        for name in ("f", "pm", "pn", "pf"):
            r.section_block(name)
        r.encode("n")
        r.reduce_cores("pm")
        r.xrecv(2, "n")
        r.xrecv(3, "n")
        r.encode("pn")
        r.reduce_cores("n")
        r.encode("f")
        r.reduce_cores("pn")
        r.xrecv(2, "f")
        r.xrecv(3, "f")
        r.reduce_cores("f")
        r.encode("pf")
        r.reduce_cores("pf")
        for name in order_end:
            r.reduce_heads(name)
        r.place()
        r.finish()

    for wanted_end, layer, program in (
        (False, 1, mid_upper), (False, 0, mid_lower), (True, 1, end_upper), (True, 0, end_lower)
    ):
        place_here = at_end if wanted_end else jnp.logical_not(at_end)
        pl.when(place_here & (seg == layer))(program)


def run_chain(scalars, owners, top, q, k, v, wo, wq, wk, wv, devices):
    micro = scalars.shape[0]
    q_rows, k_rows = top.shape[0] // micro, k.shape[1] // micro
    width, depth = top.shape[1], q.shape[2]
    half, blocks = width // 2, width // BLOCK
    keys = micro * k_rows
    tiles = keys // TILE
    smem, vmem, any_ = (pl.BlockSpec(memory_space=m) for m in (pltpu.SMEM, pltpu.VMEM, pl.ANY))
    dma = pltpu.SemaphoreType.DMA

    def buf(*shape, dtype=BF16):
        return pltpu.VMEM(shape, dtype)

    return pl.pallas_call(
        functools.partial(chain_kernel, (q_rows, k_rows, depth // DH, devices)),
        in_specs=[smem, smem] + [any_] * 8,
        out_specs=[vmem, vmem],
        out_shape=[
            jax.ShapeDtypeStruct((1, micro * q_rows, half), BF16),
            jax.ShapeDtypeStruct((keys, width // 4), BF16),
        ],
        scratch_shapes=[
            buf(4, blocks, depth, BLOCK),
            buf(blocks, micro * q_rows, BLOCK),
            buf(micro * q_rows, depth),
            buf(keys, depth),
            buf(keys, depth),
            buf(micro * q_rows, depth, dtype=F32),
            buf(micro * q_rows, depth),
            buf(keys, depth),
            buf(keys, depth),
            buf(blocks, micro * q_rows, BLOCK),
            buf(blocks, micro * q_rows, BLOCK),
            buf(blocks, keys, BLOCK),
            buf(4, keys, BLOCK),
            buf(2, keys, BLOCK),
            buf(2, keys, BLOCK),
            buf(keys, depth),
            buf(keys, depth),
            buf(blocks, keys, BLOCK),
            buf(4, keys, BLOCK),
            buf(2, keys, BLOCK),
            buf(2, tiles, TILE, BLOCK),
            buf(2, 2 * CAP, TILE, BLOCK),
            buf(2, 2 * CAP, TILE, BLOCK),
        ]
        + [dma((4,)), dma((8,)), dma((3,))]
        + [dma((9, 4))] * 2
        + [dma((4, 4))] * 2
        + [dma((8,))] * 4
        + [dma((2,))] * 2
        + [dma((8,))] * 2
        + [dma((2,))] * 2
        + [dma((4,))] * 2
        + [dma((4,)), dma((2,))]
        + [dma((2, 2))] * 2
        + [pltpu.SemaphoreType.REGULAR],
        compiler_params=pltpu.CompilerParams(
            collective_id=0, has_side_effects=True, vmem_limit_bytes=60 << 20
        ),
    )(scalars, owners, top, q, k, v, wo, wq, wk, wv)


def ranked(marked):
    ids = jnp.arange(marked.shape[0], dtype=jnp.int32)
    upto = ids[None, :] <= ids[:, None]
    return jnp.sum((upto & marked[None, :]).astype(jnp.int32), axis=1) - 1


def on_device(
    grad_top,
    saved_query,
    saved_key,
    saved_value,
    w_query,
    w_key,
    w_value,
    w_out,
    query_length,
    key_offset,
    key_length,
    tile_owner,
):
    seg = lax.axis_index("segment")
    mp = lax.axis_index("mp")
    devices = lax.axis_size("dp")
    me = lax.axis_index("dp")
    micro = query_length.shape[0]
    q_rows = grad_top.shape[0] // micro
    k_rows = saved_key.shape[1] // micro
    half = grad_top.shape[1] // 2
    mp_swap = [(0, 1), (1, 0)]
    if w_out.shape[2] == BLOCK and devices == 8 and micro == 2:
        table = jnp.concatenate([query_length, key_offset, key_length], axis=1)
        return run_chain(
            table, tile_owner, grad_top, saved_query, saved_key, saved_value, w_out, w_query, w_key,
            w_value, devices,
        )

    wo, sources = gathered(w_out[0])
    wq, _ = gathered(w_query[0])
    wk, _ = gathered(w_key[0])
    wv, _ = gathered(w_value[0])
    order = jnp.stack(sources).astype(jnp.int32)

    top = grad_top.reshape(grad_top.shape[0], 2, half).transpose(1, 0, 2)
    scalars = [
        jnp.concatenate([order, query_length[s], key_offset[s], key_length[s]])
        for s in range(micro)
    ]

    def tick(s, grad, at):
        return run_tick(
            scalars[s], grad, at, s, saved_query, saved_key, saved_value, wo, wq, q_rows, k_rows
        )

    upper = [tick(s, top, s) for s in range(micro)]
    upper_half, incoming = [], []
    for s in range(micro):
        mixed = upper[s][0]
        other = lax.ppermute(mixed, "mp", mp_swap)
        rows = top[:, s * q_rows : (s + 1) * q_rows]
        section = (rows.astype(F32) + (mixed.astype(F32) + other.astype(F32))).astype(BF16)
        incoming.append(lax.ppermute(section, "segment", [(1, 0)]))
        upper_half.append(lax.dynamic_index_in_dim(section, mp, 0, keepdims=False))
    lower = [tick(s, incoming[s], 0) for s in range(micro)]
    halves = []
    for s in range(micro):
        mixed = lower[s][0]
        other = lax.ppermute(
            lax.dynamic_index_in_dim(mixed, 1 - mp, 0, keepdims=False), "mp", mp_swap
        )
        own = lax.dynamic_index_in_dim(mixed, mp, 0, keepdims=False)
        base = lax.dynamic_index_in_dim(incoming[s], mp, 0, keepdims=False)
        low = (base.astype(F32) + (own.astype(F32) + other.astype(F32))).astype(BF16)
        halves.append(jnp.where(seg == 1, upper_half[s], low))
    sections = jnp.concatenate(halves, axis=0)[None]

    kg = jnp.concatenate([jnp.where(seg == 1, upper[s][1], lower[s][1]) for s in range(micro)], 0)
    vg = jnp.concatenate([jnp.where(seg == 1, upper[s][2], lower[s][2]) for s in range(micro)], 0)
    parts = run_encoder(order, kg, vg, wk, wv)
    away = lax.dynamic_slice_in_dim(parts, (1 - seg) * 2, 2, 0)
    mine = lax.dynamic_slice_in_dim(parts, seg * 2, 2, 0)
    arrived = lax.ppermute(away, "segment", mp_swap)
    summed = (mine.astype(F32) + arrived.astype(F32)).astype(BF16)
    crossing = lax.ppermute(
        lax.dynamic_index_in_dim(summed, 1 - mp, 0, keepdims=False), "mp", mp_swap
    )
    kept = lax.dynamic_index_in_dim(summed, mp, 0, keepdims=False)
    kept = (kept.astype(F32) + crossing.astype(F32)).astype(BF16)

    tiles = kept.shape[0] // TILE
    features = kept.shape[1]
    owners = tile_owner.reshape(devices, tiles)
    slot_ids = jnp.arange(CAP, dtype=jnp.int32)[:, None]
    tile_ids = jnp.arange(tiles, dtype=jnp.int32)

    def plan(source):
        source = source % devices
        row = lax.dynamic_index_in_dim(owners, source, 0, keepdims=False)
        return (row // tiles - source + devices) % devices, row % tiles

    def ranks_of(marked):
        return (ranked(marked)[None, :] == slot_ids) & marked[None, :]

    step, slot = plan(me)
    left_step, left_slot = plan(me - 1 + devices)
    right_step, right_slot = plan(me + 1)
    send_left = jnp.sum(jnp.where(ranks_of(step == devices - 1), tile_ids[None, :], 0), axis=1)
    send_right = jnp.sum(jnp.where(ranks_of(step == 1), tile_ids[None, :], 0), axis=1)
    left_hit = ranks_of(left_step == 1)
    right_hit = ranks_of(right_step == devices - 1)
    target = jnp.concatenate(
        [
            jnp.sum(jnp.where(left_hit, left_slot[None, :], 0), axis=1),
            slot,
            jnp.sum(jnp.where(right_hit, right_slot[None, :], 0), axis=1),
        ]
    )
    usable = jnp.concatenate([jnp.any(left_hit, axis=1), step == 0, jnp.any(right_hit, axis=1)])
    chosen = (tile_ids[:, None] == target[None, :]) & usable[None, :]
    candidate_ids = jnp.arange(target.shape[0], dtype=jnp.int32)
    take = jnp.sum(jnp.where(chosen, candidate_ids[None, :], 0), axis=1)

    tiled = (tiles, TILE, features)
    shape = jax.ShapeDtypeStruct(tiled, BF16)
    handed = jax.ShapeDtypeStruct((CAP, TILE, features), BF16)
    local = kept.reshape(tiled)
    to_left, to_right = small_call(
        pick_kernel, jnp.concatenate([send_left, send_right]), [local], [handed, handed]
    )
    forward = [(i, (i + 1) % devices) for i in range(devices)]
    backward = [(b, a) for a, b in forward]
    from_left = lax.ppermute(to_right, "dp", forward)
    from_right = lax.ppermute(to_left, "dp", backward)
    owned = small_call(place_kernel, take, [from_left, local, from_right], shape)
    return sections, owned.reshape(tiles * TILE, features)


def solution(mesh):
    in_specs = (
        P("dp", None),
        P("segment", "dp", "mp"),
        P("segment", "dp", "mp"),
        P("segment", "dp", "mp"),
        P("segment", "mp", "dp"),
        P("segment", "mp", "dp"),
        P("segment", "mp", "dp"),
        P("segment", "mp", "dp"),
        P("dp", None),
        P("dp", None),
        P("dp", None),
        P(),
    )
    out_specs = (P("segment", "dp", "mp"), P("dp", ("segment", "mp")))
    return jax.shard_map(
        on_device, mesh=mesh, in_specs=in_specs, out_specs=out_specs, check_vma=False
    )
```

```python
import functools

import jax
import jax.numpy as jnp
from jax import lax
from jax.experimental import pallas as pl
from jax.experimental.pallas import tpu as pltpu
from jax.sharding import PartitionSpec as P

DH = 256
TILE = 128
CAP = 2
BLOCK = 256
masked_floor = -1e30
BF16, F32 = jnp.bfloat16, jnp.float32


def dot(a, b, ca, cb):
    return lax.dot_general(a, b, (((ca,), (cb,)), ((), ())), preferred_element_type=F32)


def tick_kernel(count, half, sc, g_ref, q_ref, k_ref, v_ref, *rest):
    wo, wq = rest[:count], rest[count : 2 * count]
    mixed_ref, kg_ref, vg_ref, acc = rest[2 * count :]
    head = pl.program_id(0)
    per = half // BLOCK
    scale = DH ** (-0.5)

    def place(b):
        src = sc[b]
        return src // per, pl.ds(pl.multiple_of((src % per) * BLOCK, BLOCK), BLOCK)

    og = None
    for b in range(count):
        at, cols = place(b)
        term = dot(g_ref[at, :, cols], wo[b][...], 1, 1)
        og = term if og is None else og + term
    og = og.astype(BF16)
    q, k, v = q_ref[0], k_ref[0], v_ref[0]
    scores = dot(q, k, 1, 1) * scale
    rows = lax.broadcasted_iota(jnp.int32, scores.shape, 0)
    cols_id = lax.broadcasted_iota(jnp.int32, scores.shape, 1)
    allowed = None
    for e in range(2):
        q_len, k_off, k_len = sc[count + e], sc[count + 2 + e] * TILE, sc[count + 4 + e]
        hit = (rows >= e * TILE) & (rows < e * TILE + q_len)
        hit = hit & (cols_id >= k_off) & (cols_id < k_off + k_len)
        allowed = hit if allowed is None else allowed | hit
    masked = jnp.where(allowed, scores, masked_floor)
    top = jnp.max(masked, axis=-1, keepdims=True)
    terms = jnp.where(allowed, jnp.exp(masked - top), 0.0)
    prob = terms / jnp.maximum(jnp.sum(terms, axis=-1, keepdims=True), 1.0)
    prob_bf = prob.astype(BF16)
    attended = dot(prob_bf, v, 1, 0)
    out_dot = jnp.sum(og.astype(F32) * attended, axis=-1, keepdims=True)
    sg = (prob * (dot(og, v, 1, 1) - out_dot)).astype(BF16)
    qg = (dot(sg, k, 1, 0) * scale).astype(BF16)
    kg_ref[...] = (dot(sg, q, 0, 0) * scale).astype(BF16)
    vg_ref[...] = dot(prob_bf, og, 0, 0).astype(BF16)

    @pl.when(head == 0)
    def _():
        acc[...] = jnp.zeros_like(acc)

    for b in range(count):
        at, cols = place(b)
        acc[at, :, cols] += dot(qg, wq[b][...], 1, 0)

    @pl.when(head == pl.num_programs(0) - 1)
    def _():
        mixed_ref[...] = acc[...].astype(BF16)


def run_tick(scalars, grad, at, seq, saved_q, saved_k, saved_v, wo, wq, q_rows, k_rows):
    half = grad.shape[2]
    heads = saved_q.shape[2] // DH
    count = len(wo)
    weight = pl.BlockSpec((DH, BLOCK), lambda h, sc: (h, 0))
    macs = heads * q_rows * DH * (4 * half + 6 * k_rows)
    return pl.pallas_call(
        functools.partial(tick_kernel, count, half),
        grid_spec=pltpu.PrefetchScalarGridSpec(
            num_scalar_prefetch=1,
            grid=(heads,),
            in_specs=[
                pl.BlockSpec((2, q_rows, half), lambda h, sc: (0, at, 0)),
                pl.BlockSpec((1, q_rows, DH), lambda h, sc: (0, seq, h)),
                pl.BlockSpec((1, k_rows, DH), lambda h, sc: (0, seq, h)),
                pl.BlockSpec((1, k_rows, DH), lambda h, sc: (0, seq, h)),
            ]
            + [weight] * (2 * count),
            out_specs=[
                pl.BlockSpec((2, q_rows, half), lambda h, sc: (0, 0, 0)),
                pl.BlockSpec((k_rows, DH), lambda h, sc: (0, h)),
                pl.BlockSpec((k_rows, DH), lambda h, sc: (0, h)),
            ],
            scratch_shapes=[pltpu.VMEM((2, q_rows, half), F32)],
        ),
        out_shape=[
            jax.ShapeDtypeStruct((2, q_rows, half), BF16),
            jax.ShapeDtypeStruct((k_rows, heads * DH), BF16),
            jax.ShapeDtypeStruct((k_rows, heads * DH), BF16),
        ],
        compiler_params=pltpu.CompilerParams(vmem_limit_bytes=40 << 20),
        cost_estimate=pl.CostEstimate(
            flops=2 * macs, bytes_accessed=16 << 20, transcendentals=heads * q_rows * k_rows
        ),
    )(scalars, grad, saved_q, saved_k, saved_v, *wo, *wq)


def encoder_kernel(count, quarter, sc, kg_ref, vg_ref, *rest):
    wk, wv, out_ref = rest[:count], rest[count : 2 * count], rest[2 * count]
    per = quarter // BLOCK
    kg, vg = kg_ref[...], vg_ref[...]
    for b in range(count):
        src = sc[b]
        cols = pl.ds(pl.multiple_of((src % per) * BLOCK, BLOCK), BLOCK)
        part = dot(kg, wk[b][...], 1, 0) + dot(vg, wv[b][...], 1, 0)
        out_ref[src // per, :, cols] = part.astype(BF16)


def run_encoder(scalars, kg, vg, wk, wv):
    count = len(wk)
    rows, depth = kg.shape
    quarter = count * BLOCK // 4
    step = 256
    whole = pl.BlockSpec((depth, BLOCK), lambda i, sc: (0, 0))
    return pl.pallas_call(
        functools.partial(encoder_kernel, count, quarter),
        grid_spec=pltpu.PrefetchScalarGridSpec(
            num_scalar_prefetch=1,
            grid=(rows // step,),
            in_specs=[pl.BlockSpec((step, depth), lambda i, sc: (i, 0))] * 2
            + [whole] * (2 * count),
            out_specs=pl.BlockSpec((4, step, quarter), lambda i, sc: (0, i, 0)),
        ),
        out_shape=jax.ShapeDtypeStruct((4, rows, quarter), BF16),
        compiler_params=pltpu.CompilerParams(vmem_limit_bytes=48 << 20),
        cost_estimate=pl.CostEstimate(
            flops=16 * rows * depth * quarter, bytes_accessed=14 << 20, transcendentals=0
        ),
    )(scalars, kg, vg, *wk, *wv)


def pick_kernel(sc, local_ref, left_ref, right_ref):
    for c in range(CAP):
        left_ref[c] = local_ref[sc[c]]
        right_ref[c] = local_ref[sc[CAP + c]]


def place_kernel(sc, left_ref, local_ref, right_ref, out_ref):
    tiles = local_ref.shape[0]
    for s in range(tiles):
        i = sc[s]

        @pl.when(i < CAP)
        def _():
            out_ref[s] = left_ref[jnp.minimum(i, CAP - 1)]

        @pl.when((i >= CAP) & (i < CAP + tiles))
        def _():
            out_ref[s] = local_ref[jnp.clip(i - CAP, 0, tiles - 1)]

        @pl.when(i >= CAP + tiles)
        def _():
            out_ref[s] = right_ref[jnp.clip(i - CAP - tiles, 0, CAP - 1)]


def small_call(body, scalars, arrays, outs):
    vmem = pl.BlockSpec(memory_space=pltpu.VMEM)
    single = not isinstance(outs, list)
    return pl.pallas_call(
        body,
        in_specs=[pl.BlockSpec(memory_space=pltpu.SMEM)] + [vmem] * len(arrays),
        out_specs=vmem if single else [vmem] * len(outs),
        out_shape=outs,
        compiler_params=pltpu.CompilerParams(vmem_limit_bytes=24 << 20),
    )(scalars, *arrays)


def gathered(shard):
    full = lax.all_gather(shard, "dp", axis=1, tiled=True)
    blocks = [full[:, i : i + BLOCK] for i in range(0, full.shape[1], BLOCK)]
    return blocks, list(jnp.arange(len(blocks), dtype=jnp.int32))


def chain_kernel(dims, sc, own, top_hbm, q_hbm, k_hbm, v_hbm, wo_hbm, wq_hbm, wk_hbm, wv_hbm,
                 sections_ref, out_ref,
                 wbuf, g, q_ref, k_ref, v_ref, acc, qg, kg, vg, mixed, other, parts, near, fwd, far,
                 kg_in, vg_in, lent, lent_in, back, loc, inc, snd,
                 ldw, ldg, ldq, zs, zr, xs, xr, ms, mr, gs, gr, ks, kr, ps, pr, ys, yr,
                 us, ur, rs, rr, hs, hr, gate):
    q_rows, k_rows, heads, devices = dims
    depth = heads * DH
    scale = DH ** (-0.5)
    seg, me, mp = lax.axis_index("segment"), lax.axis_index("dp"), lax.axis_index("mp")
    z, x = me // 2, me % 2
    side = z // 2
    mesh_id = pl.DeviceIdType.MESH
    plane = {"e": 3 * side, "m": 1 + side, "n": 2 - side, "f": 3 - 3 * side}
    blk = {c: plane[c] * 2 + x for c in plane}
    blk.update({"p" + c: plane[c] * 2 + 1 - x for c in plane})
    at_end = (z == 0) | (z == 3)
    side_peer, cross, core = (seg, z * 2 + 1 - x, mp), (seg, me, 1 - mp), (1 - seg, me, mp)
    diag = jnp.where(x == 0, (me + devices - 1) % devices, (me + 1) % devices)
    end_peer, mid_peer = (seg, plane["e"] * 2 + x, mp), (seg, plane["m"] * 2 + x, mp)
    far_mid = (seg, plane["n"] * 2 + x, mp)
    upper, lower = pl.ds(0, depth // 2), pl.ds(depth // 2, depth // 2)
    whole = pl.ds(0, depth)
    step = 256

    def load(src, dst, sem):
        return pltpu.make_async_copy(src, dst, sem)

    weights = (wo_hbm, wq_hbm, wk_hbm, wv_hbm)
    w_loads = [load(weights[u].at[0], wbuf.at[u, me], ldw.at[u]) for u in range(4)]
    in_loads = [load(a.at[0], b, ldq.at[i])
                for i, (a, b) in enumerate(((q_hbm, q_ref), (k_hbm, k_ref), (v_hbm, v_ref)))]

    def g_load(b):
        cols = pl.ds(pl.multiple_of(b * BLOCK, BLOCK), BLOCK)
        return load(top_hbm.at[:, cols], g.at[b], ldg.at[b])

    w_loads[0].start()

    barrier = pltpu.get_barrier_semaphore()

    def greet(peers):
        for peer in peers:
            pl.semaphore_signal(barrier, inc=1, device_id=peer, device_id_type=mesh_id)

    all_peers = [side_peer, cross, core, (seg, diag, mp)]
    greet(all_peers)

    @pl.when(at_end)
    def _():
        greet([mid_peer])

        @pl.when(seg == 0)
        def _():
            greet([(1, plane["m"] * 2 + x, mp)])

    @pl.when(jnp.logical_not(at_end))
    def _():
        greet([end_peer, far_mid])

        @pl.when(seg == 1)
        def _():
            greet([(0, plane["e"] * 2 + x, mp)])

    @pl.when(seg == 1)
    def _():
        for b in range(8):
            g_load(b).start()

    for c in w_loads[1:] + in_loads:
        c.start()
    for c in w_loads:
        c.wait()

    pl.semaphore_wait(barrier, jnp.where(at_end, 6 - seg, 6 + seg))

    def loop(rows, body):
        def one(i, carry):
            body(pl.ds(pl.multiple_of(i * step, step), step))
            return carry

        lax.fori_loop(0, rows // step, one, 0)

    def each(names, body):
        ids = [blk[n] for n in names]

        def one(i, carry):
            b = ids[0]
            for j in range(1, len(ids)):
                b = jnp.where(i == j, ids[j], b)
            body(b)
            return carry

        if len(ids) == 1:
            body(ids[0])
        else:
            lax.fori_loop(0, len(ids), one, 0)

    class Role:
        def __init__(self, end, layer):
            self.end, self.layer = end, layer
            self.pending = []
            self.started = False
            upper_end = end and layer == 1
            self.makers = [self.mixed_copy, self.far_copy, self.left_copy, self.right_copy]
            if layer == 1:
                self.makers.append(self.section_copy)
            if not upper_end:
                self.makers.append(self.part_copy)
            if layer == 1 and not end:
                self.makers += [self.lent_copy, self.back_copy]


        def send(self, src, dst, a, b, peer, cond=None):
            copy = pltpu.make_async_remote_copy(
                src_ref=src, dst_ref=dst, send_sem=a, recv_sem=b, device_id=peer, device_id_type=mesh_id
            )
            self.pending.append((cond, copy))
            if cond is None:
                copy.start()
            else:
                pl.when(cond)(copy.start)

        def recv(self, dst, a, b):
            pltpu.make_async_remote_copy(
                src_ref=dst, dst_ref=dst, send_sem=a, recv_sem=b, device_id=side_peer,
                device_id_type=mesh_id,
            ).wait_recv()

        def remote(self, src, dst, a, b, peer):
            return pltpu.make_async_remote_copy(
                src_ref=src, dst_ref=dst, send_sem=a, recv_sem=b, device_id=peer, device_id_type=mesh_id
            )

        def finish(self):
            for _, copy in self.pending:
                copy.wait_send()

            def one(b, carry):
                for make in self.makers:
                    copy, cond = make(b)
                    if cond is None:
                        copy.wait_send()
                    else:
                        pl.when(cond)(copy.wait_send)
                return carry

            lax.fori_loop(0, 8, one, 0)

        def start(self, make, b):
            copy, cond = make(b)
            if cond is None:
                copy.start()
            else:
                pl.when(cond)(copy.start)

        def w(self, u, name, rows=whole):
            return wbuf.at[u, blk[name], rows]

        def zsend(self, kind, u, name, peer, rows=whole):
            ref = self.w(u, name, rows)
            self.send(ref, ref, zs.at[kind, u], zr.at[kind, u], peer)

        def zrecv(self, kind, u, name, rows=whole):
            self.recv(self.w(u, name, rows), zs.at[kind, u], zr.at[kind, u])

        def lent_unit(self, u):
            return self.layer == 1 and u >= 2

        def x_rows(self, u, name):
            if name != "f":
                return whole
            if self.end:
                return lower if u < 2 else whole
            return whole if self.lent_unit(u) else lower

        def xsend(self, u, name):
            ref = self.w(u, name, self.x_rows(u, name))
            i = "emnf".index(name)
            self.send(ref, ref, xs.at[i, u], xr.at[i, u], side_peer)

        def xrecv(self, u, name):
            i = "emnf".index(name)
            self.recv(self.w(u, "p" + name, self.x_rows(u, name)), xs.at[i, u], xr.at[i, u])

        def A(self, u):
            if self.end:
                self.zsend(0, u, "e", mid_peer)
                if not self.lent_unit(u):
                    self.xsend(u, "e")
            else:
                if not self.lent_unit(u):
                    self.zsend(2, u, "m", end_peer)
                self.zsend(6, u, "m", far_mid)
                self.xsend(u, "m")

        def Be(self, u):
            self.zrecv(0, u, "e")
            self.zsend(7, u, "e", far_mid)
            if self.lent_unit(u):
                self.xsend(u, "e")

        def Bp(self, u):
            if self.end:
                self.xrecv(u, "e")
                self.zsend(1, u, "pe", mid_peer)
            elif not self.lent_unit(u):
                self.zrecv(1, u, "pe")
                self.zsend(8, u, "pe", far_mid, upper)

        def Cm(self, u):
            self.zrecv(2, u, "m")
            self.xsend(u, "m")

        def C(self, u):
            if self.end:
                self.zrecv(3, u, "n")
                self.xsend(u, "n")
            else:
                self.zrecv(6, u, "n")
                if not self.lent_unit(u):
                    self.zsend(3, u, "n", end_peer)
                self.xsend(u, "n")

        def Df(self, u):
            if self.end:
                self.zrecv(4, u, "f")
            else:
                self.zrecv(7, u, "f")
                if not self.lent_unit(u):
                    self.zsend(4, u, "f", end_peer)
            self.xsend(u, "f")

        def Dp(self, u):
            if self.end:
                if u < 2:
                    self.zrecv(5, u, "pf", upper)
            elif not self.lent_unit(u):
                self.zrecv(8, u, "pf", upper)
                if u < 2:
                    self.zsend(5, u, "pf", end_peer, upper)


        def mixed_copy(self, b):
            return (self.remote(mixed.at[b], other.at[b], ms.at[b], mr.at[b], cross),
                    None if self.layer == 1 else b // 4 != mp)

        def section_copy(self, b):
            return self.remote(g.at[b], g.at[b], gs.at[b], gr.at[b], core), None

        def part_copy(self, b):
            return (self.remote(parts.at[b], near.at[b % 4], ps.at[b], pr.at[b], core),
                    b // 4 != self.layer)

        def lent_copy(self, b):
            i = (b // 4) * 2 + b % 2
            return (self.remote(lent.at[b], lent_in.at[i], us.at[i], ur.at[i], cross),
                    (b // 2) % 2 != mp)

        def back_copy(self, b):
            i, j = (b // 4) * 2 + b % 2, b % 2
            return (self.remote(lent.at[b], back.at[j], rs.at[i], rr.at[j],
                                (b // 4, plane["e"] * 2 + x, mp)), (b // 2) % 2 == mp)

        def onward(self, b):
            return (b // 4 == self.layer) & ((b // 2) % 2 != mp)

        def mine(self, b):
            return (b // 4 == self.layer) & ((b // 2) % 2 == mp)

        def far_copy(self, b):
            j = b % 2
            if self.end:
                src = parts.at[b] if self.layer == 0 else near.at[b % 4]
            else:
                src = fwd.at[j]
            return self.remote(src, far.at[j], ys.at[j], yr.at[j], cross), self.onward(b)

        def left_copy(self, b):
            j = b % 2
            return (self.remote(snd.at[j, pl.ds(0, CAP)], inc.at[j, pl.ds(CAP, CAP)], hs.at[j, 0],
                                hr.at[j, 0], (seg, (me + devices - 1) % devices, mp)), self.mine(b))

        def right_copy(self, b):
            j = b % 2
            return (self.remote(snd.at[j, pl.ds(CAP, CAP)], inc.at[j, pl.ds(0, CAP)], hs.at[j, 1],
                                hr.at[j, 1], (seg, (me + 1) % devices, mp)), self.mine(b))


        def out_blocks(self, names):
            if not self.started:
                acc[...] = jnp.zeros_like(acc)
            self.started = True

            def block(b):
                if self.layer == 1:
                    g_load(b).wait()
                else:
                    self.recv(g.at[b], gs.at[b], gr.at[b])

                def body(rows):
                    acc[rows, :] += dot(g[b, rows, :], wbuf[0, b], 1, 1)

                loop(2 * q_rows, body)

            each(names, block)

        def attend(self):
            rows = lax.broadcasted_iota(jnp.int32, (k_rows, q_rows), 1)
            cols = lax.broadcasted_iota(jnp.int32, (k_rows, q_rows), 0)

            def one_sequence(s, carry):
                qr = pl.ds(pl.multiple_of(s * q_rows, q_rows), q_rows)
                kr_ = pl.ds(pl.multiple_of(s * k_rows, k_rows), k_rows)
                allowed = None
                for e in range(2):
                    q_len, k_off, k_len = sc[s, e], sc[s, 2 + e] * TILE, sc[s, 4 + e]
                    hit = (rows >= e * TILE) & (rows < e * TILE + q_len)
                    hit = hit & (cols >= k_off) & (cols < k_off + k_len)
                    allowed = hit if allowed is None else allowed | hit

                def one_head(h, carry):
                    hd = pl.ds(pl.multiple_of(h * DH, DH), DH)
                    og = acc[qr, hd].astype(BF16)
                    q, k, v = q_ref[qr, hd], k_ref[kr_, hd], v_ref[kr_, hd]
                    masked = jnp.where(allowed, dot(k, q, 1, 1) * scale, masked_floor)
                    change = dot(v, og, 1, 1)
                    peak = jnp.maximum(jnp.max(masked, axis=0, keepdims=True), masked_floor / 2)
                    terms = jnp.exp(masked - peak)
                    prob = terms * (1.0 / jnp.maximum(jnp.sum(terms, axis=0, keepdims=True), 1.0))
                    prob_bf = prob.astype(BF16)
                    out_dot = jnp.sum(prob_bf.astype(F32) * change, axis=0, keepdims=True)
                    sg = (prob * (change - out_dot)).astype(BF16)
                    vg[kr_, hd] = dot(prob_bf, og, 1, 0).astype(BF16)
                    kg[kr_, hd] = (dot(sg, q, 1, 0) * scale).astype(BF16)
                    qg[qr, hd] = (dot(sg, k, 0, 0) * scale).astype(BF16)
                    return carry

                return lax.fori_loop(0, heads, one_head, carry)

            lax.fori_loop(0, 2, one_sequence, 0)

        def query_blocks(self, names):
            def block(b):
                def body(rows):
                    mixed[b, rows, :] = dot(qg[rows, :], wbuf[1, b], 1, 0).astype(BF16)

                loop(2 * q_rows, body)
                self.start(self.mixed_copy, b)

            each(names, block)

        def section_blocks(self, names):
            def total(b, rows):
                change = mixed[b, rows, :].astype(F32) + other[b, rows, :].astype(F32)
                return (g[b, rows, :].astype(F32) + change).astype(BF16)

            def block(b):
                cols = pl.ds(pl.multiple_of((b % 4) * BLOCK, BLOCK), BLOCK)
                if self.layer == 1:
                    self.recv(other.at[b], ms.at[b], mr.at[b])

                    def body(rows):
                        g[b, rows, :] = total(b, rows)

                    loop(2 * q_rows, body)
                    self.start(self.section_copy, b)

                @pl.when(b // 4 == mp)
                def _():
                    if self.layer == 0:
                        self.recv(other.at[b], ms.at[b], mr.at[b])

                    def body(rows):
                        sections_ref[0, rows, cols] = (
                            g[b, rows, :] if self.layer == 1 else total(b, rows)
                        )

                    loop(2 * q_rows, body)

            each(names, block)

        def project(self, kref, vref, dst, b):
            def body(rows):
                part = dot(kref[rows, :], wbuf[2, b], 1, 0) + dot(vref[rows, :], wbuf[3, b], 1, 0)
                dst[b, rows, :] = part.astype(BF16)

            loop(2 * k_rows, body)

        def encode(self, names):
            def block(b):
                self.project(kg, vg, parts, b)
                self.start(self.part_copy, b)

            each(names, block)

        def encode_lent(self, names):
            def block(b):
                self.project(kg_in, vg_in, lent, b)
                self.start(self.lent_copy, b)

            each(names, block)

        def give_back(self, names):
            def block(b):
                i = (b // 4) * 2 + b % 2

                @pl.when((b // 2) % 2 == mp)
                def _():
                    self.recv(lent_in.at[i], us.at[i], ur.at[i])

                    def body(rows):
                        both = lent[b, rows, :].astype(F32) + lent_in[i, rows, :].astype(F32)
                        lent[b, rows, :] = both.astype(BF16)

                    loop(2 * k_rows, body)

                self.start(self.back_copy, b)

            each(names, block)

        def reduce_cores(self, names):
            def block(b):
                if not (self.end and self.layer == 0):

                    @pl.when(b // 4 == self.layer)
                    def _():
                        self.recv(near.at[b % 4], ps.at[b], pr.at[b])

                if not self.end:

                    @pl.when(self.onward(b))
                    def _():
                        def body(rows):
                            both = parts[b, rows, :].astype(F32) + near[b % 4, rows, :].astype(F32)
                            fwd[b % 2, rows, :] = both.astype(BF16)

                        loop(2 * k_rows, body)

                self.start(self.far_copy, b)

            each(names, block)

        def reduce_heads(self, names):
            def block(b):
                j = b % 2

                @pl.when(self.mine(b))
                def _():
                    self.recv(far.at[j], ys.at[j], yr.at[j])
                    if self.end:
                        self.recv(back.at[j], rs.at[j], rr.at[j])

                    def body(t, carry):
                        rows = pl.ds(pl.multiple_of(t * TILE, TILE), TILE)
                        total = far[j, rows, :].astype(F32)
                        if self.end:
                            total += back[j, rows, :].astype(F32)
                        if not (self.end and self.layer == 1):
                            total += parts[b, rows, :].astype(F32)
                        if not (self.end and self.layer == 0):
                            total += near[b % 4, rows, :].astype(F32)
                        loc[j, t] = total.astype(BF16)
                        return carry

                    lax.fori_loop(0, 2 * k_rows // TILE, body, 0)
                    for c in range(CAP):
                        snd[j, c] = loc[j, pick_left[c]]
                        snd[j, CAP + c] = loc[j, pick_right[c]]

                self.start(self.left_copy, b)
                self.start(self.right_copy, b)

            each(names, block)

        def place(self):
            for j in range(2):
                self.recv(inc.at[j, pl.ds(CAP, CAP)], hs.at[j, 0], hr.at[j, 0])
                self.recv(inc.at[j, pl.ds(0, CAP)], hs.at[j, 1], hr.at[j, 1])
            for j in range(2):
                for t in range(tiles):
                    i = take[t]
                    kept = loc[j, jnp.minimum(i, tiles - 1)]
                    came = inc[j, jnp.clip(i - tiles, 0, 2 * CAP - 1)]
                    out_ref[t * TILE : (t + 1) * TILE, j * BLOCK : (j + 1) * BLOCK] = jnp.where(
                        i < tiles, kept, came
                    )

    tiles = 2 * k_rows // TILE
    per = tiles // 2

    def globals_of(source):
        return [own[source * 2 + t // per, t % per] for t in range(tiles)]

    def picks(goes, to):
        seen, chosen = jnp.int32(0), [jnp.int32(0)] * CAP
        for t in range(tiles):
            hit = (goes[t] >= to * tiles) & (goes[t] < (to + 1) * tiles)
            chosen = [jnp.where(hit & (seen == c), t, chosen[c]) for c in range(CAP)]
            seen = seen + hit.astype(jnp.int32)
        return chosen

    left_of, right_of = (me + devices - 1) % devices, (me + 1) % devices
    mine_goes = globals_of(me)
    pick_left, pick_right = picks(mine_goes, left_of), picks(mine_goes, right_of)
    take = [jnp.int32(0)] * tiles
    for source, base in ((me, 0), (left_of, tiles), (right_of, tiles + CAP)):
        goes = mine_goes if base == 0 else globals_of(source)
        seen = jnp.int32(0)
        for t in range(tiles):
            slot = goes[t] - me * tiles
            hit = (slot >= 0) & (slot < tiles)
            value = t if base == 0 else base + seen
            take = [jnp.where(slot == s, value, take[s]) for s in range(tiles)]
            seen = seen + hit.astype(jnp.int32)

    def mid_upper():
        r = Role(False, 1)
        r.A(0)
        r.Be(0)
        r.C(0)
        pl.semaphore_signal(gate, inc=1, device_id=core, device_id_type=mesh_id)
        r.xrecv(0,"m")
        r.out_blocks(["m", "e", "n", "pm"])
        r.Bp(0)
        r.A(1)
        r.Df(0)
        r.xrecv(0,"n")
        r.out_blocks(["pe", "pn", "f"])
        r.Be(1)
        r.Dp(0)
        r.C(1)
        r.Bp(1)
        r.xrecv(0,"f")
        r.out_blocks(["pf"])
        for c in in_loads:
            c.wait()
        r.attend()
        r.Df(1)
        r.Dp(1)
        r.A(2)
        r.A(3)
        r.Be(2)
        r.Be(3)
        r.xrecv(1,"m")
        r.query_blocks(["m", "e", "n", "pm"])
        r.xrecv(1,"n")
        r.query_blocks(["pe", "pn", "f"])
        r.xrecv(1,"f")
        r.query_blocks(["pf"])
        r.C(2)
        r.C(3)
        r.section_blocks(["m", "e", "n", "pm"])
        r.Df(2)
        r.section_blocks(["pe", "pn", "f"])
        r.section_blocks(["pf"])
        r.Df(3)
        r.xrecv(2,"m")
        r.xrecv(3,"m")
        r.xrecv(2,"e")
        r.xrecv(3,"e")
        r.xrecv(2,"n")
        r.xrecv(3,"n")
        r.encode(["m", "e", "n", "pm", "pe", "pn"])
        r.recv(kg_in, ks.at[0], kr.at[0])
        r.recv(vg_in, ks.at[1], kr.at[1])
        r.encode_lent(["m", "e", "n", "pm", "pe", "pn"])
        r.xrecv(2,"f")
        r.xrecv(3,"f")
        r.encode(["f", "pf"])
        r.encode_lent(["f", "pf"])
        r.give_back(["m", "e", "n", "pm", "pe", "pn"])
        r.reduce_cores(["m", "e", "n", "pm"])
        r.reduce_cores(["f"])
        r.give_back(["f", "pf"])
        r.reduce_cores(["pe", "pn"])
        r.reduce_cores(["pf"])
        r.reduce_heads(["m", "e", "n", "pm"])
        r.reduce_heads(["f"])
        r.reduce_heads(["pe", "pn"])
        r.reduce_heads(["pf"])
        r.place()
        r.finish()

    def mid_lower():
        r = Role(False, 0)
        pl.semaphore_wait(gate, 1)
        r.A(0)
        r.C(0)
        r.Be(0)
        r.Df(0)
        r.A(1)
        r.Be(1)
        r.Bp(0)
        r.xrecv(0,"m")
        r.xrecv(0,"n")
        r.out_blocks(["m", "e", "n", "pm", "pe", "pn"])
        r.Bp(1)
        r.C(1)
        r.Df(1)
        r.A(3)
        r.Dp(0)
        r.xrecv(0,"f")
        r.out_blocks(["f", "pf"])
        for c in in_loads:
            c.wait()
        r.attend()
        r.Dp(1)
        r.A(2)
        r.C(3)
        r.xrecv(1,"m")
        r.xrecv(1,"n")
        r.query_blocks(["m", "e", "n", "pm", "pe", "pn"])
        r.xrecv(1,"f")
        r.query_blocks(["f", "pf"])
        r.C(2)
        r.Be(2)
        r.Be(3)
        r.Df(2)
        r.section_blocks(["m", "e", "n", "pm", "pe", "pn", "f", "pf"])
        r.Bp(2)
        r.Df(3)
        r.xrecv(2,"m")
        r.xrecv(3,"m")
        r.encode(["m", "e", "n", "pm"])
        r.Dp(2)
        r.Bp(3)
        r.reduce_cores(["m", "e", "n", "pm"])
        r.encode(["f"])
        r.reduce_cores(["f"])
        r.xrecv(2,"n")
        r.xrecv(3,"n")
        r.encode(["pe", "pn"])
        r.Dp(3)
        r.reduce_cores(["pe", "pn"])
        r.xrecv(2,"f")
        r.xrecv(3,"f")
        r.encode(["pf"])
        r.reduce_cores(["pf"])
        r.reduce_heads(["m", "e", "n", "pm"])
        r.reduce_heads(["f"])
        r.reduce_heads(["pe", "pn"])
        r.reduce_heads(["pf"])
        r.place()
        r.finish()

    def end_upper():
        r = Role(True, 1)
        r.A(0)
        r.Bp(0)
        r.Cm(0)
        r.A(1)
        r.xrecv(0,"m")
        r.out_blocks(["e", "pe", "m", "pm"])
        r.C(0)
        r.Bp(1)
        r.Cm(1)
        r.A(2)
        r.A(3)
        r.Df(0)
        pl.semaphore_signal(gate, inc=1, device_id=core, device_id_type=mesh_id)
        r.xrecv(0,"n")
        r.out_blocks(["n", "pn", "f"])
        r.Dp(0)
        r.xrecv(0,"f")
        r.out_blocks(["pf"])
        for c in in_loads:
            c.wait()
        r.attend()
        r.C(1)
        r.send(kg, kg_in, ks.at[0], kr.at[0], mid_peer)
        r.send(vg, vg_in, ks.at[1], kr.at[1], mid_peer)
        r.xrecv(1,"m")
        r.query_blocks(["e", "pe", "m", "pm"])
        r.Df(1)
        r.Dp(1)
        r.xrecv(1,"n")
        r.query_blocks(["n", "pn", "f"])
        r.section_blocks(["e", "pe", "m", "pm"])
        r.xrecv(1,"f")
        r.query_blocks(["pf"])
        r.section_blocks(["n", "pn", "f"])
        r.section_blocks(["pf"])
        r.reduce_cores(["e", "pe", "m", "pm"])
        r.reduce_cores(["n", "pn"])
        r.reduce_cores(["f"])
        r.reduce_heads(["e", "pe", "m", "pm"])
        r.reduce_heads(["n", "pn"])
        r.reduce_cores(["pf"])
        r.reduce_heads(["f"])
        r.reduce_heads(["pf"])
        r.place()
        r.finish()

    def end_lower():
        r = Role(True, 0)
        pl.semaphore_wait(gate, 1)
        r.A(0)
        r.A(1)
        r.Cm(0)
        r.C(0)
        r.Bp(0)
        r.Bp(1)
        r.Df(0)
        r.Cm(1)
        r.xrecv(0,"m")
        r.xrecv(0,"n")
        r.out_blocks(["e", "pe", "m", "pm", "n", "pn"])
        r.C(1)
        r.Df(1)
        r.A(2)
        r.A(3)
        r.Cm(3)
        r.Dp(0)
        r.xrecv(0,"f")
        r.out_blocks(["f", "pf"])
        for c in in_loads:
            c.wait()
        r.attend()
        r.Cm(2)
        r.Bp(2)
        r.Dp(1)
        r.xrecv(1,"m")
        r.xrecv(1,"n")
        r.query_blocks(["e", "pe", "m", "pm", "n", "pn"])
        r.Bp(3)
        r.C(3)
        r.xrecv(1,"f")
        r.query_blocks(["f", "pf"])
        r.C(2)
        r.xrecv(2,"m")
        r.xrecv(3,"m")
        r.encode(["e", "pe", "m", "pm"])
        r.Df(2)
        r.reduce_cores(["e", "pe", "m", "pm"])
        r.section_blocks(["e", "pe", "m", "pm", "n", "pn", "f", "pf"])
        r.Df(3)
        r.xrecv(2,"n")
        r.xrecv(3,"n")
        r.encode(["n", "pn"])
        r.reduce_cores(["n", "pn"])
        r.encode(["f"])
        r.reduce_cores(["f"])
        r.xrecv(2,"f")
        r.xrecv(3,"f")
        r.encode(["pf"])
        r.reduce_cores(["pf"])
        r.reduce_heads(["e", "pe", "m", "pm"])
        r.reduce_heads(["n", "pn"])
        r.reduce_heads(["f"])
        r.reduce_heads(["pf"])
        r.place()
        r.finish()

    for wanted_end, layer, program in (
        (False, 1, mid_upper), (False, 0, mid_lower), (True, 1, end_upper), (True, 0, end_lower)
    ):
        place_here = at_end if wanted_end else jnp.logical_not(at_end)
        pl.when(place_here & (seg == layer))(program)


def run_chain(scalars, owners, top, q, k, v, wo, wq, wk, wv, devices):
    micro = scalars.shape[0]
    q_rows, k_rows = top.shape[0] // micro, k.shape[1] // micro
    width, depth = top.shape[1], q.shape[2]
    half, blocks = width // 2, width // BLOCK
    keys = micro * k_rows
    tiles = keys // TILE
    smem, vmem, any_ = (pl.BlockSpec(memory_space=m) for m in (pltpu.SMEM, pltpu.VMEM, pl.ANY))
    dma = pltpu.SemaphoreType.DMA

    def buf(*shape, dtype=BF16):
        return pltpu.VMEM(shape, dtype)

    return pl.pallas_call(
        functools.partial(chain_kernel, (q_rows, k_rows, depth // DH, devices)),
        in_specs=[smem, smem] + [any_] * 8,
        out_specs=[vmem, vmem],
        out_shape=[
            jax.ShapeDtypeStruct((1, micro * q_rows, half), BF16),
            jax.ShapeDtypeStruct((keys, width // 4), BF16),
        ],
        scratch_shapes=[
            buf(4, blocks, depth, BLOCK),
            buf(blocks, micro * q_rows, BLOCK),
            buf(micro * q_rows, depth),
            buf(keys, depth),
            buf(keys, depth),
            buf(micro * q_rows, depth, dtype=F32),
            buf(micro * q_rows, depth),
            buf(keys, depth),
            buf(keys, depth),
            buf(blocks, micro * q_rows, BLOCK),
            buf(blocks, micro * q_rows, BLOCK),
            buf(blocks, keys, BLOCK),
            buf(4, keys, BLOCK),
            buf(2, keys, BLOCK),
            buf(2, keys, BLOCK),
            buf(keys, depth),
            buf(keys, depth),
            buf(blocks, keys, BLOCK),
            buf(4, keys, BLOCK),
            buf(2, keys, BLOCK),
            buf(2, tiles, TILE, BLOCK),
            buf(2, 2 * CAP, TILE, BLOCK),
            buf(2, 2 * CAP, TILE, BLOCK),
        ]
        + [dma((4,)), dma((8,)), dma((3,))]
        + [dma((9, 4))] * 2
        + [dma((4, 4))] * 2
        + [dma((8,))] * 4
        + [dma((2,))] * 2
        + [dma((8,))] * 2
        + [dma((2,))] * 2
        + [dma((4,))] * 2
        + [dma((4,)), dma((2,))]
        + [dma((2, 2))] * 2
        + [pltpu.SemaphoreType.REGULAR],
        compiler_params=pltpu.CompilerParams(
            collective_id=0, has_side_effects=True, vmem_limit_bytes=60 << 20
        ),
    )(scalars, owners, top, q, k, v, wo, wq, wk, wv)


def ranked(marked):
    ids = jnp.arange(marked.shape[0], dtype=jnp.int32)
    upto = ids[None, :] <= ids[:, None]
    return jnp.sum((upto & marked[None, :]).astype(jnp.int32), axis=1) - 1


def on_device(
    grad_top,
    saved_query,
    saved_key,
    saved_value,
    w_query,
    w_key,
    w_value,
    w_out,
    query_length,
    key_offset,
    key_length,
    tile_owner,
):
    seg = lax.axis_index("segment")
    mp = lax.axis_index("mp")
    devices = lax.axis_size("dp")
    me = lax.axis_index("dp")
    micro = query_length.shape[0]
    q_rows = grad_top.shape[0] // micro
    k_rows = saved_key.shape[1] // micro
    half = grad_top.shape[1] // 2
    mp_swap = [(0, 1), (1, 0)]
    if w_out.shape[2] == BLOCK and devices == 8 and micro == 2:
        table = jnp.concatenate([query_length, key_offset, key_length], axis=1)
        return run_chain(
            table, tile_owner, grad_top, saved_query, saved_key, saved_value, w_out, w_query, w_key,
            w_value, devices,
        )

    wo, sources = gathered(w_out[0])
    wq, _ = gathered(w_query[0])
    wk, _ = gathered(w_key[0])
    wv, _ = gathered(w_value[0])
    order = jnp.stack(sources).astype(jnp.int32)

    top = grad_top.reshape(grad_top.shape[0], 2, half).transpose(1, 0, 2)
    scalars = [
        jnp.concatenate([order, query_length[s], key_offset[s], key_length[s]])
        for s in range(micro)
    ]

    def tick(s, grad, at):
        return run_tick(
            scalars[s], grad, at, s, saved_query, saved_key, saved_value, wo, wq, q_rows, k_rows
        )

    upper = [tick(s, top, s) for s in range(micro)]
    upper_half, incoming = [], []
    for s in range(micro):
        mixed = upper[s][0]
        other = lax.ppermute(mixed, "mp", mp_swap)
        rows = top[:, s * q_rows : (s + 1) * q_rows]
        section = (rows.astype(F32) + (mixed.astype(F32) + other.astype(F32))).astype(BF16)
        incoming.append(lax.ppermute(section, "segment", [(1, 0)]))
        upper_half.append(lax.dynamic_index_in_dim(section, mp, 0, keepdims=False))
    lower = [tick(s, incoming[s], 0) for s in range(micro)]
    halves = []
    for s in range(micro):
        mixed = lower[s][0]
        other = lax.ppermute(
            lax.dynamic_index_in_dim(mixed, 1 - mp, 0, keepdims=False), "mp", mp_swap
        )
        own = lax.dynamic_index_in_dim(mixed, mp, 0, keepdims=False)
        base = lax.dynamic_index_in_dim(incoming[s], mp, 0, keepdims=False)
        low = (base.astype(F32) + (own.astype(F32) + other.astype(F32))).astype(BF16)
        halves.append(jnp.where(seg == 1, upper_half[s], low))
    sections = jnp.concatenate(halves, axis=0)[None]

    kg = jnp.concatenate([jnp.where(seg == 1, upper[s][1], lower[s][1]) for s in range(micro)], 0)
    vg = jnp.concatenate([jnp.where(seg == 1, upper[s][2], lower[s][2]) for s in range(micro)], 0)
    parts = run_encoder(order, kg, vg, wk, wv)
    away = lax.dynamic_slice_in_dim(parts, (1 - seg) * 2, 2, 0)
    mine = lax.dynamic_slice_in_dim(parts, seg * 2, 2, 0)
    arrived = lax.ppermute(away, "segment", mp_swap)
    summed = (mine.astype(F32) + arrived.astype(F32)).astype(BF16)
    crossing = lax.ppermute(
        lax.dynamic_index_in_dim(summed, 1 - mp, 0, keepdims=False), "mp", mp_swap
    )
    kept = lax.dynamic_index_in_dim(summed, mp, 0, keepdims=False)
    kept = (kept.astype(F32) + crossing.astype(F32)).astype(BF16)

    tiles = kept.shape[0] // TILE
    features = kept.shape[1]
    owners = tile_owner.reshape(devices, tiles)
    slot_ids = jnp.arange(CAP, dtype=jnp.int32)[:, None]
    tile_ids = jnp.arange(tiles, dtype=jnp.int32)

    def plan(source):
        source = source % devices
        row = lax.dynamic_index_in_dim(owners, source, 0, keepdims=False)
        return (row // tiles - source + devices) % devices, row % tiles

    def ranks_of(marked):
        return (ranked(marked)[None, :] == slot_ids) & marked[None, :]

    step, slot = plan(me)
    left_step, left_slot = plan(me - 1 + devices)
    right_step, right_slot = plan(me + 1)
    send_left = jnp.sum(jnp.where(ranks_of(step == devices - 1), tile_ids[None, :], 0), axis=1)
    send_right = jnp.sum(jnp.where(ranks_of(step == 1), tile_ids[None, :], 0), axis=1)
    left_hit = ranks_of(left_step == 1)
    right_hit = ranks_of(right_step == devices - 1)
    target = jnp.concatenate(
        [
            jnp.sum(jnp.where(left_hit, left_slot[None, :], 0), axis=1),
            slot,
            jnp.sum(jnp.where(right_hit, right_slot[None, :], 0), axis=1),
        ]
    )
    usable = jnp.concatenate([jnp.any(left_hit, axis=1), step == 0, jnp.any(right_hit, axis=1)])
    chosen = (tile_ids[:, None] == target[None, :]) & usable[None, :]
    candidate_ids = jnp.arange(target.shape[0], dtype=jnp.int32)
    take = jnp.sum(jnp.where(chosen, candidate_ids[None, :], 0), axis=1)

    tiled = (tiles, TILE, features)
    shape = jax.ShapeDtypeStruct(tiled, BF16)
    handed = jax.ShapeDtypeStruct((CAP, TILE, features), BF16)
    local = kept.reshape(tiled)
    to_left, to_right = small_call(
        pick_kernel, jnp.concatenate([send_left, send_right]), [local], [handed, handed]
    )
    forward = [(i, (i + 1) % devices) for i in range(devices)]
    backward = [(b, a) for a, b in forward]
    from_left = lax.ppermute(to_right, "dp", forward)
    from_right = lax.ppermute(to_left, "dp", backward)
    owned = small_call(place_kernel, take, [from_left, local, from_right], shape)
    return sections, owned.reshape(tiles * TILE, features)


def solution(mesh):
    in_specs = (
        P("dp", None),
        P("segment", "dp", "mp"),
        P("segment", "dp", "mp"),
        P("segment", "dp", "mp"),
        P("segment", "mp", "dp"),
        P("segment", "mp", "dp"),
        P("segment", "mp", "dp"),
        P("segment", "mp", "dp"),
        P("dp", None),
        P("dp", None),
        P("dp", None),
        P(),
    )
    out_specs = (P("segment", "dp", "mp"), P("dp", ("segment", "mp")))
    return jax.shard_map(
        on_device, mesh=mesh, in_specs=in_specs, out_specs=out_specs, check_vma=False
    )
```

```python
import functools

import jax
import jax.numpy as jnp
from jax import lax
from jax.experimental import pallas as pl
from jax.experimental.pallas import tpu as pltpu
from jax.sharding import PartitionSpec as P

DH = 256
TILE = 128
CAP = 2
BLOCK = 256
masked_floor = -1e30
BF16, F32 = jnp.bfloat16, jnp.float32


def dot(a, b, ca, cb):
    return lax.dot_general(a, b, (((ca,), (cb,)), ((), ())), preferred_element_type=F32)


def tick_kernel(count, half, sc, g_ref, q_ref, k_ref, v_ref, *rest):
    wo, wq = rest[:count], rest[count : 2 * count]
    mixed_ref, kg_ref, vg_ref, acc = rest[2 * count :]
    head = pl.program_id(0)
    per = half // BLOCK
    scale = DH ** (-0.5)

    def place(b):
        src = sc[b]
        return src // per, pl.ds(pl.multiple_of((src % per) * BLOCK, BLOCK), BLOCK)

    og = None
    for b in range(count):
        at, cols = place(b)
        term = dot(g_ref[at, :, cols], wo[b][...], 1, 1)
        og = term if og is None else og + term
    og = og.astype(BF16)
    q, k, v = q_ref[0], k_ref[0], v_ref[0]
    scores = dot(q, k, 1, 1) * scale
    rows = lax.broadcasted_iota(jnp.int32, scores.shape, 0)
    cols_id = lax.broadcasted_iota(jnp.int32, scores.shape, 1)
    allowed = None
    for e in range(2):
        q_len, k_off, k_len = sc[count + e], sc[count + 2 + e] * TILE, sc[count + 4 + e]
        hit = (rows >= e * TILE) & (rows < e * TILE + q_len)
        hit = hit & (cols_id >= k_off) & (cols_id < k_off + k_len)
        allowed = hit if allowed is None else allowed | hit
    masked = jnp.where(allowed, scores, masked_floor)
    top = jnp.max(masked, axis=-1, keepdims=True)
    terms = jnp.where(allowed, jnp.exp(masked - top), 0.0)
    prob = terms / jnp.maximum(jnp.sum(terms, axis=-1, keepdims=True), 1.0)
    prob_bf = prob.astype(BF16)
    attended = dot(prob_bf, v, 1, 0)
    out_dot = jnp.sum(og.astype(F32) * attended, axis=-1, keepdims=True)
    sg = (prob * (dot(og, v, 1, 1) - out_dot)).astype(BF16)
    qg = (dot(sg, k, 1, 0) * scale).astype(BF16)
    kg_ref[...] = (dot(sg, q, 0, 0) * scale).astype(BF16)
    vg_ref[...] = dot(prob_bf, og, 0, 0).astype(BF16)

    @pl.when(head == 0)
    def _():
        acc[...] = jnp.zeros_like(acc)

    for b in range(count):
        at, cols = place(b)
        acc[at, :, cols] += dot(qg, wq[b][...], 1, 0)

    @pl.when(head == pl.num_programs(0) - 1)
    def _():
        mixed_ref[...] = acc[...].astype(BF16)


def run_tick(scalars, grad, at, seq, saved_q, saved_k, saved_v, wo, wq, q_rows, k_rows):
    half = grad.shape[2]
    heads = saved_q.shape[2] // DH
    count = len(wo)
    weight = pl.BlockSpec((DH, BLOCK), lambda h, sc: (h, 0))
    macs = heads * q_rows * DH * (4 * half + 6 * k_rows)
    return pl.pallas_call(
        functools.partial(tick_kernel, count, half),
        grid_spec=pltpu.PrefetchScalarGridSpec(
            num_scalar_prefetch=1,
            grid=(heads,),
            in_specs=[
                pl.BlockSpec((2, q_rows, half), lambda h, sc: (0, at, 0)),
                pl.BlockSpec((1, q_rows, DH), lambda h, sc: (0, seq, h)),
                pl.BlockSpec((1, k_rows, DH), lambda h, sc: (0, seq, h)),
                pl.BlockSpec((1, k_rows, DH), lambda h, sc: (0, seq, h)),
            ]
            + [weight] * (2 * count),
            out_specs=[
                pl.BlockSpec((2, q_rows, half), lambda h, sc: (0, 0, 0)),
                pl.BlockSpec((k_rows, DH), lambda h, sc: (0, h)),
                pl.BlockSpec((k_rows, DH), lambda h, sc: (0, h)),
            ],
            scratch_shapes=[pltpu.VMEM((2, q_rows, half), F32)],
        ),
        out_shape=[
            jax.ShapeDtypeStruct((2, q_rows, half), BF16),
            jax.ShapeDtypeStruct((k_rows, heads * DH), BF16),
            jax.ShapeDtypeStruct((k_rows, heads * DH), BF16),
        ],
        compiler_params=pltpu.CompilerParams(vmem_limit_bytes=40 << 20),
        cost_estimate=pl.CostEstimate(
            flops=2 * macs, bytes_accessed=16 << 20, transcendentals=heads * q_rows * k_rows
        ),
    )(scalars, grad, saved_q, saved_k, saved_v, *wo, *wq)


def encoder_kernel(count, quarter, sc, kg_ref, vg_ref, *rest):
    wk, wv, out_ref = rest[:count], rest[count : 2 * count], rest[2 * count]
    per = quarter // BLOCK
    kg, vg = kg_ref[...], vg_ref[...]
    for b in range(count):
        src = sc[b]
        cols = pl.ds(pl.multiple_of((src % per) * BLOCK, BLOCK), BLOCK)
        part = dot(kg, wk[b][...], 1, 0) + dot(vg, wv[b][...], 1, 0)
        out_ref[src // per, :, cols] = part.astype(BF16)


def run_encoder(scalars, kg, vg, wk, wv):
    count = len(wk)
    rows, depth = kg.shape
    quarter = count * BLOCK // 4
    step = 256
    whole = pl.BlockSpec((depth, BLOCK), lambda i, sc: (0, 0))
    return pl.pallas_call(
        functools.partial(encoder_kernel, count, quarter),
        grid_spec=pltpu.PrefetchScalarGridSpec(
            num_scalar_prefetch=1,
            grid=(rows // step,),
            in_specs=[pl.BlockSpec((step, depth), lambda i, sc: (i, 0))] * 2
            + [whole] * (2 * count),
            out_specs=pl.BlockSpec((4, step, quarter), lambda i, sc: (0, i, 0)),
        ),
        out_shape=jax.ShapeDtypeStruct((4, rows, quarter), BF16),
        compiler_params=pltpu.CompilerParams(vmem_limit_bytes=48 << 20),
        cost_estimate=pl.CostEstimate(
            flops=16 * rows * depth * quarter, bytes_accessed=14 << 20, transcendentals=0
        ),
    )(scalars, kg, vg, *wk, *wv)


def pick_kernel(sc, local_ref, left_ref, right_ref):
    for c in range(CAP):
        left_ref[c] = local_ref[sc[c]]
        right_ref[c] = local_ref[sc[CAP + c]]


def place_kernel(sc, left_ref, local_ref, right_ref, out_ref):
    tiles = local_ref.shape[0]
    for s in range(tiles):
        i = sc[s]

        @pl.when(i < CAP)
        def _():
            out_ref[s] = left_ref[jnp.minimum(i, CAP - 1)]

        @pl.when((i >= CAP) & (i < CAP + tiles))
        def _():
            out_ref[s] = local_ref[jnp.clip(i - CAP, 0, tiles - 1)]

        @pl.when(i >= CAP + tiles)
        def _():
            out_ref[s] = right_ref[jnp.clip(i - CAP - tiles, 0, CAP - 1)]


def small_call(body, scalars, arrays, outs):
    vmem = pl.BlockSpec(memory_space=pltpu.VMEM)
    single = not isinstance(outs, list)
    return pl.pallas_call(
        body,
        in_specs=[pl.BlockSpec(memory_space=pltpu.SMEM)] + [vmem] * len(arrays),
        out_specs=vmem if single else [vmem] * len(outs),
        out_shape=outs,
        compiler_params=pltpu.CompilerParams(vmem_limit_bytes=24 << 20),
    )(scalars, *arrays)


def gathered(shard):
    full = lax.all_gather(shard, "dp", axis=1, tiled=True)
    blocks = [full[:, i : i + BLOCK] for i in range(0, full.shape[1], BLOCK)]
    return blocks, list(jnp.arange(len(blocks), dtype=jnp.int32))


def chain_kernel(dims, ql_hbm, ko_hbm, kl_hbm, own_hbm, top_hbm, q_hbm, k_hbm, v_hbm, wo_hbm, wq_hbm, wk_hbm, wv_hbm,
                 sections_hbm, out_ref,
                 wbuf, g, q_ref, k_ref, v_ref, acc, qg, kg, vg, mixed, other, parts, near, fwd, far,
                 kg_in, vg_in, lent, lent_in, back, loc, inc, snd,
                 ldw, ldg, ldq, zs, zr, xs, xr, ms, mr, gs, gr, ks, kr, ps, pr, ys, yr,
                 us, ur, rs, rr, hs, hr, so, gate,
                 q_len_of, k_off_of, k_len_of, own, ldt):
    q_rows, k_rows, heads, devices = dims
    depth = heads * DH
    scale = DH ** (-0.5)
    seg, me, mp = lax.axis_index("segment"), lax.axis_index("dp"), lax.axis_index("mp")
    z, x = me // 2, me % 2
    side = z // 2
    mesh_id = pl.DeviceIdType.MESH
    plane = {"e": 3 * side, "m": 1 + side, "n": 2 - side, "f": 3 - 3 * side}
    blk = {c: plane[c] * 2 + x for c in plane}
    blk.update({"p" + c: plane[c] * 2 + 1 - x for c in plane})
    at_end = (z == 0) | (z == 3)
    side_peer, cross, core = (seg, z * 2 + 1 - x, mp), (seg, me, 1 - mp), (1 - seg, me, mp)
    diag = jnp.where(x == 0, (me + devices - 1) % devices, (me + 1) % devices)
    end_peer, mid_peer = (seg, plane["e"] * 2 + x, mp), (seg, plane["m"] * 2 + x, mp)
    far_mid = (seg, plane["n"] * 2 + x, mp)
    upper, lower = pl.ds(0, depth // 2), pl.ds(depth // 2, depth // 2)
    whole = pl.ds(0, depth)
    step = 256

    def load(src, dst, sem):
        return pltpu.make_async_copy(src, dst, sem)

    weights = (wo_hbm, wq_hbm, wk_hbm, wv_hbm)
    w_loads = [load(weights[u].at[0], wbuf.at[u, me], ldw.at[u]) for u in range(4)]
    in_loads = [load(a.at[0], b, ldq.at[i])
                for i, (a, b) in enumerate(((q_hbm, q_ref), (k_hbm, k_ref), (v_hbm, v_ref)))]

    def g_load(b):
        cols = pl.ds(pl.multiple_of(b * BLOCK, BLOCK), BLOCK)
        return load(top_hbm.at[:, cols], g.at[b], ldg.at[b])

    tables = ((ql_hbm, q_len_of), (ko_hbm, k_off_of), (kl_hbm, k_len_of), (own_hbm, own))
    table_loads = [load(a, b, ldt.at[i]) for i, (a, b) in enumerate(tables)]
    w_loads[0].start()

    barrier = pltpu.get_barrier_semaphore()

    def greet(peers):
        for peer in peers:
            pl.semaphore_signal(barrier, inc=1, device_id=peer, device_id_type=mesh_id)

    all_peers = [side_peer, cross, core, (seg, diag, mp)]
    greet(all_peers)

    @pl.when(at_end)
    def _():
        greet([mid_peer])

        @pl.when(seg == 0)
        def _():
            greet([(1, plane["m"] * 2 + x, mp)])

    @pl.when(jnp.logical_not(at_end))
    def _():
        greet([end_peer, far_mid])

        @pl.when(seg == 1)
        def _():
            greet([(0, plane["e"] * 2 + x, mp)])

    @pl.when(seg == 1)
    def _():
        for b in range(8):
            g_load(b).start()

    for c in w_loads[1:] + in_loads + table_loads:
        c.start()
    for c in w_loads:
        c.wait()

    pl.semaphore_wait(barrier, jnp.where(at_end, 6 - seg, 6 + seg))

    def loop(rows, body):
        def one(i, carry):
            body(pl.ds(pl.multiple_of(i * step, step), step))
            return carry

        lax.fori_loop(0, rows // step, one, 0)

    def each(names, body):
        ids = [blk[n] for n in names]

        def one(i, carry):
            b = ids[0]
            for j in range(1, len(ids)):
                b = jnp.where(i == j, ids[j], b)
            body(b)
            return carry

        if len(ids) == 1:
            body(ids[0])
        else:
            lax.fori_loop(0, len(ids), one, 0)

    class Role:
        def __init__(self, end, layer):
            self.end, self.layer = end, layer
            self.pending = []
            self.started = False
            upper_end = end and layer == 1
            self.makers = [self.mixed_copy, self.far_copy, self.left_copy, self.right_copy]
            if layer == 1:
                self.makers.append(self.section_copy)
            if not upper_end:
                self.makers.append(self.part_copy)
            if layer == 1 and not end:
                self.makers += [self.lent_copy, self.back_copy]


        def send(self, src, dst, a, b, peer, cond=None):
            copy = pltpu.make_async_remote_copy(
                src_ref=src, dst_ref=dst, send_sem=a, recv_sem=b, device_id=peer, device_id_type=mesh_id
            )
            self.pending.append((cond, copy))
            if cond is None:
                copy.start()
            else:
                pl.when(cond)(copy.start)

        def recv(self, dst, a, b):
            pltpu.make_async_remote_copy(
                src_ref=dst, dst_ref=dst, send_sem=a, recv_sem=b, device_id=side_peer,
                device_id_type=mesh_id,
            ).wait_recv()

        def remote(self, src, dst, a, b, peer):
            return pltpu.make_async_remote_copy(
                src_ref=src, dst_ref=dst, send_sem=a, recv_sem=b, device_id=peer, device_id_type=mesh_id
            )

        def finish(self):
            for _, copy in self.pending:
                copy.wait_send()

            def one(b, carry):
                for make in self.makers:
                    copy, cond = make(b)
                    if cond is None:
                        copy.wait_send()
                    else:
                        pl.when(cond)(copy.wait_send)
                return carry

            lax.fori_loop(0, 8, one, 0)
            for i in range(4):
                self.output_copy(4 * mp + i).wait()

        def start(self, make, b):
            copy, cond = make(b)
            if cond is None:
                copy.start()
            else:
                pl.when(cond)(copy.start)

        def w(self, u, name, rows=whole):
            return wbuf.at[u, blk[name], rows]

        def zsend(self, kind, u, name, peer, rows=whole):
            ref = self.w(u, name, rows)
            self.send(ref, ref, zs.at[kind, u], zr.at[kind, u], peer)

        def zrecv(self, kind, u, name, rows=whole):
            self.recv(self.w(u, name, rows), zs.at[kind, u], zr.at[kind, u])

        def lent_unit(self, u):
            return self.layer == 1 and u >= 2

        def twice(self, u):
            return u < (2 if self.layer == 1 else 1)

        def x_rows(self, u, name):
            if name != "f":
                return whole
            return lower if not self.end or self.twice(u) else whole

        def xsend(self, u, name):
            ref = self.w(u, name, self.x_rows(u, name))
            i = "emnf".index(name)
            self.send(ref, ref, xs.at[i, u], xr.at[i, u], side_peer)

        def xrecv(self, u, name):
            i = "emnf".index(name)
            self.recv(self.w(u, "p" + name, self.x_rows(u, name)), xs.at[i, u], xr.at[i, u])

        def A(self, u):
            if self.end:
                self.zsend(0, u, "e", mid_peer)
                if not self.lent_unit(u):
                    self.xsend(u, "e")
            else:
                if not self.lent_unit(u):
                    self.zsend(2, u, "m", end_peer)
                self.zsend(6, u, "m", far_mid)
                self.xsend(u, "m")

        def Be(self, u):
            self.zrecv(0, u, "e")
            self.zsend(7, u, "e", far_mid)
            if self.lent_unit(u):
                self.xsend(u, "e")

        def Bp(self, u):
            if self.end:
                self.xrecv(u, "e")
                self.zsend(1, u, "pe", mid_peer)
            else:
                if self.lent_unit(u):
                    self.xrecv(u, "e")
                else:
                    self.zrecv(1, u, "pe")
                self.zsend(8, u, "pe", far_mid, upper)

        def Cm(self, u):
            self.zrecv(2, u, "m")
            self.xsend(u, "m")

        def C(self, u):
            if self.end:
                self.zrecv(3, u, "n")
                self.xsend(u, "n")
            else:
                self.zrecv(6, u, "n")
                if not self.lent_unit(u):
                    self.zsend(3, u, "n", end_peer)
                self.xsend(u, "n")

        def Df(self, u):
            if self.end:
                self.zrecv(4, u, "f")
            else:
                self.zrecv(7, u, "f")
                if not self.lent_unit(u):
                    self.zsend(4, u, "f", end_peer)
            self.xsend(u, "f")

        def Dp(self, u):
            if self.end:
                self.zrecv(5, u, "pf", upper)
            else:
                self.zrecv(8, u, "pf", upper)
                if self.twice(u):
                    self.zsend(5, u, "pf", end_peer, upper)


        def mixed_copy(self, b):
            return (self.remote(mixed.at[b], other.at[b], ms.at[b], mr.at[b], cross),
                    None if self.layer == 1 else b // 4 != mp)

        def section_copy(self, b):
            return self.remote(g.at[b], g.at[b], gs.at[b], gr.at[b], core), None

        def part_copy(self, b):
            return (self.remote(parts.at[b], near.at[b % 4], ps.at[b], pr.at[b], core),
                    b // 4 != self.layer)

        def lent_copy(self, b):
            i = (b // 4) * 2 + b % 2
            return (self.remote(lent.at[b], lent_in.at[i], us.at[i], ur.at[i], cross),
                    (b // 2) % 2 != mp)

        def back_copy(self, b):
            i, j = (b // 4) * 2 + b % 2, b % 2
            return (self.remote(lent.at[b], back.at[j], rs.at[i], rr.at[j],
                                (b // 4, plane["e"] * 2 + x, mp)), (b // 2) % 2 == mp)

        def onward(self, b):
            return (b // 4 == self.layer) & ((b // 2) % 2 != mp)

        def mine(self, b):
            return (b // 4 == self.layer) & ((b // 2) % 2 == mp)

        def far_copy(self, b):
            j = b % 2
            if self.end:
                src = parts.at[b] if self.layer == 0 else near.at[b % 4]
            else:
                src = fwd.at[j]
            return self.remote(src, far.at[j], ys.at[j], yr.at[j], cross), self.onward(b)

        def left_copy(self, b):
            j = b % 2
            return (self.remote(snd.at[j, pl.ds(0, CAP)], inc.at[j, pl.ds(CAP, CAP)], hs.at[j, 0],
                                hr.at[j, 0], (seg, (me + devices - 1) % devices, mp)), self.mine(b))

        def right_copy(self, b):
            j = b % 2
            return (self.remote(snd.at[j, pl.ds(CAP, CAP)], inc.at[j, pl.ds(0, CAP)], hs.at[j, 1],
                                hr.at[j, 1], (seg, (me + 1) % devices, mp)), self.mine(b))

        def output_copy(self, b):
            cols = pl.ds(pl.multiple_of((b % 4) * BLOCK, BLOCK), BLOCK)
            src = g.at[b] if self.layer == 1 else mixed.at[b]
            return load(src, sections_hbm.at[0, :, cols], so.at[b % 4])


        def out_blocks(self, names):
            if not self.started:
                acc[...] = jnp.zeros_like(acc)
            self.started = True

            def block(b):
                if self.layer == 1:
                    g_load(b).wait()
                else:
                    self.recv(g.at[b], gs.at[b], gr.at[b])

                def body(rows):
                    acc[rows, :] += dot(g[b, rows, :], wbuf[0, b], 1, 1)

                loop(2 * q_rows, body)

            each(names, block)

        def attend(self):
            rows = lax.broadcasted_iota(jnp.int32, (k_rows, q_rows), 1)
            cols = lax.broadcasted_iota(jnp.int32, (k_rows, q_rows), 0)

            def one_sequence(s, carry):
                qr = pl.ds(pl.multiple_of(s * q_rows, q_rows), q_rows)
                kr_ = pl.ds(pl.multiple_of(s * k_rows, k_rows), k_rows)
                allowed = None
                for e in range(2):
                    q_len, k_off, k_len = q_len_of[s, e], k_off_of[s, e] * TILE, k_len_of[s, e]
                    hit = (rows >= e * TILE) & (rows < e * TILE + q_len)
                    hit = hit & (cols >= k_off) & (cols < k_off + k_len)
                    allowed = hit if allowed is None else allowed | hit

                def one_head(h, carry):
                    hd = pl.ds(pl.multiple_of(h * DH, DH), DH)
                    og = acc[qr, hd].astype(BF16)
                    q, k, v = q_ref[qr, hd], k_ref[kr_, hd], v_ref[kr_, hd]
                    masked = jnp.where(allowed, dot(k, q, 1, 1) * scale, masked_floor)
                    change = dot(v, og, 1, 1)
                    peak = jnp.maximum(jnp.max(masked, axis=0, keepdims=True), masked_floor / 2)
                    terms = jnp.exp(masked - peak)
                    prob = terms * (1.0 / jnp.maximum(jnp.sum(terms, axis=0, keepdims=True), 1.0))
                    prob_bf = prob.astype(BF16)
                    out_dot = jnp.sum(prob_bf.astype(F32) * change, axis=0, keepdims=True)
                    sg = (prob * (change - out_dot)).astype(BF16)
                    vg[kr_, hd] = dot(prob_bf, og, 1, 0).astype(BF16)
                    kg[kr_, hd] = (dot(sg, q, 1, 0) * scale).astype(BF16)
                    qg[qr, hd] = (dot(sg, k, 0, 0) * scale).astype(BF16)
                    return carry

                return lax.fori_loop(0, heads, one_head, carry)

            lax.fori_loop(0, 2, one_sequence, 0)

        def query_blocks(self, names):
            def block(b):
                def body(rows):
                    mixed[b, rows, :] = dot(qg[rows, :], wbuf[1, b], 1, 0).astype(BF16)

                loop(2 * q_rows, body)
                self.start(self.mixed_copy, b)

            each(names, block)

        def section_blocks(self, names):
            def total(b, rows):
                change = mixed[b, rows, :].astype(F32) + other[b, rows, :].astype(F32)
                return (g[b, rows, :].astype(F32) + change).astype(BF16)

            def block(b):
                if self.layer == 1:
                    self.recv(other.at[b], ms.at[b], mr.at[b])

                    def body(rows):
                        g[b, rows, :] = total(b, rows)

                    loop(2 * q_rows, body)
                    self.start(self.section_copy, b)
                else:

                    @pl.when(b // 4 == mp)
                    def _():
                        self.recv(other.at[b], ms.at[b], mr.at[b])

                        def body(rows):
                            mixed[b, rows, :] = total(b, rows)

                        loop(2 * q_rows, body)

                @pl.when(b // 4 == mp)
                def _():
                    self.output_copy(b).start()

            each(names, block)

        def project(self, kref, vref, dst, b):
            def body(rows):
                part = dot(kref[rows, :], wbuf[2, b], 1, 0) + dot(vref[rows, :], wbuf[3, b], 1, 0)
                dst[b, rows, :] = part.astype(BF16)

            loop(2 * k_rows, body)

        def encode(self, names):
            def block(b):
                self.project(kg, vg, parts, b)
                self.start(self.part_copy, b)

            each(names, block)

        def encode_lent(self, names):
            def block(b):
                self.project(kg_in, vg_in, lent, b)
                self.start(self.lent_copy, b)

            each(names, block)

        def give_back(self, names):
            def block(b):
                i = (b // 4) * 2 + b % 2

                @pl.when((b // 2) % 2 == mp)
                def _():
                    self.recv(lent_in.at[i], us.at[i], ur.at[i])

                    def body(rows):
                        both = lent[b, rows, :].astype(F32) + lent_in[i, rows, :].astype(F32)
                        lent[b, rows, :] = both.astype(BF16)

                    loop(2 * k_rows, body)

                self.start(self.back_copy, b)

            each(names, block)

        def reduce_cores(self, names):
            def block(b):
                if not (self.end and self.layer == 0):

                    @pl.when(b // 4 == self.layer)
                    def _():
                        self.recv(near.at[b % 4], ps.at[b], pr.at[b])

                if not self.end:

                    @pl.when(self.onward(b))
                    def _():
                        def body(rows):
                            both = parts[b, rows, :].astype(F32) + near[b % 4, rows, :].astype(F32)
                            fwd[b % 2, rows, :] = both.astype(BF16)

                        loop(2 * k_rows, body)

                self.start(self.far_copy, b)

            each(names, block)

        def reduce_heads(self, names):
            def block(b):
                j = b % 2

                @pl.when(self.mine(b))
                def _():
                    self.recv(far.at[j], ys.at[j], yr.at[j])
                    if self.end:
                        self.recv(back.at[j], rs.at[j], rr.at[j])

                    def body(t, carry):
                        rows = pl.ds(pl.multiple_of(t * TILE, TILE), TILE)
                        total = far[j, rows, :].astype(F32)
                        if self.end:
                            total += back[j, rows, :].astype(F32)
                        if not (self.end and self.layer == 1):
                            total += parts[b, rows, :].astype(F32)
                        if not (self.end and self.layer == 0):
                            total += near[b % 4, rows, :].astype(F32)
                        loc[j, t] = total.astype(BF16)
                        return carry

                    lax.fori_loop(0, 2 * k_rows // TILE, body, 0)
                    for c in range(CAP):
                        snd[j, c] = loc[j, pick_left[c]]
                        snd[j, CAP + c] = loc[j, pick_right[c]]

                self.start(self.left_copy, b)
                self.start(self.right_copy, b)

            each(names, block)

        def place(self):
            for j in range(2):
                self.recv(inc.at[j, pl.ds(CAP, CAP)], hs.at[j, 0], hr.at[j, 0])
                self.recv(inc.at[j, pl.ds(0, CAP)], hs.at[j, 1], hr.at[j, 1])
            for j in range(2):
                for t in range(tiles):
                    i = take[t]
                    kept = loc[j, jnp.minimum(i, tiles - 1)]
                    came = inc[j, jnp.clip(i - tiles, 0, 2 * CAP - 1)]
                    out_ref[t * TILE : (t + 1) * TILE, j * BLOCK : (j + 1) * BLOCK] = jnp.where(
                        i < tiles, kept, came
                    )

    for c in table_loads:
        c.wait()

    tiles = 2 * k_rows // TILE

    per = tiles // 2

    def globals_of(source):
        return [own[t % per, source * 2 + t // per] for t in range(tiles)]

    def picks(goes, to):
        seen, chosen = jnp.int32(0), [jnp.int32(0)] * CAP
        for t in range(tiles):
            hit = (goes[t] >= to * tiles) & (goes[t] < (to + 1) * tiles)
            chosen = [jnp.where(hit & (seen == c), t, chosen[c]) for c in range(CAP)]
            seen = seen + hit.astype(jnp.int32)
        return chosen

    left_of, right_of = (me + devices - 1) % devices, (me + 1) % devices
    mine_goes = globals_of(me)
    pick_left, pick_right = picks(mine_goes, left_of), picks(mine_goes, right_of)
    take = [jnp.int32(0)] * tiles
    for source, base in ((me, 0), (left_of, tiles), (right_of, tiles + CAP)):
        goes = mine_goes if base == 0 else globals_of(source)
        seen = jnp.int32(0)
        for t in range(tiles):
            slot = goes[t] - me * tiles
            hit = (slot >= 0) & (slot < tiles)
            value = t if base == 0 else base + seen
            take = [jnp.where(slot == s, value, take[s]) for s in range(tiles)]
            seen = seen + hit.astype(jnp.int32)

    def mid_upper():
        r = Role(False, 1)
        r.A(0)
        r.Be(0)
        r.C(0)
        r.A(1)
        r.Df(0)
        r.Bp(0)
        r.xrecv(0,"m")
        r.xrecv(0,"n")
        r.out_blocks(["m", "e", "n", "f", "pm", "pe", "pn"])
        r.Be(1)
        r.C(1)
        r.Dp(0)
        pl.semaphore_signal(gate, inc=1, device_id=core, device_id_type=mesh_id)
        r.xrecv(0,"f")
        r.out_blocks(["pf"])
        for c in in_loads:
            c.wait()
        r.attend()
        r.Df(1)
        r.Bp(1)
        r.A(2)
        r.A(3)
        r.Be(2)
        r.query_blocks(["m", "e", "n"])
        r.xrecv(1,"m")
        r.query_blocks(["f", "pm", "pe"])
        r.xrecv(1,"n")
        r.query_blocks(["pn"])
        r.Dp(1)
        r.xrecv(1,"f")
        r.query_blocks(["pf"])
        r.Be(3)
        r.section_blocks(["m", "e", "n"])
        r.C(2)
        r.section_blocks(["f", "pm", "pe"])
        r.section_blocks(["pn"])
        r.section_blocks(["pf"])
        r.C(3)
        r.Bp(2)
        r.Df(2)
        r.Df(3)
        r.encode(["m", "e", "n", "f"])
        r.Dp(2)
        r.Bp(3)
        r.xrecv(2,"m")
        r.xrecv(3,"m")
        r.encode(["pm", "pe"])
        r.Dp(3)
        r.recv(kg_in, ks.at[0], kr.at[0])
        r.recv(vg_in, ks.at[1], kr.at[1])
        r.encode_lent(["m", "e", "n", "f"])
        r.encode_lent(["pm", "pe"])
        r.xrecv(2,"n")
        r.xrecv(3,"n")
        r.xrecv(2,"f")
        r.xrecv(3,"f")
        r.encode(["pn", "pf"])
        r.encode_lent(["pn", "pf"])
        r.give_back(["m", "e", "n", "f"])
        r.give_back(["pm", "pe"])
        r.reduce_cores(["m", "e", "n", "f"])
        r.give_back(["pn", "pf"])
        r.reduce_cores(["pm", "pe"])
        r.reduce_cores(["pn", "pf"])
        r.reduce_heads(["m", "e", "n", "f"])
        r.reduce_heads(["pm", "pe"])
        r.reduce_heads(["pn", "pf"])
        r.place()
        r.finish()

    def mid_lower():
        r = Role(False, 0)
        pl.semaphore_wait(gate, 1)
        r.A(0)
        r.A(1)
        r.C(0)
        r.Be(0)
        r.C(1)
        r.Be(1)
        r.out_blocks(["m", "e", "n"])
        r.Bp(0)
        r.Df(0)
        r.xrecv(0,"m")
        r.out_blocks(["f", "pm", "pe"])
        r.xrecv(0,"n")
        r.out_blocks(["pn"])
        r.Bp(1)
        r.Df(1)
        r.Dp(0)
        r.xrecv(0,"f")
        r.out_blocks(["pf"])
        for c in in_loads:
            c.wait()
        r.attend()
        r.Dp(1)
        r.A(2)
        r.xrecv(1,"m")
        r.xrecv(1,"n")
        r.query_blocks(["m", "e", "n", "f", "pm", "pe", "pn"])
        r.xrecv(1,"f")
        r.query_blocks(["pf"])
        r.Be(2)
        r.C(2)
        r.A(3)
        r.Df(2)
        r.section_blocks(["m", "e", "n", "f", "pm", "pe", "pn", "pf"])
        r.Be(3)
        r.C(3)
        r.Bp(2)
        r.Df(3)
        r.encode(["m", "e", "n", "f"])
        r.Dp(2)
        r.Bp(3)
        r.reduce_cores(["m", "e", "n", "f"])
        r.xrecv(2,"m")
        r.xrecv(3,"m")
        r.encode(["pm", "pe"])
        r.reduce_cores(["pm", "pe"])
        r.Dp(3)
        r.xrecv(2,"n")
        r.xrecv(3,"n")
        r.xrecv(2,"f")
        r.xrecv(3,"f")
        r.encode(["pn", "pf"])
        r.reduce_cores(["pn", "pf"])
        r.reduce_heads(["m", "e", "n", "f"])
        r.reduce_heads(["pm", "pe"])
        r.reduce_heads(["pn", "pf"])
        r.place()
        r.finish()

    def end_upper():
        r = Role(True, 1)
        r.A(0)
        r.Bp(0)
        r.A(1)
        r.Cm(0)
        r.C(0)
        r.Bp(1)
        r.Cm(1)
        r.A(2)
        r.A(3)
        r.Df(0)
        pl.semaphore_signal(gate, inc=1, device_id=core, device_id_type=mesh_id)
        r.xrecv(0,"m")
        r.xrecv(0,"n")
        r.out_blocks(["e", "pe", "m", "pm", "n", "pn", "f"])
        r.C(1)
        r.Dp(0)
        r.xrecv(0,"f")
        r.out_blocks(["pf"])
        for c in in_loads:
            c.wait()
        r.attend()
        r.send(kg, kg_in, ks.at[0], kr.at[0], mid_peer)
        r.send(vg, vg_in, ks.at[1], kr.at[1], mid_peer)
        r.xrecv(1,"m")
        r.xrecv(1,"n")
        r.query_blocks(["e", "pe", "m", "pm", "n", "pn"])
        r.Df(1)
        r.Dp(1)
        r.xrecv(1,"f")
        r.query_blocks(["f", "pf"])
        r.section_blocks(["e", "pe", "m", "pm", "n", "pn"])
        r.section_blocks(["f", "pf"])
        r.reduce_cores(["e", "pe", "m"])
        r.reduce_cores(["pm", "n"])
        r.reduce_heads(["pm", "n"])
        r.reduce_heads(["e", "pe", "m"])
        r.reduce_cores(["pn", "f"])
        r.reduce_cores(["pf"])
        r.reduce_heads(["pn", "f"])
        r.reduce_heads(["pf"])
        r.place()
        r.finish()

    def end_lower():
        r = Role(True, 0)
        pl.semaphore_wait(gate, 1)
        r.A(0)
        r.A(1)
        r.Cm(0)
        r.Bp(0)
        r.Cm(1)
        r.Bp(1)
        r.C(0)
        r.C(1)
        r.Df(0)
        r.Df(1)
        r.A(2)
        r.Dp(0)
        r.xrecv(0,"m")
        r.out_blocks(["e", "pe", "m", "pm"])
        r.xrecv(0,"n")
        r.xrecv(0,"f")
        r.out_blocks(["n", "pn", "f", "pf"])
        for c in in_loads:
            c.wait()
        r.attend()
        r.Cm(2)
        r.A(3)
        r.Bp(2)
        r.xrecv(1,"m")
        r.query_blocks(["e", "pe", "m", "pm"])
        r.xrecv(1,"n")
        r.query_blocks(["n", "pn"])
        r.xrecv(1,"f")
        r.query_blocks(["f", "pf"])
        r.C(2)
        r.Cm(3)
        r.Bp(3)
        r.encode(["e", "pe", "m"])
        r.Df(2)
        r.reduce_cores(["e", "pe", "m"])
        r.section_blocks(["e", "pe", "m", "pm", "n", "pn", "f", "pf"])
        r.C(3)
        r.xrecv(2,"m")
        r.xrecv(3,"m")
        r.encode(["pm", "n"])
        r.Df(3)
        r.reduce_cores(["pm", "n"])
        r.xrecv(2,"n")
        r.xrecv(3,"n")
        r.encode(["pn", "f"])
        r.reduce_cores(["pn", "f"])
        r.reduce_heads(["pm", "n"])
        r.xrecv(2,"f")
        r.xrecv(3,"f")
        r.encode(["pf"])
        r.reduce_cores(["pf"])
        r.reduce_heads(["e", "pe", "m"])
        r.reduce_heads(["pn", "f"])
        r.reduce_heads(["pf"])
        r.place()
        r.finish()

    for wanted_end, layer, program in (
        (False, 1, mid_upper), (False, 0, mid_lower), (True, 1, end_upper), (True, 0, end_lower)
    ):
        place_here = at_end if wanted_end else jnp.logical_not(at_end)
        pl.when(place_here & (seg == layer))(program)


def run_chain(tables, top, q, k, v, wo, wq, wk, wv, devices):
    micro = tables[0].shape[0]
    q_rows, k_rows = top.shape[0] // micro, k.shape[1] // micro
    width, depth = top.shape[1], q.shape[2]
    half, blocks = width // 2, width // BLOCK
    keys = micro * k_rows
    tiles = keys // TILE
    vmem, any_ = (pl.BlockSpec(memory_space=m) for m in (pltpu.VMEM, pl.ANY))
    dma = pltpu.SemaphoreType.DMA

    def buf(*shape, dtype=BF16):
        return pltpu.VMEM(shape, dtype)

    sections, owned = pl.pallas_call(
        functools.partial(chain_kernel, (q_rows, k_rows, depth // DH, devices)),
        in_specs=[any_] * 12,
        out_specs=[any_, vmem],
        out_shape=[
            jax.ShapeDtypeStruct((1, micro * q_rows, half), BF16),
            jax.ShapeDtypeStruct((keys, width // 4), BF16),
        ],
        scratch_shapes=[
            buf(4, blocks, depth, BLOCK),
            buf(blocks, micro * q_rows, BLOCK),
            buf(micro * q_rows, depth),
            buf(keys, depth),
            buf(keys, depth),
            buf(micro * q_rows, depth, dtype=F32),
            buf(micro * q_rows, depth),
            buf(keys, depth),
            buf(keys, depth),
            buf(blocks, micro * q_rows, BLOCK),
            buf(blocks, micro * q_rows, BLOCK),
            buf(blocks, keys, BLOCK),
            buf(4, keys, BLOCK),
            buf(2, keys, BLOCK),
            buf(2, keys, BLOCK),
            buf(keys, depth),
            buf(keys, depth),
            buf(blocks, keys, BLOCK),
            buf(4, keys, BLOCK),
            buf(2, keys, BLOCK),
            buf(2, tiles, TILE, BLOCK),
            buf(2, 2 * CAP, TILE, BLOCK),
            buf(2, 2 * CAP, TILE, BLOCK),
        ]
        + [dma((4,)), dma((8,)), dma((3,))]
        + [dma((9, 4))] * 2
        + [dma((4, 4))] * 2
        + [dma((8,))] * 4
        + [dma((2,))] * 2
        + [dma((8,))] * 2
        + [dma((2,))] * 2
        + [dma((4,))] * 2
        + [dma((4,)), dma((2,))]
        + [dma((2, 2))] * 2
        + [dma((4,))]
        + [pltpu.SemaphoreType.REGULAR]
        + [pltpu.SMEM(t.shape, jnp.int32) for t in tables]
        + [dma((4,))],
        compiler_params=pltpu.CompilerParams(
            collective_id=0, has_side_effects=True, vmem_limit_bytes=60 << 20
        ),
    )(*tables, top, q, k, v, wo, wq, wk, wv)
    return pl.pallas_call(
        hand_over_kernel,
        in_specs=[any_] * 2,
        out_specs=[any_] * 2,
        out_shape=[jax.ShapeDtypeStruct(a.shape, a.dtype) for a in (sections, owned)],
        scratch_shapes=[pltpu.VMEM(a.shape, a.dtype) for a in (sections, owned)] + [dma((2, 2, 4))],
    )(sections, owned)


def hand_over_kernel(a_in, b_in, a_out, b_out, a_mid, b_mid, sems):
    inward, outward = [], []
    for i in range(4):
        for n, (src, mid, dst) in enumerate(
            ((a_in.at[0], a_mid.at[0], a_out.at[0]), (b_in, b_mid, b_out))
        ):
            rows = src.shape[0] // 4
            at = pl.ds(i * rows, rows)
            inward.append(pltpu.make_async_copy(src.at[at], mid.at[at], sems.at[0, n, i]))
            outward.append(pltpu.make_async_copy(mid.at[at], dst.at[at], sems.at[1, n, i]))
    for c in inward:
        c.start()
    for c, d in zip(inward, outward):
        c.wait()
        d.start()
    for d in outward:
        d.wait()


def ranked(marked):
    ids = jnp.arange(marked.shape[0], dtype=jnp.int32)
    upto = ids[None, :] <= ids[:, None]
    return jnp.sum((upto & marked[None, :]).astype(jnp.int32), axis=1) - 1


def on_device(
    grad_top,
    saved_query,
    saved_key,
    saved_value,
    w_query,
    w_key,
    w_value,
    w_out,
    query_length,
    key_offset,
    key_length,
    tile_owner,
):
    seg = lax.axis_index("segment")
    mp = lax.axis_index("mp")
    devices = lax.axis_size("dp")
    me = lax.axis_index("dp")
    micro = query_length.shape[0]
    q_rows = grad_top.shape[0] // micro
    k_rows = saved_key.shape[1] // micro
    half = grad_top.shape[1] // 2
    mp_swap = [(0, 1), (1, 0)]
    if w_out.shape[2] == BLOCK and devices == 8 and micro == 2:
        return run_chain(
            (query_length, key_offset, key_length, tile_owner.T), grad_top, saved_query, saved_key,
            saved_value, w_out, w_query, w_key, w_value, devices,
        )

    wo, sources = gathered(w_out[0])
    wq, _ = gathered(w_query[0])
    wk, _ = gathered(w_key[0])
    wv, _ = gathered(w_value[0])
    order = jnp.stack(sources).astype(jnp.int32)

    top = grad_top.reshape(grad_top.shape[0], 2, half).transpose(1, 0, 2)
    scalars = [
        jnp.concatenate([order, query_length[s], key_offset[s], key_length[s]])
        for s in range(micro)
    ]

    def tick(s, grad, at):
        return run_tick(
            scalars[s], grad, at, s, saved_query, saved_key, saved_value, wo, wq, q_rows, k_rows
        )

    upper = [tick(s, top, s) for s in range(micro)]
    upper_half, incoming = [], []
    for s in range(micro):
        mixed = upper[s][0]
        other = lax.ppermute(mixed, "mp", mp_swap)
        rows = top[:, s * q_rows : (s + 1) * q_rows]
        section = (rows.astype(F32) + (mixed.astype(F32) + other.astype(F32))).astype(BF16)
        incoming.append(lax.ppermute(section, "segment", [(1, 0)]))
        upper_half.append(lax.dynamic_index_in_dim(section, mp, 0, keepdims=False))
    lower = [tick(s, incoming[s], 0) for s in range(micro)]
    halves = []
    for s in range(micro):
        mixed = lower[s][0]
        other = lax.ppermute(
            lax.dynamic_index_in_dim(mixed, 1 - mp, 0, keepdims=False), "mp", mp_swap
        )
        own = lax.dynamic_index_in_dim(mixed, mp, 0, keepdims=False)
        base = lax.dynamic_index_in_dim(incoming[s], mp, 0, keepdims=False)
        low = (base.astype(F32) + (own.astype(F32) + other.astype(F32))).astype(BF16)
        halves.append(jnp.where(seg == 1, upper_half[s], low))
    sections = jnp.concatenate(halves, axis=0)[None]

    kg = jnp.concatenate([jnp.where(seg == 1, upper[s][1], lower[s][1]) for s in range(micro)], 0)
    vg = jnp.concatenate([jnp.where(seg == 1, upper[s][2], lower[s][2]) for s in range(micro)], 0)
    parts = run_encoder(order, kg, vg, wk, wv)
    away = lax.dynamic_slice_in_dim(parts, (1 - seg) * 2, 2, 0)
    mine = lax.dynamic_slice_in_dim(parts, seg * 2, 2, 0)
    arrived = lax.ppermute(away, "segment", mp_swap)
    summed = (mine.astype(F32) + arrived.astype(F32)).astype(BF16)
    crossing = lax.ppermute(
        lax.dynamic_index_in_dim(summed, 1 - mp, 0, keepdims=False), "mp", mp_swap
    )
    kept = lax.dynamic_index_in_dim(summed, mp, 0, keepdims=False)
    kept = (kept.astype(F32) + crossing.astype(F32)).astype(BF16)

    tiles = kept.shape[0] // TILE
    features = kept.shape[1]
    owners = tile_owner.reshape(devices, tiles)
    slot_ids = jnp.arange(CAP, dtype=jnp.int32)[:, None]
    tile_ids = jnp.arange(tiles, dtype=jnp.int32)

    def plan(source):
        source = source % devices
        row = lax.dynamic_index_in_dim(owners, source, 0, keepdims=False)
        return (row // tiles - source + devices) % devices, row % tiles

    def ranks_of(marked):
        return (ranked(marked)[None, :] == slot_ids) & marked[None, :]

    step, slot = plan(me)
    left_step, left_slot = plan(me - 1 + devices)
    right_step, right_slot = plan(me + 1)
    send_left = jnp.sum(jnp.where(ranks_of(step == devices - 1), tile_ids[None, :], 0), axis=1)
    send_right = jnp.sum(jnp.where(ranks_of(step == 1), tile_ids[None, :], 0), axis=1)
    left_hit = ranks_of(left_step == 1)
    right_hit = ranks_of(right_step == devices - 1)
    target = jnp.concatenate(
        [
            jnp.sum(jnp.where(left_hit, left_slot[None, :], 0), axis=1),
            slot,
            jnp.sum(jnp.where(right_hit, right_slot[None, :], 0), axis=1),
        ]
    )
    usable = jnp.concatenate([jnp.any(left_hit, axis=1), step == 0, jnp.any(right_hit, axis=1)])
    chosen = (tile_ids[:, None] == target[None, :]) & usable[None, :]
    candidate_ids = jnp.arange(target.shape[0], dtype=jnp.int32)
    take = jnp.sum(jnp.where(chosen, candidate_ids[None, :], 0), axis=1)

    tiled = (tiles, TILE, features)
    shape = jax.ShapeDtypeStruct(tiled, BF16)
    handed = jax.ShapeDtypeStruct((CAP, TILE, features), BF16)
    local = kept.reshape(tiled)
    to_left, to_right = small_call(
        pick_kernel, jnp.concatenate([send_left, send_right]), [local], [handed, handed]
    )
    forward = [(i, (i + 1) % devices) for i in range(devices)]
    backward = [(b, a) for a, b in forward]
    from_left = lax.ppermute(to_right, "dp", forward)
    from_right = lax.ppermute(to_left, "dp", backward)
    owned = small_call(place_kernel, take, [from_left, local, from_right], shape)
    return sections, owned.reshape(tiles * TILE, features)


def solution(mesh):
    in_specs = (
        P("dp", None),
        P("segment", "dp", "mp"),
        P("segment", "dp", "mp"),
        P("segment", "dp", "mp"),
        P("segment", "mp", "dp"),
        P("segment", "mp", "dp"),
        P("segment", "mp", "dp"),
        P("segment", "mp", "dp"),
        P("dp", None),
        P("dp", None),
        P("dp", None),
        P(),
    )
    out_specs = (P("segment", "dp", "mp"), P("dp", ("segment", "mp")))
    return jax.shard_map(
        on_device, mesh=mesh, in_specs=in_specs, out_specs=out_specs, check_vma=False
    )
```

```python
import functools

import jax
import jax.numpy as jnp
from jax import lax
from jax.experimental import pallas as pl
from jax.experimental.pallas import tpu as pltpu
from jax.sharding import PartitionSpec as P

DH = 256
TILE = 128
CAP = 2
BLOCK = 256
masked_floor = -1e30
BF16, F32 = jnp.bfloat16, jnp.float32


def dot(a, b, ca, cb):
    return lax.dot_general(a, b, (((ca,), (cb,)), ((), ())), preferred_element_type=F32)


def tick_kernel(count, half, sc, g_ref, q_ref, k_ref, v_ref, *rest):
    wo, wq = rest[:count], rest[count : 2 * count]
    mixed_ref, kg_ref, vg_ref, acc = rest[2 * count :]
    head = pl.program_id(0)
    per = half // BLOCK
    scale = DH ** (-0.5)

    def place(b):
        src = sc[b]
        return src // per, pl.ds(pl.multiple_of((src % per) * BLOCK, BLOCK), BLOCK)

    og = None
    for b in range(count):
        at, cols = place(b)
        term = dot(g_ref[at, :, cols], wo[b][...], 1, 1)
        og = term if og is None else og + term
    og = og.astype(BF16)
    q, k, v = q_ref[0], k_ref[0], v_ref[0]
    scores = dot(q, k, 1, 1) * scale
    rows = lax.broadcasted_iota(jnp.int32, scores.shape, 0)
    cols_id = lax.broadcasted_iota(jnp.int32, scores.shape, 1)
    allowed = None
    for e in range(2):
        q_len, k_off, k_len = sc[count + e], sc[count + 2 + e] * TILE, sc[count + 4 + e]
        hit = (rows >= e * TILE) & (rows < e * TILE + q_len)
        hit = hit & (cols_id >= k_off) & (cols_id < k_off + k_len)
        allowed = hit if allowed is None else allowed | hit
    masked = jnp.where(allowed, scores, masked_floor)
    top = jnp.max(masked, axis=-1, keepdims=True)
    terms = jnp.where(allowed, jnp.exp(masked - top), 0.0)
    prob = terms / jnp.maximum(jnp.sum(terms, axis=-1, keepdims=True), 1.0)
    prob_bf = prob.astype(BF16)
    attended = dot(prob_bf, v, 1, 0)
    out_dot = jnp.sum(og.astype(F32) * attended, axis=-1, keepdims=True)
    sg = (prob * (dot(og, v, 1, 1) - out_dot)).astype(BF16)
    qg = (dot(sg, k, 1, 0) * scale).astype(BF16)
    kg_ref[...] = (dot(sg, q, 0, 0) * scale).astype(BF16)
    vg_ref[...] = dot(prob_bf, og, 0, 0).astype(BF16)

    @pl.when(head == 0)
    def _():
        acc[...] = jnp.zeros_like(acc)

    for b in range(count):
        at, cols = place(b)
        acc[at, :, cols] += dot(qg, wq[b][...], 1, 0)

    @pl.when(head == pl.num_programs(0) - 1)
    def _():
        mixed_ref[...] = acc[...].astype(BF16)


def run_tick(scalars, grad, at, seq, saved_q, saved_k, saved_v, wo, wq, q_rows, k_rows):
    half = grad.shape[2]
    heads = saved_q.shape[2] // DH
    count = len(wo)
    weight = pl.BlockSpec((DH, BLOCK), lambda h, sc: (h, 0))
    macs = heads * q_rows * DH * (4 * half + 6 * k_rows)
    return pl.pallas_call(
        functools.partial(tick_kernel, count, half),
        grid_spec=pltpu.PrefetchScalarGridSpec(
            num_scalar_prefetch=1,
            grid=(heads,),
            in_specs=[
                pl.BlockSpec((2, q_rows, half), lambda h, sc: (0, at, 0)),
                pl.BlockSpec((1, q_rows, DH), lambda h, sc: (0, seq, h)),
                pl.BlockSpec((1, k_rows, DH), lambda h, sc: (0, seq, h)),
                pl.BlockSpec((1, k_rows, DH), lambda h, sc: (0, seq, h)),
            ]
            + [weight] * (2 * count),
            out_specs=[
                pl.BlockSpec((2, q_rows, half), lambda h, sc: (0, 0, 0)),
                pl.BlockSpec((k_rows, DH), lambda h, sc: (0, h)),
                pl.BlockSpec((k_rows, DH), lambda h, sc: (0, h)),
            ],
            scratch_shapes=[pltpu.VMEM((2, q_rows, half), F32)],
        ),
        out_shape=[
            jax.ShapeDtypeStruct((2, q_rows, half), BF16),
            jax.ShapeDtypeStruct((k_rows, heads * DH), BF16),
            jax.ShapeDtypeStruct((k_rows, heads * DH), BF16),
        ],
        compiler_params=pltpu.CompilerParams(vmem_limit_bytes=40 << 20),
        cost_estimate=pl.CostEstimate(
            flops=2 * macs, bytes_accessed=16 << 20, transcendentals=heads * q_rows * k_rows
        ),
    )(scalars, grad, saved_q, saved_k, saved_v, *wo, *wq)


def encoder_kernel(count, quarter, sc, kg_ref, vg_ref, *rest):
    wk, wv, out_ref = rest[:count], rest[count : 2 * count], rest[2 * count]
    per = quarter // BLOCK
    kg, vg = kg_ref[...], vg_ref[...]
    for b in range(count):
        src = sc[b]
        cols = pl.ds(pl.multiple_of((src % per) * BLOCK, BLOCK), BLOCK)
        part = dot(kg, wk[b][...], 1, 0) + dot(vg, wv[b][...], 1, 0)
        out_ref[src // per, :, cols] = part.astype(BF16)


def run_encoder(scalars, kg, vg, wk, wv):
    count = len(wk)
    rows, depth = kg.shape
    quarter = count * BLOCK // 4
    step = 256
    whole = pl.BlockSpec((depth, BLOCK), lambda i, sc: (0, 0))
    return pl.pallas_call(
        functools.partial(encoder_kernel, count, quarter),
        grid_spec=pltpu.PrefetchScalarGridSpec(
            num_scalar_prefetch=1,
            grid=(rows // step,),
            in_specs=[pl.BlockSpec((step, depth), lambda i, sc: (i, 0))] * 2
            + [whole] * (2 * count),
            out_specs=pl.BlockSpec((4, step, quarter), lambda i, sc: (0, i, 0)),
        ),
        out_shape=jax.ShapeDtypeStruct((4, rows, quarter), BF16),
        compiler_params=pltpu.CompilerParams(vmem_limit_bytes=48 << 20),
        cost_estimate=pl.CostEstimate(
            flops=16 * rows * depth * quarter, bytes_accessed=14 << 20, transcendentals=0
        ),
    )(scalars, kg, vg, *wk, *wv)


def pick_kernel(sc, local_ref, left_ref, right_ref):
    for c in range(CAP):
        left_ref[c] = local_ref[sc[c]]
        right_ref[c] = local_ref[sc[CAP + c]]


def place_kernel(sc, left_ref, local_ref, right_ref, out_ref):
    tiles = local_ref.shape[0]
    for s in range(tiles):
        i = sc[s]

        @pl.when(i < CAP)
        def _():
            out_ref[s] = left_ref[jnp.minimum(i, CAP - 1)]

        @pl.when((i >= CAP) & (i < CAP + tiles))
        def _():
            out_ref[s] = local_ref[jnp.clip(i - CAP, 0, tiles - 1)]

        @pl.when(i >= CAP + tiles)
        def _():
            out_ref[s] = right_ref[jnp.clip(i - CAP - tiles, 0, CAP - 1)]


def small_call(body, scalars, arrays, outs):
    vmem = pl.BlockSpec(memory_space=pltpu.VMEM)
    single = not isinstance(outs, list)
    return pl.pallas_call(
        body,
        in_specs=[pl.BlockSpec(memory_space=pltpu.SMEM)] + [vmem] * len(arrays),
        out_specs=vmem if single else [vmem] * len(outs),
        out_shape=outs,
        compiler_params=pltpu.CompilerParams(vmem_limit_bytes=24 << 20),
    )(scalars, *arrays)


def gathered(shard):
    full = lax.all_gather(shard, "dp", axis=1, tiled=True)
    blocks = [full[:, i : i + BLOCK] for i in range(0, full.shape[1], BLOCK)]
    return blocks, list(jnp.arange(len(blocks), dtype=jnp.int32))


def chain_kernel(dims, ql_hbm, ko_hbm, kl_hbm, own_hbm, top_hbm, q_hbm, k_hbm, v_hbm, wo_hbm, wq_hbm, wk_hbm, wv_hbm,
                 sections_hbm, out_ref,
                 wbuf, g, q_ref, k_ref, v_ref, acc, qg, kg, vg, mixed, other, parts, near, fwd, far,
                 kg_in, vg_in, lent, lent_in, back, loc, inc, snd,
                 ldw, ldg, ldq, zs, zr, xs, xr, ms, mr, gs, gr, ks, kr, ps, pr, ys, yr,
                 us, ur, rs, rr, hs, hr, so, gate,
                 q_len_of, k_off_of, k_len_of, own, ldt):
    q_rows, k_rows, heads, devices = dims
    depth = heads * DH
    scale = DH ** (-0.5)
    seg, me, mp = lax.axis_index("segment"), lax.axis_index("dp"), lax.axis_index("mp")
    z, x = me // 2, me % 2
    side = z // 2
    mesh_id = pl.DeviceIdType.MESH
    plane = {"e": 3 * side, "m": 1 + side, "n": 2 - side, "f": 3 - 3 * side}
    blk = {c: plane[c] * 2 + x for c in plane}
    blk.update({"p" + c: plane[c] * 2 + 1 - x for c in plane})
    at_end = (z == 0) | (z == 3)
    side_peer, cross, core = (seg, z * 2 + 1 - x, mp), (seg, me, 1 - mp), (1 - seg, me, mp)
    diag = jnp.where(x == 0, (me + devices - 1) % devices, (me + 1) % devices)
    end_peer, mid_peer = (seg, plane["e"] * 2 + x, mp), (seg, plane["m"] * 2 + x, mp)
    far_mid = (seg, plane["n"] * 2 + x, mp)
    upper, lower = pl.ds(0, depth // 2), pl.ds(depth // 2, depth // 2)
    whole = pl.ds(0, depth)
    step = 256

    def load(src, dst, sem):
        return pltpu.make_async_copy(src, dst, sem)

    weights = (wo_hbm, wq_hbm, wk_hbm, wv_hbm)
    w_loads = [load(weights[u].at[0], wbuf.at[u, me], ldw.at[u]) for u in range(4)]
    in_loads = [load(a.at[0], b, ldq.at[i])
                for i, (a, b) in enumerate(((q_hbm, q_ref), (k_hbm, k_ref), (v_hbm, v_ref)))]

    def g_load(b):
        cols = pl.ds(pl.multiple_of(b * BLOCK, BLOCK), BLOCK)
        return load(top_hbm.at[:, cols], g.at[b], ldg.at[b])

    tables = ((ql_hbm, q_len_of), (ko_hbm, k_off_of), (kl_hbm, k_len_of), (own_hbm, own))
    table_loads = [load(a, b, ldt.at[i]) for i, (a, b) in enumerate(tables)]
    w_loads[0].start()

    barrier = pltpu.get_barrier_semaphore()

    def greet(peers):
        for peer in peers:
            pl.semaphore_signal(barrier, inc=1, device_id=peer, device_id_type=mesh_id)

    all_peers = [side_peer, cross, core, (seg, diag, mp)]
    greet(all_peers)

    @pl.when(at_end)
    def _():
        greet([mid_peer])

        @pl.when(seg == 0)
        def _():
            greet([(1, plane["m"] * 2 + x, mp)])

    @pl.when(jnp.logical_not(at_end))
    def _():
        greet([end_peer, far_mid])

        @pl.when(seg == 1)
        def _():
            greet([(0, plane["e"] * 2 + x, mp)])

    @pl.when(seg == 1)
    def _():
        for b in range(8):
            g_load(b).start()

    for c in w_loads[1:] + in_loads + table_loads:
        c.start()
    for c in w_loads:
        c.wait()

    pl.semaphore_wait(barrier, jnp.where(at_end, 6 - seg, 6 + seg))

    def loop(rows, body):
        def one(i, carry):
            body(pl.ds(pl.multiple_of(i * step, step), step))
            return carry

        lax.fori_loop(0, rows // step, one, 0)

    def each(names, body):
        ids = [blk[n] for n in names]

        def one(i, carry):
            b = ids[0]
            for j in range(1, len(ids)):
                b = jnp.where(i == j, ids[j], b)
            body(b)
            return carry

        if len(ids) == 1:
            body(ids[0])
        else:
            lax.fori_loop(0, len(ids), one, 0)

    class Role:
        def __init__(self, end, layer):
            self.end, self.layer = end, layer
            self.pending = []
            self.started = False
            upper_end = end and layer == 1
            self.makers = [self.mixed_copy, self.far_copy, self.left_copy, self.right_copy]
            if layer == 1:
                self.makers.append(self.section_copy)
            if not upper_end:
                self.makers.append(self.part_copy)
            if layer == 1 and not end:
                self.makers += [self.lent_copy, self.back_copy]


        def send(self, src, dst, a, b, peer, cond=None):
            copy = pltpu.make_async_remote_copy(
                src_ref=src, dst_ref=dst, send_sem=a, recv_sem=b, device_id=peer, device_id_type=mesh_id
            )
            self.pending.append((cond, copy))
            if cond is None:
                copy.start()
            else:
                pl.when(cond)(copy.start)

        def recv(self, dst, a, b):
            pltpu.make_async_remote_copy(
                src_ref=dst, dst_ref=dst, send_sem=a, recv_sem=b, device_id=side_peer,
                device_id_type=mesh_id,
            ).wait_recv()

        def remote(self, src, dst, a, b, peer):
            return pltpu.make_async_remote_copy(
                src_ref=src, dst_ref=dst, send_sem=a, recv_sem=b, device_id=peer, device_id_type=mesh_id
            )

        def finish(self):
            for _, copy in self.pending:
                copy.wait_send()

            def one(b, carry):
                for make in self.makers:
                    copy, cond = make(b)
                    if cond is None:
                        copy.wait_send()
                    else:
                        pl.when(cond)(copy.wait_send)
                return carry

            lax.fori_loop(0, 8, one, 0)
            for i in range(4):
                self.output_copy(4 * mp + i).wait()

        def start(self, make, b):
            copy, cond = make(b)
            if cond is None:
                copy.start()
            else:
                pl.when(cond)(copy.start)

        def w(self, u, name, rows=whole):
            return wbuf.at[u, blk[name], rows]

        def zsend(self, kind, u, name, peer, rows=whole):
            ref = self.w(u, name, rows)
            self.send(ref, ref, zs.at[kind, u], zr.at[kind, u], peer)

        def zrecv(self, kind, u, name, rows=whole):
            self.recv(self.w(u, name, rows), zs.at[kind, u], zr.at[kind, u])

        def lent_unit(self, u):
            return self.layer == 1 and u >= 2

        def twice(self, u):
            return u < (2 if self.layer == 1 else 1)

        def x_rows(self, u, name):
            if name != "f":
                return whole
            return lower if not self.end or self.twice(u) else whole

        def xsend(self, u, name):
            ref = self.w(u, name, self.x_rows(u, name))
            i = "emnf".index(name)
            self.send(ref, ref, xs.at[i, u], xr.at[i, u], side_peer)

        def xrecv(self, u, name):
            i = "emnf".index(name)
            self.recv(self.w(u, "p" + name, self.x_rows(u, name)), xs.at[i, u], xr.at[i, u])

        def A(self, u):
            if self.end:
                self.zsend(0, u, "e", mid_peer)
                if not self.lent_unit(u):
                    self.xsend(u, "e")
            else:
                if not self.lent_unit(u):
                    self.zsend(2, u, "m", end_peer)
                self.zsend(6, u, "m", far_mid)
                self.xsend(u, "m")

        def Be(self, u):
            self.zrecv(0, u, "e")
            self.zsend(7, u, "e", far_mid)
            if self.lent_unit(u):
                self.xsend(u, "e")

        def Bp(self, u):
            if self.end:
                self.xrecv(u, "e")
                self.zsend(1, u, "pe", mid_peer)
            else:
                if self.lent_unit(u):
                    self.xrecv(u, "e")
                else:
                    self.zrecv(1, u, "pe")
                self.zsend(8, u, "pe", far_mid, upper)

        def Cm(self, u):
            self.zrecv(2, u, "m")
            self.xsend(u, "m")

        def C(self, u):
            if self.end:
                self.zrecv(3, u, "n")
                self.xsend(u, "n")
            else:
                self.zrecv(6, u, "n")
                if not self.lent_unit(u):
                    self.zsend(3, u, "n", end_peer)
                self.xsend(u, "n")

        def Df(self, u):
            if self.end:
                self.zrecv(4, u, "f")
            else:
                self.zrecv(7, u, "f")
                if not self.lent_unit(u):
                    self.zsend(4, u, "f", end_peer)
            self.xsend(u, "f")

        def Dp(self, u):
            if self.end:
                self.zrecv(5, u, "pf", upper)
            else:
                self.zrecv(8, u, "pf", upper)
                if self.twice(u):
                    self.zsend(5, u, "pf", end_peer, upper)


        def mixed_copy(self, b):
            return (self.remote(mixed.at[b], other.at[b], ms.at[b], mr.at[b], cross),
                    None if self.layer == 1 else b // 4 != mp)

        def section_copy(self, b):
            return self.remote(g.at[b], g.at[b], gs.at[b], gr.at[b], core), None

        def part_copy(self, b):
            return (self.remote(parts.at[b], near.at[b % 4], ps.at[b], pr.at[b], core),
                    b // 4 != self.layer)

        def lent_copy(self, b):
            i = (b // 4) * 2 + b % 2
            return (self.remote(lent.at[b], lent_in.at[i], us.at[i], ur.at[i], cross),
                    (b // 2) % 2 != mp)

        def back_copy(self, b):
            i, j = (b // 4) * 2 + b % 2, b % 2
            return (self.remote(lent.at[b], back.at[j], rs.at[i], rr.at[j],
                                (b // 4, plane["e"] * 2 + x, mp)), (b // 2) % 2 == mp)

        def onward(self, b):
            return (b // 4 == self.layer) & ((b // 2) % 2 != mp)

        def mine(self, b):
            return (b // 4 == self.layer) & ((b // 2) % 2 == mp)

        def far_copy(self, b):
            j = b % 2
            if self.end:
                src = parts.at[b] if self.layer == 0 else near.at[b % 4]
            else:
                src = fwd.at[j]
            return self.remote(src, far.at[j], ys.at[j], yr.at[j], cross), self.onward(b)

        def left_copy(self, b):
            j = b % 2
            return (self.remote(snd.at[j, pl.ds(0, CAP)], inc.at[j, pl.ds(CAP, CAP)], hs.at[j, 0],
                                hr.at[j, 0], (seg, (me + devices - 1) % devices, mp)), self.mine(b))

        def right_copy(self, b):
            j = b % 2
            return (self.remote(snd.at[j, pl.ds(CAP, CAP)], inc.at[j, pl.ds(0, CAP)], hs.at[j, 1],
                                hr.at[j, 1], (seg, (me + 1) % devices, mp)), self.mine(b))

        def output_copy(self, b):
            cols = pl.ds(pl.multiple_of((b % 4) * BLOCK, BLOCK), BLOCK)
            src = g.at[b] if self.layer == 1 else mixed.at[b]
            return load(src, sections_hbm.at[0, :, cols], so.at[b % 4])


        def out_blocks(self, names):
            if not self.started:
                acc[...] = jnp.zeros_like(acc)
            self.started = True

            def block(b):
                if self.layer == 1:
                    g_load(b).wait()
                else:
                    self.recv(g.at[b], gs.at[b], gr.at[b])

                def body(rows):
                    acc[rows, :] += dot(g[b, rows, :], wbuf[0, b], 1, 1)

                loop(2 * q_rows, body)

            each(names, block)

        def attend(self):
            rows = lax.broadcasted_iota(jnp.int32, (k_rows, q_rows), 1)
            cols = lax.broadcasted_iota(jnp.int32, (k_rows, q_rows), 0)

            def one_sequence(s, carry):
                qr = pl.ds(pl.multiple_of(s * q_rows, q_rows), q_rows)
                kr_ = pl.ds(pl.multiple_of(s * k_rows, k_rows), k_rows)
                allowed = None
                for e in range(2):
                    q_len, k_off, k_len = q_len_of[s, e], k_off_of[s, e] * TILE, k_len_of[s, e]
                    hit = (rows >= e * TILE) & (rows < e * TILE + q_len)
                    hit = hit & (cols >= k_off) & (cols < k_off + k_len)
                    allowed = hit if allowed is None else allowed | hit

                def one_head(h, carry):
                    hd = pl.ds(pl.multiple_of(h * DH, DH), DH)
                    og = acc[qr, hd].astype(BF16)
                    q, k, v = q_ref[qr, hd], k_ref[kr_, hd], v_ref[kr_, hd]
                    masked = jnp.where(allowed, dot(k, q, 1, 1) * scale, masked_floor)
                    change = dot(v, og, 1, 1)
                    peak = jnp.maximum(jnp.max(masked, axis=0, keepdims=True), masked_floor / 2)
                    terms = jnp.exp(masked - peak)
                    prob = terms * (1.0 / jnp.maximum(jnp.sum(terms, axis=0, keepdims=True), 1.0))
                    prob_bf = prob.astype(BF16)
                    out_dot = jnp.sum(prob_bf.astype(F32) * change, axis=0, keepdims=True)
                    sg = (prob * (change - out_dot)).astype(BF16)
                    vg[kr_, hd] = dot(prob_bf, og, 1, 0).astype(BF16)
                    kg[kr_, hd] = (dot(sg, q, 1, 0) * scale).astype(BF16)
                    qg[qr, hd] = (dot(sg, k, 0, 0) * scale).astype(BF16)
                    return carry

                return lax.fori_loop(0, heads, one_head, carry)

            lax.fori_loop(0, 2, one_sequence, 0)

        def query_blocks(self, names):
            def block(b):
                def body(rows):
                    mixed[b, rows, :] = dot(qg[rows, :], wbuf[1, b], 1, 0).astype(BF16)

                loop(2 * q_rows, body)
                self.start(self.mixed_copy, b)

            each(names, block)

        def section_blocks(self, names):
            def total(b, rows):
                change = mixed[b, rows, :].astype(F32) + other[b, rows, :].astype(F32)
                return (g[b, rows, :].astype(F32) + change).astype(BF16)

            def block(b):
                if self.layer == 1:
                    self.recv(other.at[b], ms.at[b], mr.at[b])

                    def body(rows):
                        g[b, rows, :] = total(b, rows)

                    loop(2 * q_rows, body)
                    self.start(self.section_copy, b)
                else:

                    @pl.when(b // 4 == mp)
                    def _():
                        self.recv(other.at[b], ms.at[b], mr.at[b])

                        def body(rows):
                            mixed[b, rows, :] = total(b, rows)

                        loop(2 * q_rows, body)

                @pl.when(b // 4 == mp)
                def _():
                    self.output_copy(b).start()

            each(names, block)

        def project(self, kref, vref, dst, b):
            def body(rows):
                part = dot(kref[rows, :], wbuf[2, b], 1, 0) + dot(vref[rows, :], wbuf[3, b], 1, 0)
                dst[b, rows, :] = part.astype(BF16)

            loop(2 * k_rows, body)

        def encode(self, names):
            def block(b):
                self.project(kg, vg, parts, b)
                self.start(self.part_copy, b)

            each(names, block)

        def encode_lent(self, names):
            def block(b):
                self.project(kg_in, vg_in, lent, b)
                self.start(self.lent_copy, b)

            each(names, block)

        def give_back(self, names):
            def block(b):
                i = (b // 4) * 2 + b % 2

                @pl.when((b // 2) % 2 == mp)
                def _():
                    self.recv(lent_in.at[i], us.at[i], ur.at[i])

                    def body(rows):
                        both = lent[b, rows, :].astype(F32) + lent_in[i, rows, :].astype(F32)
                        lent[b, rows, :] = both.astype(BF16)

                    loop(2 * k_rows, body)

                self.start(self.back_copy, b)

            each(names, block)

        def reduce_cores(self, names):
            def block(b):
                if not (self.end and self.layer == 0):

                    @pl.when(b // 4 == self.layer)
                    def _():
                        self.recv(near.at[b % 4], ps.at[b], pr.at[b])

                if not self.end:

                    @pl.when(self.onward(b))
                    def _():
                        def body(rows):
                            both = parts[b, rows, :].astype(F32) + near[b % 4, rows, :].astype(F32)
                            fwd[b % 2, rows, :] = both.astype(BF16)

                        loop(2 * k_rows, body)

                self.start(self.far_copy, b)

            each(names, block)

        def reduce_heads(self, names):
            def block(b):
                j = b % 2

                @pl.when(self.mine(b))
                def _():
                    self.recv(far.at[j], ys.at[j], yr.at[j])
                    if self.end:
                        self.recv(back.at[j], rs.at[j], rr.at[j])

                    def body(t, carry):
                        rows = pl.ds(pl.multiple_of(t * TILE, TILE), TILE)
                        total = far[j, rows, :].astype(F32)
                        if self.end:
                            total += back[j, rows, :].astype(F32)
                        if not (self.end and self.layer == 1):
                            total += parts[b, rows, :].astype(F32)
                        if not (self.end and self.layer == 0):
                            total += near[b % 4, rows, :].astype(F32)
                        loc[j, t] = total.astype(BF16)
                        return carry

                    lax.fori_loop(0, 2 * k_rows // TILE, body, 0)
                    for c in range(CAP):
                        snd[j, c] = loc[j, pick_left[c]]
                        snd[j, CAP + c] = loc[j, pick_right[c]]

                self.start(self.left_copy, b)
                self.start(self.right_copy, b)

            each(names, block)

        def place(self):
            for j in range(2):
                self.recv(inc.at[j, pl.ds(CAP, CAP)], hs.at[j, 0], hr.at[j, 0])
                self.recv(inc.at[j, pl.ds(0, CAP)], hs.at[j, 1], hr.at[j, 1])
            for j in range(2):
                for t in range(tiles):
                    i = take[t]
                    kept = loc[j, jnp.minimum(i, tiles - 1)]
                    came = inc[j, jnp.clip(i - tiles, 0, 2 * CAP - 1)]
                    out_ref[t * TILE : (t + 1) * TILE, j * BLOCK : (j + 1) * BLOCK] = jnp.where(
                        i < tiles, kept, came
                    )

    for c in table_loads:
        c.wait()

    tiles = 2 * k_rows // TILE

    per = tiles // 2

    def globals_of(source):
        return [own[t % per, source * 2 + t // per] for t in range(tiles)]

    def picks(goes, to):
        seen, chosen = jnp.int32(0), [jnp.int32(0)] * CAP
        for t in range(tiles):
            hit = (goes[t] >= to * tiles) & (goes[t] < (to + 1) * tiles)
            chosen = [jnp.where(hit & (seen == c), t, chosen[c]) for c in range(CAP)]
            seen = seen + hit.astype(jnp.int32)
        return chosen

    left_of, right_of = (me + devices - 1) % devices, (me + 1) % devices
    mine_goes = globals_of(me)
    pick_left, pick_right = picks(mine_goes, left_of), picks(mine_goes, right_of)
    take = [jnp.int32(0)] * tiles
    for source, base in ((me, 0), (left_of, tiles), (right_of, tiles + CAP)):
        goes = mine_goes if base == 0 else globals_of(source)
        seen = jnp.int32(0)
        for t in range(tiles):
            slot = goes[t] - me * tiles
            hit = (slot >= 0) & (slot < tiles)
            value = t if base == 0 else base + seen
            take = [jnp.where(slot == s, value, take[s]) for s in range(tiles)]
            seen = seen + hit.astype(jnp.int32)

    def mid_upper():
        r = Role(False, 1)
        r.A(0)
        r.Be(0)
        r.C(0)
        r.A(1)
        r.Df(0)
        r.Bp(0)
        r.xrecv(0,"m")
        r.xrecv(0,"n")
        r.out_blocks(["m", "e", "n", "f", "pm", "pe", "pn"])
        r.Be(1)
        r.C(1)
        r.Dp(0)
        pl.semaphore_signal(gate, inc=1, device_id=core, device_id_type=mesh_id)
        r.xrecv(0,"f")
        r.out_blocks(["pf"])
        for c in in_loads:
            c.wait()
        r.attend()
        r.Df(1)
        r.Bp(1)
        r.A(2)
        r.Be(2)
        r.query_blocks(["m", "e", "n"])
        r.xrecv(1,"m")
        r.query_blocks(["f", "pm", "pe"])
        r.xrecv(1,"n")
        r.query_blocks(["pn"])
        r.Dp(1)
        r.xrecv(1,"f")
        r.query_blocks(["pf"])
        r.section_blocks(["m", "e", "n"])
        r.C(2)
        r.section_blocks(["f", "pm", "pe"])
        r.section_blocks(["pn"])
        r.section_blocks(["pf"])
        r.Bp(2)
        r.Df(2)
        r.A(3)
        r.Be(3)
        r.Dp(2)
        r.C(3)
        r.Df(3)
        r.encode(["m", "e", "n", "f"])
        r.Bp(3)
        r.xrecv(2,"m")
        r.xrecv(3,"m")
        r.encode(["pm", "pe"])
        r.recv(kg_in, ks.at[0], kr.at[0])
        r.recv(vg_in, ks.at[1], kr.at[1])
        r.encode_lent(["m", "e", "n", "f"])
        r.Dp(3)
        r.encode_lent(["pm", "pe"])
        r.xrecv(2,"n")
        r.xrecv(3,"n")
        r.xrecv(2,"f")
        r.xrecv(3,"f")
        r.encode(["pn", "pf"])
        r.encode_lent(["pn", "pf"])
        r.give_back(["m", "e", "n", "f"])
        r.give_back(["pm", "pe"])
        r.reduce_cores(["m", "e", "n", "f"])
        r.give_back(["pn", "pf"])
        r.reduce_cores(["pm", "pe"])
        r.reduce_cores(["pn", "pf"])
        r.reduce_heads(["m", "e", "n", "f"])
        r.reduce_heads(["pm", "pe"])
        r.reduce_heads(["pn", "pf"])
        r.place()
        r.finish()

    def mid_lower():
        r = Role(False, 0)
        pl.semaphore_wait(gate, 1)
        r.A(0)
        r.A(1)
        r.C(0)
        r.Be(0)
        r.C(1)
        r.Be(1)
        r.out_blocks(["m", "e", "n"])
        r.Bp(0)
        r.Df(0)
        r.xrecv(0,"m")
        r.out_blocks(["f", "pm", "pe"])
        r.xrecv(0,"n")
        r.out_blocks(["pn"])
        r.Df(1)
        r.Bp(1)
        r.Dp(0)
        r.xrecv(0,"f")
        r.out_blocks(["pf"])
        for c in in_loads:
            c.wait()
        r.attend()
        r.Dp(1)
        r.A(2)
        r.xrecv(1,"m")
        r.query_blocks(["m", "e", "n", "f", "pm", "pe"])
        r.xrecv(1,"n")
        r.xrecv(1,"f")
        r.query_blocks(["pn", "pf"])
        r.Be(2)
        r.C(2)
        r.A(3)
        r.Df(2)
        r.section_blocks(["m", "e", "n", "f", "pm", "pe", "pn", "pf"])
        r.Be(3)
        r.C(3)
        r.Bp(2)
        r.Df(3)
        r.encode(["m", "e", "n", "f"])
        r.Dp(2)
        r.Bp(3)
        r.reduce_cores(["m", "e", "n", "f"])
        r.xrecv(2,"m")
        r.xrecv(3,"m")
        r.encode(["pm", "pe"])
        r.Dp(3)
        r.reduce_cores(["pm", "pe"])
        r.xrecv(2,"n")
        r.xrecv(3,"n")
        r.xrecv(2,"f")
        r.xrecv(3,"f")
        r.encode(["pn", "pf"])
        r.reduce_cores(["pn", "pf"])
        r.reduce_heads(["m", "e", "n", "f"])
        r.reduce_heads(["pm", "pe"])
        r.reduce_heads(["pn", "pf"])
        r.place()
        r.finish()

    def end_upper():
        r = Role(True, 1)
        r.A(0)
        r.Bp(0)
        r.A(1)
        r.Cm(0)
        r.C(0)
        r.Bp(1)
        r.Cm(1)
        r.A(2)
        r.A(3)
        r.Df(0)
        pl.semaphore_signal(gate, inc=1, device_id=core, device_id_type=mesh_id)
        r.xrecv(0,"m")
        r.xrecv(0,"n")
        r.out_blocks(["e", "pe", "m", "pm", "n", "pn", "f"])
        r.C(1)
        r.Dp(0)
        r.xrecv(0,"f")
        r.out_blocks(["pf"])
        for c in in_loads:
            c.wait()
        r.attend()
        r.send(kg, kg_in, ks.at[0], kr.at[0], mid_peer)
        r.send(vg, vg_in, ks.at[1], kr.at[1], mid_peer)
        r.xrecv(1,"m")
        r.xrecv(1,"n")
        r.query_blocks(["e", "pe", "m", "pm", "n", "pn"])
        r.Df(1)
        r.Dp(1)
        r.xrecv(1,"f")
        r.query_blocks(["f", "pf"])
        r.section_blocks(["e", "pe", "m", "pm", "n", "pn"])
        r.section_blocks(["f", "pf"])
        r.reduce_cores(["e", "pe", "m"])
        r.reduce_cores(["pm", "n"])
        r.reduce_heads(["pm", "n"])
        r.reduce_heads(["e", "pe", "m"])
        r.reduce_cores(["pn", "f"])
        r.reduce_cores(["pf"])
        r.reduce_heads(["pn", "f"])
        r.reduce_heads(["pf"])
        r.place()
        r.finish()

    def end_lower():
        r = Role(True, 0)
        pl.semaphore_wait(gate, 1)
        r.A(0)
        r.A(1)
        r.Cm(0)
        r.Bp(0)
        r.Cm(1)
        r.Bp(1)
        r.C(0)
        r.C(1)
        r.Df(0)
        r.Df(1)
        r.A(2)
        r.Dp(0)
        r.xrecv(0,"m")
        r.out_blocks(["e", "pe", "m", "pm"])
        r.xrecv(0,"n")
        r.xrecv(0,"f")
        r.out_blocks(["n", "pn", "f", "pf"])
        for c in in_loads:
            c.wait()
        r.attend()
        r.Cm(2)
        r.A(3)
        r.Bp(2)
        r.xrecv(1,"m")
        r.query_blocks(["e", "pe", "m", "pm"])
        r.xrecv(1,"n")
        r.query_blocks(["n", "pn"])
        r.C(2)
        r.xrecv(1,"f")
        r.query_blocks(["f", "pf"])
        r.Cm(3)
        r.Bp(3)
        r.encode(["e", "pe", "m"])
        r.Df(2)
        r.reduce_cores(["e", "pe", "m"])
        r.section_blocks(["e", "pe", "m", "pm", "n", "pn", "f", "pf"])
        r.C(3)
        r.xrecv(2,"m")
        r.xrecv(3,"m")
        r.encode(["pm", "n"])
        r.Df(3)
        r.reduce_cores(["pm", "n"])
        r.xrecv(2,"n")
        r.xrecv(3,"n")
        r.encode(["pn", "f"])
        r.reduce_cores(["pn", "f"])
        r.reduce_heads(["pm", "n"])
        r.xrecv(2,"f")
        r.xrecv(3,"f")
        r.encode(["pf"])
        r.reduce_cores(["pf"])
        r.reduce_heads(["e", "pe", "m"])
        r.reduce_heads(["pn", "f"])
        r.reduce_heads(["pf"])
        r.place()
        r.finish()

    for wanted_end, layer, program in (
        (False, 1, mid_upper), (False, 0, mid_lower), (True, 1, end_upper), (True, 0, end_lower)
    ):
        place_here = at_end if wanted_end else jnp.logical_not(at_end)
        pl.when(place_here & (seg == layer))(program)


def run_chain(tables, top, q, k, v, wo, wq, wk, wv, devices):
    micro = tables[0].shape[0]
    q_rows, k_rows = top.shape[0] // micro, k.shape[1] // micro
    width, depth = top.shape[1], q.shape[2]
    half, blocks = width // 2, width // BLOCK
    keys = micro * k_rows
    tiles = keys // TILE
    vmem, any_ = (pl.BlockSpec(memory_space=m) for m in (pltpu.VMEM, pl.ANY))
    dma = pltpu.SemaphoreType.DMA

    def buf(*shape, dtype=BF16):
        return pltpu.VMEM(shape, dtype)

    sections, owned = pl.pallas_call(
        functools.partial(chain_kernel, (q_rows, k_rows, depth // DH, devices)),
        in_specs=[any_] * 12,
        out_specs=[any_, vmem],
        out_shape=[
            jax.ShapeDtypeStruct((1, micro * q_rows, half), BF16),
            jax.ShapeDtypeStruct((keys, width // 4), BF16),
        ],
        scratch_shapes=[
            buf(4, blocks, depth, BLOCK),
            buf(blocks, micro * q_rows, BLOCK),
            buf(micro * q_rows, depth),
            buf(keys, depth),
            buf(keys, depth),
            buf(micro * q_rows, depth, dtype=F32),
            buf(micro * q_rows, depth),
            buf(keys, depth),
            buf(keys, depth),
            buf(blocks, micro * q_rows, BLOCK),
            buf(blocks, micro * q_rows, BLOCK),
            buf(blocks, keys, BLOCK),
            buf(4, keys, BLOCK),
            buf(2, keys, BLOCK),
            buf(2, keys, BLOCK),
            buf(keys, depth),
            buf(keys, depth),
            buf(blocks, keys, BLOCK),
            buf(4, keys, BLOCK),
            buf(2, keys, BLOCK),
            buf(2, tiles, TILE, BLOCK),
            buf(2, 2 * CAP, TILE, BLOCK),
            buf(2, 2 * CAP, TILE, BLOCK),
        ]
        + [dma((4,)), dma((8,)), dma((3,))]
        + [dma((9, 4))] * 2
        + [dma((4, 4))] * 2
        + [dma((8,))] * 4
        + [dma((2,))] * 2
        + [dma((8,))] * 2
        + [dma((2,))] * 2
        + [dma((4,))] * 2
        + [dma((4,)), dma((2,))]
        + [dma((2, 2))] * 2
        + [dma((4,))]
        + [pltpu.SemaphoreType.REGULAR]
        + [pltpu.SMEM(t.shape, jnp.int32) for t in tables]
        + [dma((4,))],
        compiler_params=pltpu.CompilerParams(
            collective_id=0, has_side_effects=True, vmem_limit_bytes=60 << 20
        ),
    )(*tables, top, q, k, v, wo, wq, wk, wv)
    return pl.pallas_call(
        hand_over_kernel,
        in_specs=[any_] * 2,
        out_specs=[any_] * 2,
        out_shape=[jax.ShapeDtypeStruct(a.shape, a.dtype) for a in (sections, owned)],
        scratch_shapes=[pltpu.VMEM(a.shape, a.dtype) for a in (sections, owned)] + [dma((2, 2, 4))],
    )(sections, owned)


def hand_over_kernel(a_in, b_in, a_out, b_out, a_mid, b_mid, sems):
    inward, outward = [], []
    for i in range(4):
        for n, (src, mid, dst) in enumerate(
            ((a_in.at[0], a_mid.at[0], a_out.at[0]), (b_in, b_mid, b_out))
        ):
            rows = src.shape[0] // 4
            at = pl.ds(i * rows, rows)
            inward.append(pltpu.make_async_copy(src.at[at], mid.at[at], sems.at[0, n, i]))
            outward.append(pltpu.make_async_copy(mid.at[at], dst.at[at], sems.at[1, n, i]))
    for c in inward:
        c.start()
    for c, d in zip(inward, outward):
        c.wait()
        d.start()
    for d in outward:
        d.wait()


def ranked(marked):
    ids = jnp.arange(marked.shape[0], dtype=jnp.int32)
    upto = ids[None, :] <= ids[:, None]
    return jnp.sum((upto & marked[None, :]).astype(jnp.int32), axis=1) - 1


def on_device(
    grad_top,
    saved_query,
    saved_key,
    saved_value,
    w_query,
    w_key,
    w_value,
    w_out,
    query_length,
    key_offset,
    key_length,
    tile_owner,
):
    seg = lax.axis_index("segment")
    mp = lax.axis_index("mp")
    devices = lax.axis_size("dp")
    me = lax.axis_index("dp")
    micro = query_length.shape[0]
    q_rows = grad_top.shape[0] // micro
    k_rows = saved_key.shape[1] // micro
    half = grad_top.shape[1] // 2
    mp_swap = [(0, 1), (1, 0)]
    if w_out.shape[2] == BLOCK and devices == 8 and micro == 2:
        return run_chain(
            (query_length, key_offset, key_length, tile_owner.T), grad_top, saved_query, saved_key,
            saved_value, w_out, w_query, w_key, w_value, devices,
        )

    wo, sources = gathered(w_out[0])
    wq, _ = gathered(w_query[0])
    wk, _ = gathered(w_key[0])
    wv, _ = gathered(w_value[0])
    order = jnp.stack(sources).astype(jnp.int32)

    top = grad_top.reshape(grad_top.shape[0], 2, half).transpose(1, 0, 2)
    scalars = [
        jnp.concatenate([order, query_length[s], key_offset[s], key_length[s]])
        for s in range(micro)
    ]

    def tick(s, grad, at):
        return run_tick(
            scalars[s], grad, at, s, saved_query, saved_key, saved_value, wo, wq, q_rows, k_rows
        )

    upper = [tick(s, top, s) for s in range(micro)]
    upper_half, incoming = [], []
    for s in range(micro):
        mixed = upper[s][0]
        other = lax.ppermute(mixed, "mp", mp_swap)
        rows = top[:, s * q_rows : (s + 1) * q_rows]
        section = (rows.astype(F32) + (mixed.astype(F32) + other.astype(F32))).astype(BF16)
        incoming.append(lax.ppermute(section, "segment", [(1, 0)]))
        upper_half.append(lax.dynamic_index_in_dim(section, mp, 0, keepdims=False))
    lower = [tick(s, incoming[s], 0) for s in range(micro)]
    halves = []
    for s in range(micro):
        mixed = lower[s][0]
        other = lax.ppermute(
            lax.dynamic_index_in_dim(mixed, 1 - mp, 0, keepdims=False), "mp", mp_swap
        )
        own = lax.dynamic_index_in_dim(mixed, mp, 0, keepdims=False)
        base = lax.dynamic_index_in_dim(incoming[s], mp, 0, keepdims=False)
        low = (base.astype(F32) + (own.astype(F32) + other.astype(F32))).astype(BF16)
        halves.append(jnp.where(seg == 1, upper_half[s], low))
    sections = jnp.concatenate(halves, axis=0)[None]

    kg = jnp.concatenate([jnp.where(seg == 1, upper[s][1], lower[s][1]) for s in range(micro)], 0)
    vg = jnp.concatenate([jnp.where(seg == 1, upper[s][2], lower[s][2]) for s in range(micro)], 0)
    parts = run_encoder(order, kg, vg, wk, wv)
    away = lax.dynamic_slice_in_dim(parts, (1 - seg) * 2, 2, 0)
    mine = lax.dynamic_slice_in_dim(parts, seg * 2, 2, 0)
    arrived = lax.ppermute(away, "segment", mp_swap)
    summed = (mine.astype(F32) + arrived.astype(F32)).astype(BF16)
    crossing = lax.ppermute(
        lax.dynamic_index_in_dim(summed, 1 - mp, 0, keepdims=False), "mp", mp_swap
    )
    kept = lax.dynamic_index_in_dim(summed, mp, 0, keepdims=False)
    kept = (kept.astype(F32) + crossing.astype(F32)).astype(BF16)

    tiles = kept.shape[0] // TILE
    features = kept.shape[1]
    owners = tile_owner.reshape(devices, tiles)
    slot_ids = jnp.arange(CAP, dtype=jnp.int32)[:, None]
    tile_ids = jnp.arange(tiles, dtype=jnp.int32)

    def plan(source):
        source = source % devices
        row = lax.dynamic_index_in_dim(owners, source, 0, keepdims=False)
        return (row // tiles - source + devices) % devices, row % tiles

    def ranks_of(marked):
        return (ranked(marked)[None, :] == slot_ids) & marked[None, :]

    step, slot = plan(me)
    left_step, left_slot = plan(me - 1 + devices)
    right_step, right_slot = plan(me + 1)
    send_left = jnp.sum(jnp.where(ranks_of(step == devices - 1), tile_ids[None, :], 0), axis=1)
    send_right = jnp.sum(jnp.where(ranks_of(step == 1), tile_ids[None, :], 0), axis=1)
    left_hit = ranks_of(left_step == 1)
    right_hit = ranks_of(right_step == devices - 1)
    target = jnp.concatenate(
        [
            jnp.sum(jnp.where(left_hit, left_slot[None, :], 0), axis=1),
            slot,
            jnp.sum(jnp.where(right_hit, right_slot[None, :], 0), axis=1),
        ]
    )
    usable = jnp.concatenate([jnp.any(left_hit, axis=1), step == 0, jnp.any(right_hit, axis=1)])
    chosen = (tile_ids[:, None] == target[None, :]) & usable[None, :]
    candidate_ids = jnp.arange(target.shape[0], dtype=jnp.int32)
    take = jnp.sum(jnp.where(chosen, candidate_ids[None, :], 0), axis=1)

    tiled = (tiles, TILE, features)
    shape = jax.ShapeDtypeStruct(tiled, BF16)
    handed = jax.ShapeDtypeStruct((CAP, TILE, features), BF16)
    local = kept.reshape(tiled)
    to_left, to_right = small_call(
        pick_kernel, jnp.concatenate([send_left, send_right]), [local], [handed, handed]
    )
    forward = [(i, (i + 1) % devices) for i in range(devices)]
    backward = [(b, a) for a, b in forward]
    from_left = lax.ppermute(to_right, "dp", forward)
    from_right = lax.ppermute(to_left, "dp", backward)
    owned = small_call(place_kernel, take, [from_left, local, from_right], shape)
    return sections, owned.reshape(tiles * TILE, features)


def solution(mesh):
    in_specs = (
        P("dp", None),
        P("segment", "dp", "mp"),
        P("segment", "dp", "mp"),
        P("segment", "dp", "mp"),
        P("segment", "mp", "dp"),
        P("segment", "mp", "dp"),
        P("segment", "mp", "dp"),
        P("segment", "mp", "dp"),
        P("dp", None),
        P("dp", None),
        P("dp", None),
        P(),
    )
    out_specs = (P("segment", "dp", "mp"), P("dp", ("segment", "mp")))
    return jax.shard_map(
        on_device, mesh=mesh, in_specs=in_specs, out_specs=out_specs, check_vma=False
    )
```

```python
import functools

import jax
import jax.numpy as jnp
from jax import lax
from jax.experimental import pallas as pl
from jax.experimental.pallas import tpu as pltpu
from jax.sharding import PartitionSpec as P

DH = 256
TILE = 128
CAP = 2
BLOCK = 256
masked_floor = -1e30
BF16, F32 = jnp.bfloat16, jnp.float32


def dot(a, b, ca, cb):
    return lax.dot_general(a, b, (((ca,), (cb,)), ((), ())), preferred_element_type=F32)


def tick_kernel(count, half, sc, g_ref, q_ref, k_ref, v_ref, *rest):
    wo, wq = rest[:count], rest[count : 2 * count]
    mixed_ref, kg_ref, vg_ref, acc = rest[2 * count :]
    head = pl.program_id(0)
    per = half // BLOCK
    scale = DH ** (-0.5)

    def place(b):
        src = sc[b]
        return src // per, pl.ds(pl.multiple_of((src % per) * BLOCK, BLOCK), BLOCK)

    og = None
    for b in range(count):
        at, cols = place(b)
        term = dot(g_ref[at, :, cols], wo[b][...], 1, 1)
        og = term if og is None else og + term
    og = og.astype(BF16)
    q, k, v = q_ref[0], k_ref[0], v_ref[0]
    scores = dot(q, k, 1, 1) * scale
    rows = lax.broadcasted_iota(jnp.int32, scores.shape, 0)
    cols_id = lax.broadcasted_iota(jnp.int32, scores.shape, 1)
    allowed = None
    for e in range(2):
        q_len, k_off, k_len = sc[count + e], sc[count + 2 + e] * TILE, sc[count + 4 + e]
        hit = (rows >= e * TILE) & (rows < e * TILE + q_len)
        hit = hit & (cols_id >= k_off) & (cols_id < k_off + k_len)
        allowed = hit if allowed is None else allowed | hit
    masked = jnp.where(allowed, scores, masked_floor)
    top = jnp.max(masked, axis=-1, keepdims=True)
    terms = jnp.where(allowed, jnp.exp(masked - top), 0.0)
    prob = terms / jnp.maximum(jnp.sum(terms, axis=-1, keepdims=True), 1.0)
    prob_bf = prob.astype(BF16)
    attended = dot(prob_bf, v, 1, 0)
    out_dot = jnp.sum(og.astype(F32) * attended, axis=-1, keepdims=True)
    sg = (prob * (dot(og, v, 1, 1) - out_dot)).astype(BF16)
    qg = (dot(sg, k, 1, 0) * scale).astype(BF16)
    kg_ref[...] = (dot(sg, q, 0, 0) * scale).astype(BF16)
    vg_ref[...] = dot(prob_bf, og, 0, 0).astype(BF16)

    @pl.when(head == 0)
    def _():
        acc[...] = jnp.zeros_like(acc)

    for b in range(count):
        at, cols = place(b)
        acc[at, :, cols] += dot(qg, wq[b][...], 1, 0)

    @pl.when(head == pl.num_programs(0) - 1)
    def _():
        mixed_ref[...] = acc[...].astype(BF16)


def run_tick(scalars, grad, at, seq, saved_q, saved_k, saved_v, wo, wq, q_rows, k_rows):
    half = grad.shape[2]
    heads = saved_q.shape[2] // DH
    count = len(wo)
    weight = pl.BlockSpec((DH, BLOCK), lambda h, sc: (h, 0))
    macs = heads * q_rows * DH * (4 * half + 6 * k_rows)
    return pl.pallas_call(
        functools.partial(tick_kernel, count, half),
        grid_spec=pltpu.PrefetchScalarGridSpec(
            num_scalar_prefetch=1,
            grid=(heads,),
            in_specs=[
                pl.BlockSpec((2, q_rows, half), lambda h, sc: (0, at, 0)),
                pl.BlockSpec((1, q_rows, DH), lambda h, sc: (0, seq, h)),
                pl.BlockSpec((1, k_rows, DH), lambda h, sc: (0, seq, h)),
                pl.BlockSpec((1, k_rows, DH), lambda h, sc: (0, seq, h)),
            ]
            + [weight] * (2 * count),
            out_specs=[
                pl.BlockSpec((2, q_rows, half), lambda h, sc: (0, 0, 0)),
                pl.BlockSpec((k_rows, DH), lambda h, sc: (0, h)),
                pl.BlockSpec((k_rows, DH), lambda h, sc: (0, h)),
            ],
            scratch_shapes=[pltpu.VMEM((2, q_rows, half), F32)],
        ),
        out_shape=[
            jax.ShapeDtypeStruct((2, q_rows, half), BF16),
            jax.ShapeDtypeStruct((k_rows, heads * DH), BF16),
            jax.ShapeDtypeStruct((k_rows, heads * DH), BF16),
        ],
        compiler_params=pltpu.CompilerParams(vmem_limit_bytes=40 << 20),
        cost_estimate=pl.CostEstimate(
            flops=2 * macs, bytes_accessed=16 << 20, transcendentals=heads * q_rows * k_rows
        ),
    )(scalars, grad, saved_q, saved_k, saved_v, *wo, *wq)


def encoder_kernel(count, quarter, sc, kg_ref, vg_ref, *rest):
    wk, wv, out_ref = rest[:count], rest[count : 2 * count], rest[2 * count]
    per = quarter // BLOCK
    kg, vg = kg_ref[...], vg_ref[...]
    for b in range(count):
        src = sc[b]
        cols = pl.ds(pl.multiple_of((src % per) * BLOCK, BLOCK), BLOCK)
        part = dot(kg, wk[b][...], 1, 0) + dot(vg, wv[b][...], 1, 0)
        out_ref[src // per, :, cols] = part.astype(BF16)


def run_encoder(scalars, kg, vg, wk, wv):
    count = len(wk)
    rows, depth = kg.shape
    quarter = count * BLOCK // 4
    step = 256
    whole = pl.BlockSpec((depth, BLOCK), lambda i, sc: (0, 0))
    return pl.pallas_call(
        functools.partial(encoder_kernel, count, quarter),
        grid_spec=pltpu.PrefetchScalarGridSpec(
            num_scalar_prefetch=1,
            grid=(rows // step,),
            in_specs=[pl.BlockSpec((step, depth), lambda i, sc: (i, 0))] * 2
            + [whole] * (2 * count),
            out_specs=pl.BlockSpec((4, step, quarter), lambda i, sc: (0, i, 0)),
        ),
        out_shape=jax.ShapeDtypeStruct((4, rows, quarter), BF16),
        compiler_params=pltpu.CompilerParams(vmem_limit_bytes=48 << 20),
        cost_estimate=pl.CostEstimate(
            flops=16 * rows * depth * quarter, bytes_accessed=14 << 20, transcendentals=0
        ),
    )(scalars, kg, vg, *wk, *wv)


def pick_kernel(sc, local_ref, left_ref, right_ref):
    for c in range(CAP):
        left_ref[c] = local_ref[sc[c]]
        right_ref[c] = local_ref[sc[CAP + c]]


def place_kernel(sc, left_ref, local_ref, right_ref, out_ref):
    tiles = local_ref.shape[0]
    for s in range(tiles):
        i = sc[s]

        @pl.when(i < CAP)
        def _():
            out_ref[s] = left_ref[jnp.minimum(i, CAP - 1)]

        @pl.when((i >= CAP) & (i < CAP + tiles))
        def _():
            out_ref[s] = local_ref[jnp.clip(i - CAP, 0, tiles - 1)]

        @pl.when(i >= CAP + tiles)
        def _():
            out_ref[s] = right_ref[jnp.clip(i - CAP - tiles, 0, CAP - 1)]


def small_call(body, scalars, arrays, outs):
    vmem = pl.BlockSpec(memory_space=pltpu.VMEM)
    single = not isinstance(outs, list)
    return pl.pallas_call(
        body,
        in_specs=[pl.BlockSpec(memory_space=pltpu.SMEM)] + [vmem] * len(arrays),
        out_specs=vmem if single else [vmem] * len(outs),
        out_shape=outs,
        compiler_params=pltpu.CompilerParams(vmem_limit_bytes=24 << 20),
    )(scalars, *arrays)


def gathered(shard):
    full = lax.all_gather(shard, "dp", axis=1, tiled=True)
    blocks = [full[:, i : i + BLOCK] for i in range(0, full.shape[1], BLOCK)]
    return blocks, list(jnp.arange(len(blocks), dtype=jnp.int32))


def chain_kernel(dims, ql_hbm, ko_hbm, kl_hbm, own_hbm, top_hbm, q_hbm, k_hbm, v_hbm, wo_hbm, wq_hbm, wk_hbm, wv_hbm,
                 sections_hbm, out_ref,
                 wbuf, g, q_ref, k_ref, v_ref, acc, qg, kg, vg, mixed, other, parts, near, fwd, far,
                 kg_in, vg_in, lent, lent_in, back, loc, inc, snd,
                 ldw, ldg, ldq, zs, zr, xs, xr, ms, mr, gs, gr, ks, kr, ps, pr, ys, yr,
                 us, ur, rs, rr, hs, hr, so, gate,
                 q_len_of, k_off_of, k_len_of, own, ldt):
    q_rows, k_rows, heads, devices = dims
    depth = heads * DH
    scale = DH ** (-0.5)
    seg, me, mp = lax.axis_index("segment"), lax.axis_index("dp"), lax.axis_index("mp")
    z, x = me // 2, me % 2
    side = z // 2
    mesh_id = pl.DeviceIdType.MESH
    plane = {"e": 3 * side, "m": 1 + side, "n": 2 - side, "f": 3 - 3 * side}
    blk = {c: plane[c] * 2 + x for c in plane}
    blk.update({"p" + c: plane[c] * 2 + 1 - x for c in plane})
    at_end = (z == 0) | (z == 3)
    side_peer, cross, core = (seg, z * 2 + 1 - x, mp), (seg, me, 1 - mp), (1 - seg, me, mp)
    diag = jnp.where(x == 0, (me + devices - 1) % devices, (me + 1) % devices)
    end_peer, mid_peer = (seg, plane["e"] * 2 + x, mp), (seg, plane["m"] * 2 + x, mp)
    far_mid = (seg, plane["n"] * 2 + x, mp)
    upper, lower = pl.ds(0, depth // 2), pl.ds(depth // 2, depth // 2)
    whole = pl.ds(0, depth)
    step = 256

    def load(src, dst, sem):
        return pltpu.make_async_copy(src, dst, sem)

    weights = (wo_hbm, wq_hbm, wk_hbm, wv_hbm)
    w_loads = [load(weights[u].at[0], wbuf.at[u, me], ldw.at[u]) for u in range(4)]
    in_loads = [load(a.at[0], b, ldq.at[i])
                for i, (a, b) in enumerate(((q_hbm, q_ref), (k_hbm, k_ref), (v_hbm, v_ref)))]

    def g_load(b):
        cols = pl.ds(pl.multiple_of(b * BLOCK, BLOCK), BLOCK)
        return load(top_hbm.at[:, cols], g.at[b], ldg.at[b])

    tables = ((ql_hbm, q_len_of), (ko_hbm, k_off_of), (kl_hbm, k_len_of), (own_hbm, own))
    table_loads = [load(a, b, ldt.at[i]) for i, (a, b) in enumerate(tables)]
    w_loads[0].start()

    barrier = pltpu.get_barrier_semaphore()

    def greet(peers):
        for peer in peers:
            pl.semaphore_signal(barrier, inc=1, device_id=peer, device_id_type=mesh_id)

    all_peers = [side_peer, cross, core, (seg, diag, mp)]
    greet(all_peers)

    @pl.when(at_end)
    def _():
        greet([mid_peer])

        @pl.when(seg == 0)
        def _():
            greet([(1, plane["m"] * 2 + x, mp)])

    @pl.when(jnp.logical_not(at_end))
    def _():
        greet([end_peer, far_mid])

        @pl.when(seg == 1)
        def _():
            greet([(0, plane["e"] * 2 + x, mp)])

    @pl.when(seg == 1)
    def _():
        for b in range(8):
            g_load(b).start()

    for c in w_loads[1:] + in_loads + table_loads:
        c.start()
    for c in w_loads:
        c.wait()

    pl.semaphore_wait(barrier, jnp.where(at_end, 6 - seg, 6 + seg))

    def loop(rows, body):
        def one(i, carry):
            body(pl.ds(pl.multiple_of(i * step, step), step))
            return carry

        lax.fori_loop(0, rows // step, one, 0)

    def each(names, body):
        ids = [blk[n] for n in names]

        def one(i, carry):
            b = ids[0]
            for j in range(1, len(ids)):
                b = jnp.where(i == j, ids[j], b)
            body(b)
            return carry

        if len(ids) == 1:
            body(ids[0])
        else:
            lax.fori_loop(0, len(ids), one, 0)

    class Role:
        def __init__(self, end, layer):
            self.end, self.layer = end, layer
            self.pending = []
            self.started = False
            upper_end = end and layer == 1
            self.makers = [self.mixed_copy, self.far_copy, self.left_copy, self.right_copy]
            if layer == 1:
                self.makers.append(self.section_copy)
            if not upper_end:
                self.makers.append(self.part_copy)
            if layer == 1 and not end:
                self.makers += [self.lent_copy, self.back_copy]


        def send(self, src, dst, a, b, peer, cond=None):
            copy = pltpu.make_async_remote_copy(
                src_ref=src, dst_ref=dst, send_sem=a, recv_sem=b, device_id=peer, device_id_type=mesh_id
            )
            self.pending.append((cond, copy))
            if cond is None:
                copy.start()
            else:
                pl.when(cond)(copy.start)

        def recv(self, dst, a, b):
            pltpu.make_async_remote_copy(
                src_ref=dst, dst_ref=dst, send_sem=a, recv_sem=b, device_id=side_peer,
                device_id_type=mesh_id,
            ).wait_recv()

        def remote(self, src, dst, a, b, peer):
            return pltpu.make_async_remote_copy(
                src_ref=src, dst_ref=dst, send_sem=a, recv_sem=b, device_id=peer, device_id_type=mesh_id
            )

        def finish(self):
            for _, copy in self.pending:
                copy.wait_send()

            def one(b, carry):
                for make in self.makers:
                    copy, cond = make(b)
                    if cond is None:
                        copy.wait_send()
                    else:
                        pl.when(cond)(copy.wait_send)
                return carry

            lax.fori_loop(0, 8, one, 0)
            for i in range(4):
                self.output_copy(4 * mp + i).wait()

        def start(self, make, b):
            copy, cond = make(b)
            if cond is None:
                copy.start()
            else:
                pl.when(cond)(copy.start)

        def w(self, u, name, rows=whole):
            return wbuf.at[u, blk[name], rows]

        def zsend(self, kind, u, name, peer, rows=whole):
            ref = self.w(u, name, rows)
            self.send(ref, ref, zs.at[kind, u], zr.at[kind, u], peer)

        def zrecv(self, kind, u, name, rows=whole):
            self.recv(self.w(u, name, rows), zs.at[kind, u], zr.at[kind, u])

        def lent_unit(self, u):
            return self.layer == 1 and u >= 2

        def twice(self, u):
            return u < (2 if self.layer == 1 else 1)

        def x_rows(self, u, name):
            if name != "f":
                return whole
            return lower if not self.end or self.twice(u) else whole

        def xsend(self, u, name):
            ref = self.w(u, name, self.x_rows(u, name))
            i = "emnf".index(name)
            self.send(ref, ref, xs.at[i, u], xr.at[i, u], side_peer)

        def xrecv(self, u, name):
            i = "emnf".index(name)
            self.recv(self.w(u, "p" + name, self.x_rows(u, name)), xs.at[i, u], xr.at[i, u])

        def A(self, u):
            if self.end:
                self.zsend(0, u, "e", mid_peer)
                if not self.lent_unit(u):
                    self.xsend(u, "e")
            else:
                if not self.lent_unit(u):
                    self.zsend(2, u, "m", end_peer)
                self.zsend(6, u, "m", far_mid)
                self.xsend(u, "m")

        def Be(self, u):
            self.zrecv(0, u, "e")
            self.zsend(7, u, "e", far_mid)
            if self.lent_unit(u):
                self.xsend(u, "e")

        def Bp(self, u):
            if self.end:
                self.xrecv(u, "e")
                self.zsend(1, u, "pe", mid_peer)
            else:
                if self.lent_unit(u):
                    self.xrecv(u, "e")
                else:
                    self.zrecv(1, u, "pe")
                self.zsend(8, u, "pe", far_mid, upper)

        def Cm(self, u):
            self.zrecv(2, u, "m")
            self.xsend(u, "m")

        def C(self, u):
            if self.end:
                self.zrecv(3, u, "n")
                self.xsend(u, "n")
            else:
                self.zrecv(6, u, "n")
                if not self.lent_unit(u):
                    self.zsend(3, u, "n", end_peer)
                self.xsend(u, "n")

        def Df(self, u):
            if self.end:
                self.zrecv(4, u, "f")
            else:
                self.zrecv(7, u, "f")
                if not self.lent_unit(u):
                    self.zsend(4, u, "f", end_peer)
            self.xsend(u, "f")

        def Dp(self, u):
            if self.end:
                self.zrecv(5, u, "pf", upper)
            else:
                self.zrecv(8, u, "pf", upper)
                if self.twice(u):
                    self.zsend(5, u, "pf", end_peer, upper)


        def mixed_copy(self, b):
            return (self.remote(mixed.at[b], other.at[b], ms.at[b], mr.at[b], cross),
                    None if self.layer == 1 else b // 4 != mp)

        def section_copy(self, b):
            return self.remote(g.at[b], g.at[b], gs.at[b], gr.at[b], core), None

        def part_copy(self, b):
            return (self.remote(parts.at[b], near.at[b % 4], ps.at[b], pr.at[b], core),
                    b // 4 != self.layer)

        def lent_copy(self, b):
            i = (b // 4) * 2 + b % 2
            return (self.remote(lent.at[b], lent_in.at[i], us.at[i], ur.at[i], cross),
                    (b // 2) % 2 != mp)

        def back_copy(self, b):
            i, j = (b // 4) * 2 + b % 2, b % 2
            return (self.remote(lent.at[b], back.at[j], rs.at[i], rr.at[j],
                                (b // 4, plane["e"] * 2 + x, mp)), (b // 2) % 2 == mp)

        def onward(self, b):
            return (b // 4 == self.layer) & ((b // 2) % 2 != mp)

        def mine(self, b):
            return (b // 4 == self.layer) & ((b // 2) % 2 == mp)

        def far_copy(self, b):
            j = b % 2
            if self.end:
                src = parts.at[b] if self.layer == 0 else near.at[b % 4]
            else:
                src = fwd.at[j]
            return self.remote(src, far.at[j], ys.at[j], yr.at[j], cross), self.onward(b)

        def left_copy(self, b):
            j = b % 2
            return (self.remote(snd.at[j, pl.ds(0, CAP)], inc.at[j, pl.ds(CAP, CAP)], hs.at[j, 0],
                                hr.at[j, 0], (seg, (me + devices - 1) % devices, mp)), self.mine(b))

        def right_copy(self, b):
            j = b % 2
            return (self.remote(snd.at[j, pl.ds(CAP, CAP)], inc.at[j, pl.ds(0, CAP)], hs.at[j, 1],
                                hr.at[j, 1], (seg, (me + 1) % devices, mp)), self.mine(b))

        def output_copy(self, b):
            cols = pl.ds(pl.multiple_of((b % 4) * BLOCK, BLOCK), BLOCK)
            src = g.at[b] if self.layer == 1 else mixed.at[b]
            return load(src, sections_hbm.at[0, :, cols], so.at[b % 4])


        def out_blocks(self, names):
            if not self.started:
                acc[...] = jnp.zeros_like(acc)
            self.started = True

            def block(b):
                if self.layer == 1:
                    g_load(b).wait()
                else:
                    self.recv(g.at[b], gs.at[b], gr.at[b])

                def body(rows):
                    acc[rows, :] += dot(g[b, rows, :], wbuf[0, b], 1, 1)

                loop(2 * q_rows, body)

            each(names, block)

        def attend(self):
            rows = lax.broadcasted_iota(jnp.int32, (k_rows, q_rows), 1)
            cols = lax.broadcasted_iota(jnp.int32, (k_rows, q_rows), 0)

            def one_sequence(s, carry):
                qr = pl.ds(pl.multiple_of(s * q_rows, q_rows), q_rows)
                kr_ = pl.ds(pl.multiple_of(s * k_rows, k_rows), k_rows)
                allowed = None
                for e in range(2):
                    q_len, k_off, k_len = q_len_of[s, e], k_off_of[s, e] * TILE, k_len_of[s, e]
                    hit = (rows >= e * TILE) & (rows < e * TILE + q_len)
                    hit = hit & (cols >= k_off) & (cols < k_off + k_len)
                    allowed = hit if allowed is None else allowed | hit

                def one_head(h, carry):
                    hd = pl.ds(pl.multiple_of(h * DH, DH), DH)
                    og = acc[qr, hd].astype(BF16)
                    q, k, v = q_ref[qr, hd], k_ref[kr_, hd], v_ref[kr_, hd]
                    masked = jnp.where(allowed, dot(k, q, 1, 1) * scale, masked_floor)
                    change = dot(v, og, 1, 1)
                    peak = jnp.maximum(jnp.max(masked, axis=0, keepdims=True), masked_floor / 2)
                    terms = jnp.exp(masked - peak)
                    prob = terms * (1.0 / jnp.maximum(jnp.sum(terms, axis=0, keepdims=True), 1.0))
                    prob_bf = prob.astype(BF16)
                    out_dot = jnp.sum(prob_bf.astype(F32) * change, axis=0, keepdims=True)
                    sg = (prob * (change - out_dot)).astype(BF16)
                    vg[kr_, hd] = dot(prob_bf, og, 1, 0).astype(BF16)
                    kg[kr_, hd] = (dot(sg, q, 1, 0) * scale).astype(BF16)
                    qg[qr, hd] = (dot(sg, k, 0, 0) * scale).astype(BF16)
                    return carry

                return lax.fori_loop(0, heads, one_head, carry)

            lax.fori_loop(0, 2, one_sequence, 0)

        def query_blocks(self, names):
            def block(b):
                def body(rows):
                    mixed[b, rows, :] = dot(qg[rows, :], wbuf[1, b], 1, 0).astype(BF16)

                loop(2 * q_rows, body)
                self.start(self.mixed_copy, b)

            each(names, block)

        def section_blocks(self, names):
            def total(b, rows):
                change = mixed[b, rows, :].astype(F32) + other[b, rows, :].astype(F32)
                return (g[b, rows, :].astype(F32) + change).astype(BF16)

            def block(b):
                if self.layer == 1:
                    self.recv(other.at[b], ms.at[b], mr.at[b])

                    def body(rows):
                        g[b, rows, :] = total(b, rows)

                    loop(2 * q_rows, body)
                    self.start(self.section_copy, b)
                else:

                    @pl.when(b // 4 == mp)
                    def _():
                        self.recv(other.at[b], ms.at[b], mr.at[b])

                        def body(rows):
                            mixed[b, rows, :] = total(b, rows)

                        loop(2 * q_rows, body)

                @pl.when(b // 4 == mp)
                def _():
                    self.output_copy(b).start()

            each(names, block)

        def project(self, kref, vref, dst, b):
            def body(rows):
                part = dot(kref[rows, :], wbuf[2, b], 1, 0) + dot(vref[rows, :], wbuf[3, b], 1, 0)
                dst[b, rows, :] = part.astype(BF16)

            loop(2 * k_rows, body)

        def encode(self, names):
            def block(b):
                self.project(kg, vg, parts, b)
                self.start(self.part_copy, b)

            each(names, block)

        def encode_lent(self, names):
            def block(b):
                self.project(kg_in, vg_in, lent, b)
                self.start(self.lent_copy, b)

            each(names, block)

        def give_back(self, names):
            def block(b):
                i = (b // 4) * 2 + b % 2

                @pl.when((b // 2) % 2 == mp)
                def _():
                    self.recv(lent_in.at[i], us.at[i], ur.at[i])

                    def body(rows):
                        both = lent[b, rows, :].astype(F32) + lent_in[i, rows, :].astype(F32)
                        lent[b, rows, :] = both.astype(BF16)

                    loop(2 * k_rows, body)

                self.start(self.back_copy, b)

            each(names, block)

        def reduce_cores(self, names):
            def block(b):
                if not (self.end and self.layer == 0):

                    @pl.when(b // 4 == self.layer)
                    def _():
                        self.recv(near.at[b % 4], ps.at[b], pr.at[b])

                if not self.end:

                    @pl.when(self.onward(b))
                    def _():
                        def body(rows):
                            both = parts[b, rows, :].astype(F32) + near[b % 4, rows, :].astype(F32)
                            fwd[b % 2, rows, :] = both.astype(BF16)

                        loop(2 * k_rows, body)

                self.start(self.far_copy, b)

            each(names, block)

        def reduce_heads(self, names):
            def block(b):
                j = b % 2

                @pl.when(self.mine(b))
                def _():
                    self.recv(far.at[j], ys.at[j], yr.at[j])
                    if self.end:
                        self.recv(back.at[j], rs.at[j], rr.at[j])

                    def body(t, carry):
                        rows = pl.ds(pl.multiple_of(t * TILE, TILE), TILE)
                        total = far[j, rows, :].astype(F32)
                        if self.end:
                            total += back[j, rows, :].astype(F32)
                        if not (self.end and self.layer == 1):
                            total += parts[b, rows, :].astype(F32)
                        if not (self.end and self.layer == 0):
                            total += near[b % 4, rows, :].astype(F32)
                        loc[j, t] = total.astype(BF16)
                        return carry

                    lax.fori_loop(0, 2 * k_rows // TILE, body, 0)
                    for c in range(CAP):
                        snd[j, c] = loc[j, pick_left[c]]
                        snd[j, CAP + c] = loc[j, pick_right[c]]

                self.start(self.left_copy, b)
                self.start(self.right_copy, b)

            each(names, block)

        def place(self):
            for j in range(2):
                self.recv(inc.at[j, pl.ds(CAP, CAP)], hs.at[j, 0], hr.at[j, 0])
                self.recv(inc.at[j, pl.ds(0, CAP)], hs.at[j, 1], hr.at[j, 1])
            for j in range(2):
                for t in range(tiles):
                    i = take[t]
                    kept = loc[j, jnp.minimum(i, tiles - 1)]
                    came = inc[j, jnp.clip(i - tiles, 0, 2 * CAP - 1)]
                    out_ref[t * TILE : (t + 1) * TILE, j * BLOCK : (j + 1) * BLOCK] = jnp.where(
                        i < tiles, kept, came
                    )

    for c in table_loads:
        c.wait()

    tiles = 2 * k_rows // TILE

    per = tiles // 2

    def globals_of(source):
        return [own[t % per, source * 2 + t // per] for t in range(tiles)]

    def picks(goes, to):
        seen, chosen = jnp.int32(0), [jnp.int32(0)] * CAP
        for t in range(tiles):
            hit = (goes[t] >= to * tiles) & (goes[t] < (to + 1) * tiles)
            chosen = [jnp.where(hit & (seen == c), t, chosen[c]) for c in range(CAP)]
            seen = seen + hit.astype(jnp.int32)
        return chosen

    left_of, right_of = (me + devices - 1) % devices, (me + 1) % devices
    mine_goes = globals_of(me)
    pick_left, pick_right = picks(mine_goes, left_of), picks(mine_goes, right_of)
    take = [jnp.int32(0)] * tiles
    for source, base in ((me, 0), (left_of, tiles), (right_of, tiles + CAP)):
        goes = mine_goes if base == 0 else globals_of(source)
        seen = jnp.int32(0)
        for t in range(tiles):
            slot = goes[t] - me * tiles
            hit = (slot >= 0) & (slot < tiles)
            value = t if base == 0 else base + seen
            take = [jnp.where(slot == s, value, take[s]) for s in range(tiles)]
            seen = seen + hit.astype(jnp.int32)

    def mid_upper():
        r = Role(False, 1)
        r.A(0)
        r.Be(0)
        r.C(0)
        r.A(1)
        r.Df(0)
        r.Bp(0)
        r.xrecv(0,"m")
        r.xrecv(0,"n")
        r.out_blocks(["m", "e", "n", "f", "pm", "pe", "pn"])
        r.Be(1)
        r.C(1)
        r.Dp(0)
        pl.semaphore_signal(gate, inc=1, device_id=core, device_id_type=mesh_id)
        r.xrecv(0,"f")
        r.out_blocks(["pf"])
        for c in in_loads:
            c.wait()
        r.attend()
        r.Df(1)
        r.Bp(1)
        r.A(2)
        r.Be(2)
        r.query_blocks(["m", "e", "n"])
        r.xrecv(1,"m")
        r.query_blocks(["f", "pm", "pe"])
        r.xrecv(1,"n")
        r.query_blocks(["pn"])
        r.Dp(1)
        r.xrecv(1,"f")
        r.query_blocks(["pf"])
        r.section_blocks(["m", "e", "n"])
        r.C(2)
        r.section_blocks(["f", "pm", "pe"])
        r.section_blocks(["pn"])
        r.section_blocks(["pf"])
        r.Bp(2)
        r.Df(2)
        r.A(3)
        r.Be(3)
        r.Dp(2)
        r.C(3)
        r.Df(3)
        r.encode(["m", "e", "n", "f"])
        r.Bp(3)
        r.xrecv(2,"m")
        r.xrecv(3,"m")
        r.encode(["pm", "pe"])
        r.recv(kg_in, ks.at[0], kr.at[0])
        r.recv(vg_in, ks.at[1], kr.at[1])
        r.encode_lent(["m", "e", "n", "f"])
        r.Dp(3)
        r.encode_lent(["pm", "pe"])
        r.xrecv(2,"n")
        r.xrecv(3,"n")
        r.xrecv(2,"f")
        r.xrecv(3,"f")
        r.encode(["pn", "pf"])
        r.encode_lent(["pn", "pf"])
        r.give_back(["m", "e", "n", "f"])
        r.give_back(["pm", "pe"])
        r.reduce_cores(["m", "e", "n", "f"])
        r.give_back(["pn", "pf"])
        r.reduce_cores(["pm", "pe"])
        r.reduce_cores(["pn", "pf"])
        r.reduce_heads(["m", "e", "n", "f"])
        r.reduce_heads(["pm", "pe"])
        r.reduce_heads(["pn", "pf"])
        r.place()
        r.finish()

    def mid_lower():
        r = Role(False, 0)
        pl.semaphore_wait(gate, 1)
        r.A(0)
        r.A(1)
        r.C(0)
        r.Be(0)
        r.C(1)
        r.Be(1)
        r.Bp(0)
        r.Df(0)
        r.xrecv(0,"m")
        r.xrecv(0,"n")
        r.out_blocks(["m", "e", "n", "f", "pm", "pe", "pn"])
        r.Df(1)
        r.Bp(1)
        r.Dp(0)
        r.xrecv(0,"f")
        r.out_blocks(["pf"])
        for c in in_loads:
            c.wait()
        r.attend()
        r.Dp(1)
        r.A(2)
        r.query_blocks(["m", "e", "n"])
        r.xrecv(1,"m")
        r.query_blocks(["f", "pm", "pe"])
        r.xrecv(1,"n")
        r.xrecv(1,"f")
        r.query_blocks(["pn", "pf"])
        r.Be(2)
        r.C(2)
        r.A(3)
        r.section_blocks(["m", "e", "n", "f", "pm", "pe", "pn", "pf"])
        r.Df(2)
        r.Be(3)
        r.C(3)
        r.Bp(2)
        r.Df(3)
        r.encode(["m", "e", "n", "f"])
        r.Dp(2)
        r.Bp(3)
        r.reduce_cores(["m", "e", "n", "f"])
        r.xrecv(2,"m")
        r.xrecv(3,"m")
        r.encode(["pm", "pe"])
        r.Dp(3)
        r.reduce_cores(["pm", "pe"])
        r.xrecv(2,"n")
        r.xrecv(3,"n")
        r.xrecv(2,"f")
        r.xrecv(3,"f")
        r.encode(["pn", "pf"])
        r.reduce_cores(["pn", "pf"])
        r.reduce_heads(["m", "e", "n", "f"])
        r.reduce_heads(["pm", "pe"])
        r.reduce_heads(["pn", "pf"])
        r.place()
        r.finish()

    def end_upper():
        r = Role(True, 1)
        r.A(0)
        r.Bp(0)
        r.A(1)
        r.Cm(0)
        r.C(0)
        r.Bp(1)
        r.Cm(1)
        r.A(2)
        r.A(3)
        r.Df(0)
        pl.semaphore_signal(gate, inc=1, device_id=core, device_id_type=mesh_id)
        r.xrecv(0,"m")
        r.xrecv(0,"n")
        r.out_blocks(["e", "pe", "m", "pm", "n", "pn", "f"])
        r.C(1)
        r.Dp(0)
        r.xrecv(0,"f")
        r.out_blocks(["pf"])
        for c in in_loads:
            c.wait()
        r.attend()
        r.send(kg, kg_in, ks.at[0], kr.at[0], mid_peer)
        r.send(vg, vg_in, ks.at[1], kr.at[1], mid_peer)
        r.xrecv(1,"m")
        r.xrecv(1,"n")
        r.query_blocks(["e", "pe", "m", "pm", "n", "pn"])
        r.Df(1)
        r.Dp(1)
        r.xrecv(1,"f")
        r.query_blocks(["f", "pf"])
        r.section_blocks(["e", "pe", "m", "pm", "n", "pn"])
        r.section_blocks(["f", "pf"])
        r.reduce_cores(["e", "pe", "m"])
        r.reduce_cores(["pm", "n"])
        r.reduce_heads(["pm", "n"])
        r.reduce_heads(["e", "pe", "m"])
        r.reduce_cores(["pn", "f"])
        r.reduce_cores(["pf"])
        r.reduce_heads(["pn", "f"])
        r.reduce_heads(["pf"])
        r.place()
        r.finish()

    def end_lower():
        r = Role(True, 0)
        pl.semaphore_wait(gate, 1)
        r.A(0)
        r.A(1)
        r.Cm(0)
        r.Bp(0)
        r.Cm(1)
        r.Bp(1)
        r.C(0)
        r.C(1)
        r.Df(0)
        r.Df(1)
        r.A(2)
        r.Dp(0)
        r.xrecv(0,"m")
        r.out_blocks(["e", "pe", "m", "pm"])
        r.xrecv(0,"n")
        r.xrecv(0,"f")
        r.out_blocks(["n", "pn", "f", "pf"])
        for c in in_loads:
            c.wait()
        r.attend()
        r.Cm(2)
        r.A(3)
        r.Bp(2)
        r.xrecv(1,"m")
        r.query_blocks(["e", "pe", "m", "pm"])
        r.xrecv(1,"n")
        r.query_blocks(["n", "pn"])
        r.C(2)
        r.xrecv(1,"f")
        r.query_blocks(["f", "pf"])
        r.Cm(3)
        r.Bp(3)
        r.encode(["e", "pe", "m"])
        r.Df(2)
        r.reduce_cores(["e", "pe", "m"])
        r.section_blocks(["e", "pe", "m", "pm", "n", "pn", "f", "pf"])
        r.C(3)
        r.xrecv(2,"m")
        r.xrecv(3,"m")
        r.encode(["pm", "n"])
        r.Df(3)
        r.reduce_cores(["pm", "n"])
        r.xrecv(2,"n")
        r.xrecv(3,"n")
        r.encode(["pn", "f"])
        r.reduce_cores(["pn", "f"])
        r.reduce_heads(["pm", "n"])
        r.xrecv(2,"f")
        r.xrecv(3,"f")
        r.encode(["pf"])
        r.reduce_cores(["pf"])
        r.reduce_heads(["e", "pe", "m"])
        r.reduce_heads(["pn", "f"])
        r.reduce_heads(["pf"])
        r.place()
        r.finish()

    for wanted_end, layer, program in (
        (False, 1, mid_upper), (False, 0, mid_lower), (True, 1, end_upper), (True, 0, end_lower)
    ):
        place_here = at_end if wanted_end else jnp.logical_not(at_end)
        pl.when(place_here & (seg == layer))(program)


def run_chain(tables, top, q, k, v, wo, wq, wk, wv, devices):
    micro = tables[0].shape[0]
    q_rows, k_rows = top.shape[0] // micro, k.shape[1] // micro
    width, depth = top.shape[1], q.shape[2]
    half, blocks = width // 2, width // BLOCK
    keys = micro * k_rows
    tiles = keys // TILE
    vmem, any_ = (pl.BlockSpec(memory_space=m) for m in (pltpu.VMEM, pl.ANY))
    dma = pltpu.SemaphoreType.DMA

    def buf(*shape, dtype=BF16):
        return pltpu.VMEM(shape, dtype)

    sections, owned = pl.pallas_call(
        functools.partial(chain_kernel, (q_rows, k_rows, depth // DH, devices)),
        in_specs=[any_] * 12,
        out_specs=[any_, vmem],
        out_shape=[
            jax.ShapeDtypeStruct((1, micro * q_rows, half), BF16),
            jax.ShapeDtypeStruct((keys, width // 4), BF16),
        ],
        scratch_shapes=[
            buf(4, blocks, depth, BLOCK),
            buf(blocks, micro * q_rows, BLOCK),
            buf(micro * q_rows, depth),
            buf(keys, depth),
            buf(keys, depth),
            buf(micro * q_rows, depth, dtype=F32),
            buf(micro * q_rows, depth),
            buf(keys, depth),
            buf(keys, depth),
            buf(blocks, micro * q_rows, BLOCK),
            buf(blocks, micro * q_rows, BLOCK),
            buf(blocks, keys, BLOCK),
            buf(4, keys, BLOCK),
            buf(2, keys, BLOCK),
            buf(2, keys, BLOCK),
            buf(keys, depth),
            buf(keys, depth),
            buf(blocks, keys, BLOCK),
            buf(4, keys, BLOCK),
            buf(2, keys, BLOCK),
            buf(2, tiles, TILE, BLOCK),
            buf(2, 2 * CAP, TILE, BLOCK),
            buf(2, 2 * CAP, TILE, BLOCK),
        ]
        + [dma((4,)), dma((8,)), dma((3,))]
        + [dma((9, 4))] * 2
        + [dma((4, 4))] * 2
        + [dma((8,))] * 4
        + [dma((2,))] * 2
        + [dma((8,))] * 2
        + [dma((2,))] * 2
        + [dma((4,))] * 2
        + [dma((4,)), dma((2,))]
        + [dma((2, 2))] * 2
        + [dma((4,))]
        + [pltpu.SemaphoreType.REGULAR]
        + [pltpu.SMEM(t.shape, jnp.int32) for t in tables]
        + [dma((4,))],
        compiler_params=pltpu.CompilerParams(
            collective_id=0, has_side_effects=True, vmem_limit_bytes=60 << 20
        ),
    )(*tables, top, q, k, v, wo, wq, wk, wv)
    return pl.pallas_call(
        hand_over_kernel,
        in_specs=[any_] * 2,
        out_specs=[any_] * 2,
        out_shape=[jax.ShapeDtypeStruct(a.shape, a.dtype) for a in (sections, owned)],
        scratch_shapes=[pltpu.VMEM(a.shape, a.dtype) for a in (sections, owned)] + [dma((2, 2, 4))],
    )(sections, owned)


def hand_over_kernel(a_in, b_in, a_out, b_out, a_mid, b_mid, sems):
    inward, outward = [], []
    for i in range(4):
        for n, (src, mid, dst) in enumerate(
            ((a_in.at[0], a_mid.at[0], a_out.at[0]), (b_in, b_mid, b_out))
        ):
            rows = src.shape[0] // 4
            at = pl.ds(i * rows, rows)
            inward.append(pltpu.make_async_copy(src.at[at], mid.at[at], sems.at[0, n, i]))
            outward.append(pltpu.make_async_copy(mid.at[at], dst.at[at], sems.at[1, n, i]))
    for c in inward:
        c.start()
    for c, d in zip(inward, outward):
        c.wait()
        d.start()
    for d in outward:
        d.wait()


def ranked(marked):
    ids = jnp.arange(marked.shape[0], dtype=jnp.int32)
    upto = ids[None, :] <= ids[:, None]
    return jnp.sum((upto & marked[None, :]).astype(jnp.int32), axis=1) - 1


def on_device(
    grad_top,
    saved_query,
    saved_key,
    saved_value,
    w_query,
    w_key,
    w_value,
    w_out,
    query_length,
    key_offset,
    key_length,
    tile_owner,
):
    seg = lax.axis_index("segment")
    mp = lax.axis_index("mp")
    devices = lax.axis_size("dp")
    me = lax.axis_index("dp")
    micro = query_length.shape[0]
    q_rows = grad_top.shape[0] // micro
    k_rows = saved_key.shape[1] // micro
    half = grad_top.shape[1] // 2
    mp_swap = [(0, 1), (1, 0)]
    if w_out.shape[2] == BLOCK and devices == 8 and micro == 2:
        return run_chain(
            (query_length, key_offset, key_length, tile_owner.T), grad_top, saved_query, saved_key,
            saved_value, w_out, w_query, w_key, w_value, devices,
        )

    wo, sources = gathered(w_out[0])
    wq, _ = gathered(w_query[0])
    wk, _ = gathered(w_key[0])
    wv, _ = gathered(w_value[0])
    order = jnp.stack(sources).astype(jnp.int32)

    top = grad_top.reshape(grad_top.shape[0], 2, half).transpose(1, 0, 2)
    scalars = [
        jnp.concatenate([order, query_length[s], key_offset[s], key_length[s]])
        for s in range(micro)
    ]

    def tick(s, grad, at):
        return run_tick(
            scalars[s], grad, at, s, saved_query, saved_key, saved_value, wo, wq, q_rows, k_rows
        )

    upper = [tick(s, top, s) for s in range(micro)]
    upper_half, incoming = [], []
    for s in range(micro):
        mixed = upper[s][0]
        other = lax.ppermute(mixed, "mp", mp_swap)
        rows = top[:, s * q_rows : (s + 1) * q_rows]
        section = (rows.astype(F32) + (mixed.astype(F32) + other.astype(F32))).astype(BF16)
        incoming.append(lax.ppermute(section, "segment", [(1, 0)]))
        upper_half.append(lax.dynamic_index_in_dim(section, mp, 0, keepdims=False))
    lower = [tick(s, incoming[s], 0) for s in range(micro)]
    halves = []
    for s in range(micro):
        mixed = lower[s][0]
        other = lax.ppermute(
            lax.dynamic_index_in_dim(mixed, 1 - mp, 0, keepdims=False), "mp", mp_swap
        )
        own = lax.dynamic_index_in_dim(mixed, mp, 0, keepdims=False)
        base = lax.dynamic_index_in_dim(incoming[s], mp, 0, keepdims=False)
        low = (base.astype(F32) + (own.astype(F32) + other.astype(F32))).astype(BF16)
        halves.append(jnp.where(seg == 1, upper_half[s], low))
    sections = jnp.concatenate(halves, axis=0)[None]

    kg = jnp.concatenate([jnp.where(seg == 1, upper[s][1], lower[s][1]) for s in range(micro)], 0)
    vg = jnp.concatenate([jnp.where(seg == 1, upper[s][2], lower[s][2]) for s in range(micro)], 0)
    parts = run_encoder(order, kg, vg, wk, wv)
    away = lax.dynamic_slice_in_dim(parts, (1 - seg) * 2, 2, 0)
    mine = lax.dynamic_slice_in_dim(parts, seg * 2, 2, 0)
    arrived = lax.ppermute(away, "segment", mp_swap)
    summed = (mine.astype(F32) + arrived.astype(F32)).astype(BF16)
    crossing = lax.ppermute(
        lax.dynamic_index_in_dim(summed, 1 - mp, 0, keepdims=False), "mp", mp_swap
    )
    kept = lax.dynamic_index_in_dim(summed, mp, 0, keepdims=False)
    kept = (kept.astype(F32) + crossing.astype(F32)).astype(BF16)

    tiles = kept.shape[0] // TILE
    features = kept.shape[1]
    owners = tile_owner.reshape(devices, tiles)
    slot_ids = jnp.arange(CAP, dtype=jnp.int32)[:, None]
    tile_ids = jnp.arange(tiles, dtype=jnp.int32)

    def plan(source):
        source = source % devices
        row = lax.dynamic_index_in_dim(owners, source, 0, keepdims=False)
        return (row // tiles - source + devices) % devices, row % tiles

    def ranks_of(marked):
        return (ranked(marked)[None, :] == slot_ids) & marked[None, :]

    step, slot = plan(me)
    left_step, left_slot = plan(me - 1 + devices)
    right_step, right_slot = plan(me + 1)
    send_left = jnp.sum(jnp.where(ranks_of(step == devices - 1), tile_ids[None, :], 0), axis=1)
    send_right = jnp.sum(jnp.where(ranks_of(step == 1), tile_ids[None, :], 0), axis=1)
    left_hit = ranks_of(left_step == 1)
    right_hit = ranks_of(right_step == devices - 1)
    target = jnp.concatenate(
        [
            jnp.sum(jnp.where(left_hit, left_slot[None, :], 0), axis=1),
            slot,
            jnp.sum(jnp.where(right_hit, right_slot[None, :], 0), axis=1),
        ]
    )
    usable = jnp.concatenate([jnp.any(left_hit, axis=1), step == 0, jnp.any(right_hit, axis=1)])
    chosen = (tile_ids[:, None] == target[None, :]) & usable[None, :]
    candidate_ids = jnp.arange(target.shape[0], dtype=jnp.int32)
    take = jnp.sum(jnp.where(chosen, candidate_ids[None, :], 0), axis=1)

    tiled = (tiles, TILE, features)
    shape = jax.ShapeDtypeStruct(tiled, BF16)
    handed = jax.ShapeDtypeStruct((CAP, TILE, features), BF16)
    local = kept.reshape(tiled)
    to_left, to_right = small_call(
        pick_kernel, jnp.concatenate([send_left, send_right]), [local], [handed, handed]
    )
    forward = [(i, (i + 1) % devices) for i in range(devices)]
    backward = [(b, a) for a, b in forward]
    from_left = lax.ppermute(to_right, "dp", forward)
    from_right = lax.ppermute(to_left, "dp", backward)
    owned = small_call(place_kernel, take, [from_left, local, from_right], shape)
    return sections, owned.reshape(tiles * TILE, features)


def solution(mesh):
    in_specs = (
        P("dp", None),
        P("segment", "dp", "mp"),
        P("segment", "dp", "mp"),
        P("segment", "dp", "mp"),
        P("segment", "mp", "dp"),
        P("segment", "mp", "dp"),
        P("segment", "mp", "dp"),
        P("segment", "mp", "dp"),
        P("dp", None),
        P("dp", None),
        P("dp", None),
        P(),
    )
    out_specs = (P("segment", "dp", "mp"), P("dp", ("segment", "mp")))
    return jax.shard_map(
        on_device, mesh=mesh, in_specs=in_specs, out_specs=out_specs, check_vma=False
    )
```
